128 devices in a mesh: section: 8 (over x_lo, z), fsdp: 16 (over x_hi, y, core).
Axes of the slice: x: 4 (x_hi: 2, x_lo: 2; x = x_hi * 2 + x_lo), y: 4, z: 4, core: 2. Of those that a mesh axis runs over, the one named last changes fastest.
Arguments:
- section_inputs: bfloat16 [2, 8, 4096, 7168], P(None, 'section', 'fsdp'), may hold values from -15 to 15
- value_cotangent: bfloat16 [2, 8, 4096, 512], P(None, 'section', 'fsdp'), may hold values from -6 to 6
- down_weight: bfloat16 [8, 7168, 512], P('section', 'fsdp'), may hold values from -0.0625 to 0.0625
- up_weight: bfloat16 [8, 7168, 512], P('section', 'fsdp'), may hold values from -0.0625 to 0.0625
- down_gain: bfloat16 [8, 7168], P('section'), may hold values from 0.099609375 to 1.8984375
- up_gain: bfloat16 [8, 7168], P('section'), may hold values from 0.099609375 to 1.8984375
- image_rows: bfloat16 [2, 1024, 7168], P(None, 'fsdp'), may hold values from -15 to 15
- image_route: int32 [2, 16, 16], replicated, may hold values from 0 to 15, as said below
Outputs:
- values: bfloat16 [2, 8, 4096, 512], P(None, 'section', 'fsdp')
- input_grad: bfloat16 [2, 8, 4096, 7168], P(None, 'section', 'fsdp')
- weight_grad: float32 [8, 7168, 512], P('section', 'fsdp')
- gain_grad: float32 [8, 7168], P('section', 'fsdp')
The draws below stay inside these ranges and needn't reach their ends.
Inputs may be any that keep to these rules, and one draw needn't show every extreme that they name: `image_route`: one fsdp index sends at most 2 blocks of a pipe to any one index, and in each pipe some index takes 2 blocks from every index.
All inputs are finite; a program needn't handle non-finite values.
Results may differ from the reference program's by a relative error of at most 0.03.
Values may be sent and summed in bfloat16 or wider, within the bound.
No kernel may reach another device: no remote copies, remote signals or barrier semaphores. Data moves between devices by JAX's collectives and lax.ppermute only.
A program may use at most 192 MiB of HBM per device.

```python
import jax
import jax.numpy as jnp
from jax import lax

D = 7168
KV = 512
TOK_DEV = 256
BLOCK_ROWS = 4
ENC_BLOCKS = 16
CAP = 2
ROWS = 4096
N_SECTION = 8
N_FSDP = 16


def scale_rows(key, noise):
    key_rows, key_cols = jax.random.split(key)
    shape = noise.shape
    row_scale = jnp.exp(jax.random.uniform(key_rows, shape[:-1] + (1,), jnp.float32, -1.15, 1.15))
    col_scale = jnp.exp(jax.random.uniform(key_cols, (shape[-1],), jnp.float32, -1.15, 1.15))
    return noise * row_scale * col_scale * 0.35


def draw_section_inputs(key, part):
    key = jax.random.fold_in(key, 11)
    key_noise = jax.random.fold_in(key, 0)
    key_scale = jax.random.fold_in(key, 2)
    shape = (2, N_SECTION, TOK_DEV * N_FSDP, D)
    noise = jnp.clip(jax.random.normal(key_noise, shape, jnp.float32), -4.0, 4.0)
    return scale_rows(key_scale, noise).astype(jnp.bfloat16)


def draw_image_rows(key, part):
    key = jax.random.fold_in(key, 13)
    key_noise = jax.random.fold_in(key, 0)
    key_scale = jax.random.fold_in(key, 2)
    shape = (2, ENC_BLOCKS * BLOCK_ROWS * N_FSDP, D)
    noise = jnp.clip(jax.random.normal(key_noise, shape, jnp.float32), -4.0, 4.0)
    return scale_rows(key_scale, noise).astype(jnp.bfloat16)


def draw_image_route(key, part):
    key = jax.random.fold_in(key, 17)
    least = (ENC_BLOCKS - CAP + CAP - 1) // CAP

    def one_pipe(pipe_key):
        key_star, key_used, key_rest = jax.random.split(pipe_key, 3)
        target_full = jax.random.randint(key_star, (), 0, N_FSDP)
        spread_count = jax.random.randint(key_used, (), least, N_FSDP)

        def one_source(source_key):
            key_perm, key_order = jax.random.split(source_key)
            others = jax.random.permutation(key_perm, N_FSDP - 1)
            rest_index = jnp.arange(ENC_BLOCKS - CAP, dtype=jnp.int32) % spread_count
            rest = (target_full + 1 + others[rest_index]) % N_FSDP
            targets = jnp.concatenate([jnp.full((CAP,), target_full, jnp.int32), rest.astype(jnp.int32)])
            return targets[jax.random.permutation(key_order, ENC_BLOCKS)]
        return jax.vmap(one_source)(jax.random.split(key_rest, N_FSDP))
    return jax.vmap(one_pipe)(jax.random.split(key, 2)).astype(jnp.int32)


def level_of(stream_key, dims, shards, low, top_value):
    def one(axis_at, shards_of):
        heights = jax.random.uniform(jax.random.fold_in(jax.random.fold_in(stream_key, 6), axis_at), (shards_of,), jnp.float32, low / len(shards), top_value / len(shards))
        return jnp.repeat(jnp.exp(heights), dims[axis_at] // shards_of).reshape((-1,) + (1,) * (len(dims) - axis_at - 1))

    gain = one(*shards[0])
    for cut in shards[1:]:
        gain = gain * one(*cut)
    return gain


def normal_values(own_key, shape, scale, most, pieces=(), kind=jnp.bfloat16):
    values = jax.random.normal(own_key, shape, jnp.float32) * scale
    if len(pieces) > 0:
        values = level_of(own_key, shape, pieces, -0.22, 0.18) * values
    return jnp.clip(values, min=-most, max=most).astype(kind)


def setup_inputs(seed: int = 0) -> dict:
    arg_keys = jax.random.split(jax.random.key(seed), 9)
    section_inputs = draw_section_inputs(jax.random.fold_in(arg_keys[8], 71), 0)
    value_cotangent = normal_values(arg_keys[1], (2, N_SECTION, ROWS, KV), 1.0, 6.0, ((1, 8), (2, 16)))
    down_weight = normal_values(arg_keys[2], (N_SECTION, D, KV), D ** -0.5, 0.0625, ((0, 8), (1, 16)))
    up_weight = normal_values(arg_keys[3], (N_SECTION, D, KV), D ** -0.5, 0.0625, ((0, 8), (1, 16)))
    down_gain = jnp.clip(1.0 + 0.18 * jax.random.normal(arg_keys[4], (N_SECTION, D), jnp.float32), 0.099609375, 1.8984375).astype(jnp.bfloat16)
    up_gain = jnp.clip(1.0 + 0.18 * jax.random.normal(arg_keys[5], (N_SECTION, D), jnp.float32), 0.099609375, 1.8984375).astype(jnp.bfloat16)
    image_rows = draw_image_rows(jax.random.fold_in(arg_keys[8], 71), 0)
    image_route = draw_image_route(jax.random.fold_in(arg_keys[8], 71), 0)
    return {"section_inputs": section_inputs, "value_cotangent": value_cotangent, "down_weight": down_weight, "up_weight": up_weight, "down_gain": down_gain, "up_gain": up_gain, "image_rows": image_rows, "image_route": image_route}


EPSILON = 1e-05

def normalize(rows_in, gain_row):
    widened = rows_in.astype(jnp.float32)
    inverse = lax.rsqrt(lax.optimization_barrier(jnp.mean(widened * widened, axis=1, keepdims=True)) + EPSILON)
    normed = widened * inverse
    hidden = (normed * gain_row.astype(jnp.float32)).astype(jnp.bfloat16)
    return (normed, inverse, hidden)

def norm_backward(hidden_grad, gain_row, normed, inverse):
    scaled = hidden_grad.astype(jnp.float32) * gain_row.astype(jnp.float32)
    centre = lax.optimization_barrier(jnp.mean(scaled * normed, axis=1, keepdims=True))
    return (inverse * (scaled - normed * centre)).astype(jnp.bfloat16)

def place_images(rows_in, image_block_rows, route):
    fsdp_count = route.shape[0]
    flat = route.reshape(-1).astype(jnp.int32)
    onehot = (flat[:, None] == jnp.arange(fsdp_count, dtype=jnp.int32)[None, :]).astype(jnp.int32)
    earlier = (jnp.cumsum(onehot, axis=0) - onehot).astype(jnp.int32)
    rank = lax.optimization_barrier(jnp.sum(earlier * onehot, axis=1)).astype(jnp.int32)
    target = (flat * (TOK_DEV // BLOCK_ROWS) + rank).astype(jnp.int32)
    blocks = rows_in.reshape(-1, BLOCK_ROWS, rows_in.shape[1])
    arrived = image_block_rows.reshape(-1, BLOCK_ROWS, rows_in.shape[1])
    return blocks.at[target].set(arrived).reshape(rows_in.shape)

def layer_pass(rows_in, weight, gain_row, cotangent):
    normed, inverse, hidden = normalize(rows_in, gain_row)
    values = jnp.dot(hidden, weight, preferred_element_type=jnp.float32).astype(jnp.bfloat16)
    hidden_grad = lax.dot_general(cotangent, weight, (((1,), (1,)), ((), ())), preferred_element_type=jnp.float32).astype(jnp.bfloat16)
    input_grad = norm_backward(hidden_grad, gain_row, normed, inverse)
    hidden_blocks = hidden.reshape(N_FSDP, TOK_DEV, -1)
    cotangent_blocks = cotangent.reshape(N_FSDP, TOK_DEV, -1)
    products = (hidden_grad.astype(jnp.float32) * normed).reshape(N_FSDP, TOK_DEV, -1)

    def one_share(carry, index):
        weight_part = lax.dot_general(hidden_blocks[index], cotangent_blocks[index], (((0,), (0,)), ((), ())), preferred_element_type=jnp.float32).astype(jnp.bfloat16)
        gain_part = lax.optimization_barrier(jnp.sum(products[index], axis=0)).astype(jnp.bfloat16)
        weight_part, gain_part = lax.optimization_barrier((weight_part, gain_part))
        return ((carry[0] + weight_part.astype(jnp.float32), carry[1] + gain_part.astype(jnp.float32)), None)
    start_state = (jnp.zeros(weight.shape, jnp.float32), jnp.zeros((weight.shape[0],), jnp.float32))
    shares, _ = lax.scan(one_share, start_state, jnp.arange(N_FSDP, dtype=jnp.int32))
    return (values, input_grad, shares[0], shares[1])

def reference(section_inputs, value_cotangent, down_weight, up_weight, down_gain, up_gain, image_rows, image_route):
    lead_down = place_images(section_inputs[0, 0], image_rows[0], image_route[0])
    lead_up = place_images(section_inputs[1, N_SECTION - 1], image_rows[1], image_route[1])

    def one_section(position):
        down_rows = jnp.where(position == 0, lead_down, section_inputs[0, position])
        up_rows = jnp.where(position == N_SECTION - 1, lead_up, section_inputs[1, position])
        first = layer_pass(down_rows, down_weight[position], down_gain[position], value_cotangent[0, position])
        second = layer_pass(up_rows, up_weight[position], up_gain[position], value_cotangent[1, position])
        return first + second
    outcome = lax.map(one_section, jnp.arange(N_SECTION, dtype=jnp.int32))
    values = jnp.stack([outcome[0], outcome[4]])
    input_grad = jnp.stack([outcome[1], outcome[5]])
    weight_grad = outcome[2] + outcome[6][::-1]
    gain_grad = outcome[3] + outcome[7][::-1]
    return (values, input_grad, weight_grad, gain_grad)
```

```python
import jax
import jax.numpy as jnp
from jax import lax
from jax.experimental import pallas as pl
from jax.experimental.pallas import tpu as pltpu
from jax.sharding import PartitionSpec as P

BLOCK_ROWS = 4
CAP = 2
EPSILON = 1e-05
F32 = jnp.float32
BF16 = jnp.bfloat16

X_CHIPS, Y_CHIPS = 2, 4
CHIPS = X_CHIPS * Y_CHIPS
CORE, LIVE, FLAG, QUARTER = 8, 9, 10, 12


def fsdp_route(step):
    route = []
    for x in range(X_CHIPS):
        for y in range(Y_CHIPS):
            for core in range(2):
                to_x, to_y, to_core = step(x, y, core)
                target = (to_x % X_CHIPS * Y_CHIPS + to_y % Y_CHIPS) * 2 + to_core % 2
                route.append(((x * Y_CHIPS + y) * 2 + core, target))
    return route


def to_next(block):
    return lax.ppermute(block, "fsdp", fsdp_route(lambda x, y, core: (x, y + 1, core)))


def to_previous(block):
    return lax.ppermute(block, "fsdp", fsdp_route(lambda x, y, core: (x, y - 1, core)))


def to_across(block):
    return lax.ppermute(block, "fsdp", fsdp_route(lambda x, y, core: (x + 1, y, core)))


def to_sibling(block):
    return lax.ppermute(block, "fsdp", fsdp_route(lambda x, y, core: (x, y, core + 1)))


def to_mirror(block):
    count = lax.axis_size("section")
    return lax.ppermute(block, "section", [(s, count - 1 - s) for s in range(count)])


def columns(chip, size):
    return pl.ds(pl.multiple_of(chip * size, 128), size)


def mean_square(x_ref, width, size):
    total = jnp.zeros((x_ref.shape[2], 1), F32)
    for chip in range(CHIPS):
        part = x_ref[0, 0, :, chip * size : (chip + 1) * size].astype(F32)
        total = total + jnp.sum(part * part, axis=1, keepdims=True)
    return total / width


def prepare_kernel(table, x_ref, gain_ref, perm_ref, im0, im1, im2, im3, rows_ref, mine_ref, other_ref):
    pipe = pl.program_id(0)
    width = x_ref.shape[3]
    pair = width // CHIPS
    half = pair // 2
    rows_ref[...] = x_ref[...]

    @pl.when(table[FLAG + pipe] == 1)
    def _():
        head = perm_ref.shape[0]
        live = lax.broadcasted_iota(jnp.int32, (head, 1), 0) < table[LIVE]
        for quarter, image in enumerate((im0, im1, im2, im3)):
            where = columns(table[QUARTER + quarter], image.shape[1])
            arrived = jnp.dot(perm_ref[...], image[...], preferred_element_type=F32).astype(BF16)
            rows_ref[0, 0, :head, where] = jnp.where(live, arrived, x_ref[0, 0, :head, where])

    inverse = lax.rsqrt(mean_square(rows_ref, width, pair) + EPSILON)
    first = table[CORE] == 0
    for r in range(CHIPS):
        where = columns(table[r], pair)
        normed = rows_ref[0, 0, :, where].astype(F32) * inverse
        hidden = (normed * gain_ref[0, :, where].astype(F32)).astype(BF16)
        low, high = hidden[:, :half], hidden[:, half:]

        @pl.when(first)
        def _():
            mine_ref[0, r] = low
            other_ref[0, r] = high

        @pl.when(jnp.logical_not(first))
        def _():
            mine_ref[0, r] = high
            other_ref[0, r] = low


def prepare(table, section_inputs, gains, perm, images):
    pipes, _, tokens, width = section_inputs.shape
    pair = width // CHIPS
    halves = jax.ShapeDtypeStruct((pipes, CHIPS, tokens, pair // 2), BF16)
    rows_spec = pl.BlockSpec((1, 1, tokens, width), lambda p: (p, 0, 0, 0))
    half_spec = pl.BlockSpec((1, CHIPS, tokens, pair // 2), lambda p: (p, 0, 0, 0))
    whole = pl.BlockSpec(memory_space=pltpu.VMEM)
    return pl.pallas_call(
        prepare_kernel,
        grid=(pipes,),
        in_specs=[
            pl.BlockSpec(memory_space=pltpu.SMEM),
            rows_spec,
            pl.BlockSpec((1, 1, width), lambda p: (p, 0, 0)),
            whole,
            whole,
            whole,
            whole,
            whole,
        ],
        out_specs=[rows_spec, half_spec, half_spec],
        out_shape=[jax.ShapeDtypeStruct(section_inputs.shape, BF16), halves, halves],
        compiler_params=pltpu.CompilerParams(vmem_limit_bytes=48 * 1024 * 1024),
        name="prepare",
    )(table, section_inputs, gains, perm, *images)


def products(pipe, mine, received, cotangent, received_cotangent, groups):
    _, _, tokens, half = mine.shape
    kv = cotangent.shape[3]

    def kernel(mine_ref, received_ref, own_ct, other_ct, *outs):
        own_side, other_side = own_ct[0, 0], other_ct[0, 0]
        contract = (((0,), (0,)), ((), ()))
        for out, group in zip(outs, groups):
            for place, r in enumerate(group):
                total = lax.dot_general(mine_ref[0, r], own_side, contract, preferred_element_type=F32)
                total += lax.dot_general(
                    received_ref[0, r], other_side, contract, preferred_element_type=F32
                )
                out[place] = total.astype(BF16)

    half_spec = pl.BlockSpec((1, CHIPS, tokens, half), lambda i: (pipe, 0, 0, 0))
    ct_spec = pl.BlockSpec((1, 1, tokens, kv), lambda i: (pipe, 0, 0, 0))
    return pl.pallas_call(
        kernel,
        grid=(1,),
        in_specs=[half_spec, half_spec, ct_spec, ct_spec],
        out_specs=[pl.BlockSpec((len(g), half, kv), lambda i: (0, 0, 0)) for g in groups],
        out_shape=[jax.ShapeDtypeStruct((len(g), half, kv), BF16) for g in groups],
        compiler_params=pltpu.CompilerParams(vmem_limit_bytes=40 * 1024 * 1024),
        cost_estimate=pl.CostEstimate(
            flops=4 * CHIPS * tokens * half * kv, bytes_accessed=12_000_000, transcendentals=0
        ),
        name="products",
    )(mine, received, cotangent, received_cotangent)


def layer_kernel(table, x_ref, ct_ref, gain_ref, *refs):
    pieces = refs[: 2 * CHIPS]
    values_ref, grad_ref, weight, hidden_grad, sems = refs[-5:]
    width = x_ref.shape[3]
    pair = width // CHIPS
    half = pair // 2
    core = table[CORE]
    copies = []
    for r in range(CHIPS):
        for side in range(2):
            at = table[r] * pair + (core if side == 0 else 1 - core) * half
            copy = pltpu.make_async_copy(
                pieces[side * CHIPS + r],
                weight.at[pl.ds(pl.multiple_of(at, 64), half)],
                sems.at[side * CHIPS + r],
            )
            copy.start()
            copies.append(copy)
    inverse = lax.rsqrt(mean_square(x_ref, width, pair) + EPSILON)
    cotangent = ct_ref[0, 0]
    values = jnp.zeros(values_ref.shape[2:], F32)
    centre = jnp.zeros(inverse.shape, F32)
    for r in range(CHIPS):
        copies[2 * r].wait()
        copies[2 * r + 1].wait()
        where = columns(table[r], pair)
        block = weight[pl.ds(pl.multiple_of(table[r] * pair, 128), pair)]
        normed = x_ref[0, 0, :, where].astype(F32) * inverse
        gain = gain_ref[:, where].astype(F32)
        hidden = (normed * gain).astype(BF16)
        values += jnp.dot(hidden, block, preferred_element_type=F32)
        back = lax.dot_general(
            cotangent, block, (((1,), (1,)), ((), ())), preferred_element_type=F32
        ).astype(BF16)
        hidden_grad[:, where] = back
        centre += jnp.sum(back.astype(F32) * gain * normed, axis=1, keepdims=True)
    values_ref[0, 0] = values.astype(BF16)
    centre = centre / width
    for chip in range(CHIPS):
        where = slice(chip * pair, (chip + 1) * pair)
        normed = x_ref[0, 0, :, where].astype(F32) * inverse
        scaled = hidden_grad[:, where].astype(F32) * gain_ref[:, where].astype(F32)
        grad_ref[0, 0, :, where] = (inverse * (scaled - normed * centre)).astype(BF16)


def layer(pipe, table, rows, cotangent, gain, own_pieces, sibling_pieces, carried):
    _, _, tokens, width = rows.shape
    kv = cotangent.shape[3]
    anywhere = pl.BlockSpec(memory_space=pl.ANY)
    rows_spec = pl.BlockSpec((1, 1, tokens, width), lambda i: (pipe, 0, 0, 0))
    ct_spec = pl.BlockSpec((1, 1, tokens, kv), lambda i: (pipe, 0, 0, 0))
    pieces = [*own_pieces, *sibling_pieces]
    operands = [table, rows, cotangent, gain, *pieces, *carried]
    aliases = {4 + len(pieces) + i: i for i in range(len(carried))}
    return pl.pallas_call(
        layer_kernel,
        grid=(1,),
        in_specs=[
            pl.BlockSpec(memory_space=pltpu.SMEM),
            rows_spec,
            ct_spec,
            pl.BlockSpec((1, width), lambda i: (0, 0)),
        ]
        + [anywhere] * (len(pieces) + len(carried)),
        out_specs=[ct_spec, rows_spec],
        out_shape=[
            jax.ShapeDtypeStruct(cotangent.shape, BF16),
            jax.ShapeDtypeStruct(rows.shape, BF16),
        ],
        scratch_shapes=[
            pltpu.VMEM((width, kv), BF16),
            pltpu.VMEM((tokens, width), BF16),
            pltpu.SemaphoreType.DMA((2 * CHIPS,)),
        ],
        input_output_aliases=aliases,
        compiler_params=pltpu.CompilerParams(vmem_limit_bytes=48 * 1024 * 1024),
        cost_estimate=pl.CostEstimate(
            flops=4 * tokens * width * kv, bytes_accessed=16_000_000, transcendentals=0
        ),
        name="layer",
    )(*operands)


def route_images(image_rows, image_route, section_place, fsdp_place):
    fsdp_count = lax.axis_size("fsdp")
    section_count = lax.axis_size("section")
    quarters = section_count // 2
    width = image_rows.shape[2]
    pipe = section_place // quarters
    quarter = section_place % quarters
    enc_rows = image_rows.shape[1]
    enc_count = enc_rows // BLOCK_ROWS
    head = fsdp_count * CAP * BLOCK_ROWS
    routes = lax.dynamic_index_in_dim(image_route, pipe, 0, keepdims=False)
    own_route = lax.dynamic_index_in_dim(routes, fsdp_place, 0, keepdims=False)
    ids = jnp.arange(enc_count, dtype=jnp.int32)
    earlier = (own_route[:, None] == own_route[None, :]) & (ids[None, :] < ids[:, None])
    slot_of = own_route * CAP + jnp.sum(earlier.astype(jnp.int32), axis=1)
    goes_to = jnp.repeat(slot_of * BLOCK_ROWS, BLOCK_ROWS) + jnp.tile(
        jnp.arange(BLOCK_ROWS, dtype=jnp.int32), enc_count
    )
    row_ids = jnp.arange(head, dtype=jnp.int32)
    select = (row_ids[:, None] == goes_to[None, :]).astype(BF16)
    part = lax.dynamic_slice(
        image_rows, (pipe, 0, quarter * (width // quarters)), (1, enc_rows, width // quarters)
    )[0]
    outgoing = jnp.dot(select, part, preferred_element_type=F32).astype(BF16)
    incoming = lax.all_to_all(outgoing, "fsdp", split_axis=0, concat_axis=0, tiled=True)
    images = [incoming]
    for step in range(1, quarters):
        hop = [(step, 0), (section_count - 1 - step, section_count - 1)]
        images.append(lax.ppermute(incoming, "section", hop))
    arrivals = jnp.sum((routes == fsdp_place).astype(jnp.int32), axis=1)
    offsets = jnp.cumsum(arrivals) - arrivals
    slot_rows = CAP * BLOCK_ROWS
    sender, within = row_ids // slot_rows, row_ids % slot_rows
    lands = jnp.repeat(offsets, slot_rows) * BLOCK_ROWS + within
    valid = within < jnp.repeat(arrivals, slot_rows) * BLOCK_ROWS
    lands = jnp.where(valid, lands, head)
    perm = (row_ids[:, None] == lands[None, :]).astype(BF16)
    steps = jnp.arange(quarters, dtype=jnp.int32)
    last = section_place == section_count - 1
    numbers = jnp.concatenate(
        [
            (jnp.sum(arrivals) * BLOCK_ROWS)[None],
            (section_place == 0).astype(jnp.int32)[None],
            last.astype(jnp.int32)[None],
            jnp.where(last, quarters - 1 - steps, steps),
        ]
    )
    return images, perm, numbers


def gather(first, second):
    a, b = [None] * CHIPS, [None] * CHIPS
    a[0], b[0] = first, second
    b[4] = to_across(second)
    a[3], a[1] = to_next(first), to_previous(first)
    b[3], b[1] = to_next(second), to_previous(second)
    a[4] = to_across(first)
    a[2] = to_next(a[3])
    b[2] = to_previous(b[1])
    b[7], b[5] = to_next(b[4]), to_previous(b[4])
    a[5], a[7] = to_across(a[1]), to_across(a[3])
    b[6] = to_next(b[7])
    a[6] = to_across(a[2])
    return a, b


def scatter_y_first(blocks):
    far0, far1, near1, near0, back0, back1, own0, own1 = blocks
    from_below = to_next(far0)
    from_above = to_previous(far1)
    below1 = to_next(near1)
    above0 = to_previous(back0)
    below0 = to_next(near0 + from_below)
    above1 = to_previous(back1 + from_above)
    across = own1.astype(F32) + below1.astype(F32) + above1.astype(F32)
    kept = own0.astype(F32) + below0.astype(F32) + above0.astype(F32)
    return kept + to_across(across.astype(BF16)).astype(F32)


def scatter_x_first(blocks):
    send2, send13, send0, keep2, keep13, keep0 = blocks
    half = keep2.shape[1] // 2
    came2, came13, came0 = to_across(send2), to_across(send13), to_across(send0)
    far = keep2[0] + came2[0]
    from_below = to_next(far[:half])
    from_above = to_previous(far[half:])
    up = keep13[0] + came13[0]
    down = keep13[1] + came13[1]
    up = jnp.concatenate([up[:half] + from_below, up[half:]])
    down = jnp.concatenate([down[:half], down[half:] + from_above])
    below = to_next(up)
    above = to_previous(down)
    kept = keep0[0].astype(F32) + came0[0].astype(F32)
    return kept + below.astype(F32) + above.astype(F32)


def per_device(
    section_inputs,
    value_cotangent,
    down_weight,
    up_weight,
    down_gain,
    up_gain,
    image_rows,
    image_route,
):
    section_place = lax.axis_index("section")
    fsdp_place = lax.axis_index("fsdp")
    core = fsdp_place % 2
    y = fsdp_place // 2 % Y_CHIPS
    x = fsdp_place // (2 * Y_CHIPS)
    r = jnp.arange(CHIPS, dtype=jnp.int32)
    chips = (x ^ (r // Y_CHIPS)) * Y_CHIPS + (y + r % Y_CHIPS) % Y_CHIPS

    images, perm, numbers = route_images(image_rows, image_route, section_place, fsdp_place)
    table = jnp.concatenate([chips, core[None], numbers]).astype(jnp.int32)
    gains = jnp.stack([down_gain, up_gain])
    own_down, own_up = gather(down_weight[0], up_weight[0])
    sibling_down = [to_sibling(block) for block in own_down]
    sibling_up = [to_sibling(block) for block in own_up]

    rows, mine, other = prepare(table, section_inputs, gains, perm, images)
    received = to_sibling(other)
    received_cotangent = to_sibling(value_cotangent)

    up_groups = ((2,), (6,), (5,), (1,), (3,), (7,), (0,), (4,))
    down_groups = ((6,), (5, 7), (4,), (2,), (1, 3), (0,))
    up_blocks = products(1, mine, received, value_cotangent, received_cotangent, up_groups)
    down_blocks = products(0, mine, received, value_cotangent, received_cotangent, down_groups)

    up_share = scatter_y_first([block[0] for block in up_blocks])
    down_share = scatter_x_first(down_blocks)

    shard = down_weight.shape[1]

    def gain_share(weight, share, gain):
        part = lax.dynamic_slice(gain[0], (fsdp_place * shard,), (shard,)).astype(F32)
        return jnp.sum(weight[0].astype(F32) * share, axis=1) / part

    up_gain_share = gain_share(up_weight, up_share, up_gain)
    down_gain_share = gain_share(down_weight, down_share, down_gain)
    moved_weight = to_mirror(up_share.astype(BF16))
    moved_gain = to_mirror(up_gain_share.astype(BF16))
    weight_grad = (down_share + moved_weight.astype(F32))[None]
    gain_grad = (down_gain_share + moved_gain.astype(F32))[None]

    filled = layer(0, table, rows, value_cotangent, down_gain, own_down, sibling_down, ())
    values, input_grad = layer(
        1, table, rows, value_cotangent, up_gain, own_up, sibling_up, tuple(filled)
    )
    return (values, input_grad, weight_grad, gain_grad)


def solution(mesh):
    return jax.shard_map(
        per_device,
        mesh=mesh,
        in_specs=(
            P(None, "section", "fsdp", None),
            P(None, "section", "fsdp", None),
            P("section", "fsdp", None),
            P("section", "fsdp", None),
            P("section", None),
            P("section", None),
            P(None, "fsdp", None),
            P(),
        ),
        out_specs=(
            P(None, "section", "fsdp", None),
            P(None, "section", "fsdp", None),
            P("section", "fsdp", None),
            P("section", "fsdp"),
        ),
        check_vma=False,
    )
```

```python
import jax
import jax.numpy as jnp
from jax import lax
from jax.experimental import pallas as pl
from jax.experimental.pallas import tpu as pltpu
from jax.sharding import PartitionSpec as P

BLOCK_ROWS = 4
CAP = 2
EPSILON = 1e-05
TOKENS = 256
HEAD = 128
VMEM_BYTES = 60 * 1024 * 1024
F32 = jnp.float32
BF16 = jnp.bfloat16

X_CHIPS, Y_CHIPS = 2, 4
CHIPS = X_CHIPS * Y_CHIPS
CORE, LIVE, FLAG, PART, PIPE = 8, 9, 10, 12, 15


def fsdp_route(step):
    route = []
    for x in range(X_CHIPS):
        for y in range(Y_CHIPS):
            for core in range(2):
                to_x, to_y, to_core = step(x, y, core)
                target = (to_x % X_CHIPS * Y_CHIPS + to_y % Y_CHIPS) * 2 + to_core % 2
                route.append(((x * Y_CHIPS + y) * 2 + core, target))
    return route


def to_next(block):
    return lax.ppermute(block, "fsdp", fsdp_route(lambda x, y, core: (x, y + 1, core)))


def to_previous(block):
    return lax.ppermute(block, "fsdp", fsdp_route(lambda x, y, core: (x, y - 1, core)))


def to_across(block):
    return lax.ppermute(block, "fsdp", fsdp_route(lambda x, y, core: (x + 1, y, core)))


def to_sibling(block):
    return lax.ppermute(block, "fsdp", fsdp_route(lambda x, y, core: (x, y, core + 1)))


def to_mirror(block):
    count = lax.axis_size("section")
    return lax.ppermute(block, "section", [(s, count - 1 - s) for s in range(count)])


def columns(chip, size):
    return pl.ds(pl.multiple_of(chip * size, 128), size)


def prepare_kernel(table, x_ref, ct_ref, perm_ref, im0, im1, im2, head_ref, ct_out, inverse_out, rows):
    pipe, step = pl.program_id(0), pl.program_id(1)
    _, _, tokens, width = x_ref.shape
    pair = width // CHIPS
    rows[...] = x_ref[0, 0]

    @pl.when((table[FLAG + pipe] == 1) & (step * tokens < table[LIVE]))
    def _():
        row = lax.broadcasted_iota(jnp.int32, (tokens, 1), 0) + step * tokens
        live = row < table[LIVE]
        for part, image in enumerate((im0, im1, im2)):
            where = pl.ds(pl.multiple_of(table[PART + part], 128), image.shape[1])
            arrived = jnp.dot(perm_ref[...], image[...], preferred_element_type=F32).astype(BF16)
            rows[:, where] = jnp.where(live, arrived, rows[:, where])

    @pl.when((table[PIPE] == pipe) & (step * tokens < head_ref.shape[0]))
    def _():
        head_ref[pl.ds(pl.multiple_of(step * tokens, tokens), tokens)] = rows[...]

    total = jnp.zeros((tokens, 1), F32)
    for chip in range(CHIPS):
        part = rows[:, chip * pair : (chip + 1) * pair].astype(F32)
        total = total + jnp.sum(part * part, axis=1, keepdims=True)
    inverse = lax.rsqrt(total / width + EPSILON)
    ct_out[0, 0] = (ct_ref[0, 0].astype(F32) * inverse).astype(BF16)
    inverse_out[0] = jnp.broadcast_to(inverse, inverse_out.shape[1:])


def prepare(table, section_inputs, cotangent, perm, images):
    pipes, _, tokens, width = section_inputs.shape
    kv = cotangent.shape[3]
    tile = 64
    ct_spec = pl.BlockSpec((1, 1, tile, kv), lambda p, t: (p, 0, t, 0))
    whole = pl.BlockSpec(memory_space=pltpu.VMEM)
    return pl.pallas_call(
        prepare_kernel,
        grid=(pipes, tokens // tile),
        in_specs=[
            pl.BlockSpec(memory_space=pltpu.SMEM),
            pl.BlockSpec((1, 1, tile, width), lambda p, t: (p, 0, t, 0)),
            ct_spec,
            pl.BlockSpec((tile, perm.shape[1]), lambda p, t: (t, 0)),
            whole,
            whole,
            whole,
        ],
        out_specs=[
            pl.BlockSpec((HEAD, width), lambda p, t: (0, 0)),
            ct_spec,
            pl.BlockSpec((1, tile, 128), lambda p, t: (p, t, 0)),
        ],
        out_shape=[
            jax.ShapeDtypeStruct((HEAD, width), BF16),
            jax.ShapeDtypeStruct(cotangent.shape, BF16),
            jax.ShapeDtypeStruct((pipes, tokens, 128), F32),
        ],
        scratch_shapes=[pltpu.VMEM((tile, width), BF16)],
        compiler_params=pltpu.CompilerParams(vmem_limit_bytes=VMEM_BYTES),
        cost_estimate=pl.CostEstimate(
            flops=8 * pipes * tokens * width, bytes_accessed=12_000_000, transcendentals=0
        ),
        name="prepare",
    )(table, section_inputs, cotangent, perm, *images)


def start_rows(table, pipe, x_ref, head_ref, rows, sems, chip):
    pair = rows.shape[1] // CHIPS
    where = columns(chip, pair)
    tail = rows.shape[0] - HEAD
    flag = table[FLAG + pipe] == 1
    top = rows.at[pl.ds(0, HEAD), where]
    plain = pltpu.make_async_copy(x_ref.at[pipe, 0, pl.ds(0, HEAD), where], top, sems.at[0])
    placed = pltpu.make_async_copy(head_ref.at[:, where], top, sems.at[0])
    rest = pltpu.make_async_copy(
        x_ref.at[pipe, 0, pl.ds(HEAD, tail), where], rows.at[pl.ds(HEAD, tail), where], sems.at[1]
    )

    @pl.when(flag)
    def _():
        placed.start()

    @pl.when(jnp.logical_not(flag))
    def _():
        plain.start()

    rest.start()
    return plain, rest


def products(pipe, table, x, sibling_x, head, sibling_head, ct, sibling_ct, groups):
    _, _, tokens, width = x.shape
    pair = width // CHIPS
    half = pair // 2
    kv = ct.shape[3]
    place = {r: (g, i) for g, group in enumerate(groups) for i, r in enumerate(group)}
    order = [r for group in groups for r in group]

    def kernel(table, x_ref, sibling_x_ref, head_ref, sibling_head_ref, own_ct, other_ct, *refs):
        outs = refs[: len(groups)]
        own, other, sems = refs[len(groups) :]
        waits = {}
        for r in order:
            waits[r] = start_rows(table, pipe, x_ref, head_ref, own, sems.at[r, 0], table[r])
            waits[r] += start_rows(
                table, pipe, sibling_x_ref, sibling_head_ref, other, sems.at[r, 1], table[r]
            )
        contract = (((0,), (0,)), ((), ()))

        def block(r, low):
            where = columns(table[r], pair)
            product = lax.dot_general(
                own[:, where][:, low : low + half], own_ct[0, 0], contract, preferred_element_type=F32
            )
            product += lax.dot_general(
                other[:, where][:, low : low + half], other_ct[0, 0], contract, preferred_element_type=F32
            )
            out, at = place[r]
            outs[out][at] = product.astype(BF16)

        for r in order:
            for copy in waits[r]:
                copy.wait()
            pl.when(table[CORE] == 0)(lambda: block(r, 0))
            pl.when(table[CORE] == 1)(lambda: block(r, half))

    anywhere = pl.BlockSpec(memory_space=pl.ANY)
    ct_spec = pl.BlockSpec((1, 1, tokens, kv), lambda i: (pipe, 0, 0, 0))
    return pl.pallas_call(
        kernel,
        grid=(1,),
        in_specs=[pl.BlockSpec(memory_space=pltpu.SMEM)] + [anywhere] * 4 + [ct_spec] * 2,
        out_specs=[pl.BlockSpec((len(g), half, kv), lambda i: (0, 0, 0)) for g in groups],
        out_shape=[jax.ShapeDtypeStruct((len(g), half, kv), BF16) for g in groups],
        scratch_shapes=[
            pltpu.VMEM((tokens, width), BF16),
            pltpu.VMEM((tokens, width), BF16),
            pltpu.SemaphoreType.DMA((CHIPS, 2, 2)),
        ],
        compiler_params=pltpu.CompilerParams(vmem_limit_bytes=VMEM_BYTES),
        cost_estimate=pl.CostEstimate(
            flops=4 * tokens * width * kv, bytes_accessed=12_000_000, transcendentals=0
        ),
        name="products",
    )(table, x, sibling_x, head, sibling_head, ct, sibling_ct)


def layer(pipe, table, x, head, cotangent, scaled_ct, inverse, gain, own, sibling, carried):
    _, _, tokens, width = x.shape
    pair = width // CHIPS
    half = pair // 2
    kv = cotangent.shape[3]
    arrays = []
    for array, _ in [*own, *sibling]:
        if not any(array is known for known in arrays):
            arrays.append(array)
    position = [
        next(i for i, known in enumerate(arrays) if known is array) for array, _ in [*own, *sibling]
    ]
    index = [at for _, at in [*own, *sibling]]

    def kernel(table, x_ref, head_ref, ct_ref, scaled_ref, inverse_ref, gain_ref, *refs):
        pieces = refs[: len(arrays)]
        values_ref, grad_ref, rows, weight, grad, w_sems, x_sems, out_sems = refs[-8:]
        core = table[CORE]
        waits = []
        for r in range(CHIPS):
            copies = []
            for side in range(2):
                piece = side * CHIPS + r
                source = pieces[position[piece]]
                if index[piece] is not None:
                    source = source.at[index[piece]]
                at = table[r] * pair + (core if side == 0 else 1 - core) * half
                copy = pltpu.make_async_copy(
                    source, weight.at[pl.ds(pl.multiple_of(at, 64), half)], w_sems.at[piece]
                )
                copy.start()
                copies.append(copy)
            waits.append(copies + list(start_rows(table, pipe, x_ref, head_ref, rows, x_sems.at[r], table[r])))
        values = jnp.zeros((tokens, kv), F32)
        for r in range(CHIPS):
            for copy in waits[r]:
                copy.wait()
            where = columns(table[r], pair)
            block = weight[pl.ds(pl.multiple_of(table[r] * pair, 128), pair)]
            values += jnp.dot(rows[:, where] * gain_ref[:, where], block, preferred_element_type=F32)
        inv = inverse_ref[0, :, :1]
        values = values * inv
        values_ref[0, 0] = values.astype(BF16)
        centre = jnp.sum(values * ct_ref[0, 0].astype(F32), axis=1, keepdims=True) / width
        pull = inv * inv * centre
        outs = []
        for chip in range(CHIPS):
            where = slice(chip * pair, (chip + 1) * pair)
            back = lax.dot_general(
                scaled_ref[0, 0], weight[where], (((1,), (1,)), ((), ())), preferred_element_type=F32
            )
            grad[:, where] = (
                back * gain_ref[:, where].astype(F32) - rows[:, where].astype(F32) * pull
            ).astype(BF16)
            copy = pltpu.make_async_copy(
                grad.at[:, pl.ds(chip * pair, pair)],
                grad_ref.at[pipe, 0, :, pl.ds(chip * pair, pair)],
                out_sems.at[chip],
            )
            copy.start()
            outs.append(copy)
        for copy in outs:
            copy.wait()

    anywhere = pl.BlockSpec(memory_space=pl.ANY)
    ct_spec = pl.BlockSpec((1, 1, tokens, kv), lambda i: (pipe, 0, 0, 0))
    operands = [table, x, head, cotangent, scaled_ct, inverse, gain, *arrays, *carried]
    return pl.pallas_call(
        kernel,
        grid=(1,),
        in_specs=[
            pl.BlockSpec(memory_space=pltpu.SMEM),
            anywhere,
            anywhere,
            ct_spec,
            ct_spec,
            pl.BlockSpec((1, tokens, 128), lambda i: (pipe, 0, 0)),
            pl.BlockSpec((1, width), lambda i: (0, 0)),
        ]
        + [anywhere] * (len(arrays) + len(carried)),
        out_specs=[ct_spec, anywhere],
        out_shape=[
            jax.ShapeDtypeStruct(cotangent.shape, BF16),
            jax.ShapeDtypeStruct(x.shape, BF16),
        ],
        scratch_shapes=[
            pltpu.VMEM((tokens, width), BF16),
            pltpu.VMEM((width, kv), BF16),
            pltpu.VMEM((tokens, width), BF16),
            pltpu.SemaphoreType.DMA((2 * CHIPS,)),
            pltpu.SemaphoreType.DMA((CHIPS, 2)),
            pltpu.SemaphoreType.DMA((CHIPS,)),
        ],
        input_output_aliases={7 + len(arrays) + i: i for i in range(len(carried))},
        compiler_params=pltpu.CompilerParams(vmem_limit_bytes=VMEM_BYTES),
        cost_estimate=pl.CostEstimate(
            flops=4 * tokens * width * kv, bytes_accessed=16_000_000, transcendentals=0
        ),
        name="layer",
    )(*operands)


def route_images(image_rows, image_route, section_place, fsdp_place):
    fsdp_count = lax.axis_size("fsdp")
    section_count = lax.axis_size("section")
    ring = section_count // 2
    width = image_rows.shape[2]
    size = -(-width // (3 * 128)) * 128
    pipe = section_place // ring
    z = section_place % ring
    enc_rows = image_rows.shape[1]
    enc_count = enc_rows // BLOCK_ROWS
    head = fsdp_count * CAP * BLOCK_ROWS
    routes = lax.dynamic_index_in_dim(image_route, pipe, 0, keepdims=False)
    own_route = lax.dynamic_index_in_dim(routes, fsdp_place, 0, keepdims=False)
    ids = jnp.arange(enc_count, dtype=jnp.int32)
    earlier = (own_route[:, None] == own_route[None, :]) & (ids[None, :] < ids[:, None])
    slot_of = own_route * CAP + jnp.sum(earlier.astype(jnp.int32), axis=1)
    goes_to = jnp.repeat(slot_of * BLOCK_ROWS, BLOCK_ROWS) + jnp.tile(
        jnp.arange(BLOCK_ROWS, dtype=jnp.int32), enc_count
    )
    row_ids = jnp.arange(head, dtype=jnp.int32)
    select = (row_ids[:, None] == goes_to[None, :]).astype(BF16)
    from_end = jnp.where(pipe == 0, z, ring - 1 - z)
    own_part = jnp.where(from_end == ring - 1, 2, jnp.minimum(from_end, 1))
    starts = jnp.array([0, size, width - size], jnp.int32)
    start = jnp.where(own_part == 0, 0, jnp.where(own_part == 1, size, width - size))
    part = lax.dynamic_slice(image_rows, (pipe, 0, start), (1, enc_rows, size))[0]
    outgoing = jnp.dot(select, part, preferred_element_type=F32).astype(BF16)
    incoming = lax.all_to_all(outgoing, "fsdp", split_axis=0, concat_axis=0, tiled=True)
    end = section_count - 1
    images = [
        incoming,
        lax.ppermute(incoming, "section", [(1, 0), (end - 1, end)]),
        lax.ppermute(incoming, "section", [(ring - 1, 0), (end - ring + 1, end)]),
    ]
    arrivals = jnp.sum((routes == fsdp_place).astype(jnp.int32), axis=1)
    offsets = jnp.cumsum(arrivals) - arrivals
    slot_rows = CAP * BLOCK_ROWS
    within = row_ids % slot_rows
    lands = jnp.repeat(offsets, slot_rows) * BLOCK_ROWS + within
    valid = within < jnp.repeat(arrivals, slot_rows) * BLOCK_ROWS
    lands = jnp.where(valid, lands, -1)
    perm = (jnp.arange(TOKENS, dtype=jnp.int32)[:, None] == lands[None, :]).astype(BF16)
    numbers = jnp.concatenate(
        [
            (jnp.sum(arrivals) * BLOCK_ROWS)[None],
            (section_place == 0).astype(jnp.int32)[None],
            (section_place == end).astype(jnp.int32)[None],
            starts,
            pipe[None],
        ]
    )
    return images, perm, numbers, outgoing


def hold(value, *before):
    return lax.optimization_barrier((value, before))[0]


def per_device(
    section_inputs,
    value_cotangent,
    down_weight,
    up_weight,
    down_gain,
    up_gain,
    image_rows,
    image_route,
):
    section_place = lax.axis_index("section")
    fsdp_place = lax.axis_index("fsdp")
    core = fsdp_place % 2
    y = fsdp_place // 2 % Y_CHIPS
    x = fsdp_place // (2 * Y_CHIPS)
    r = jnp.arange(CHIPS, dtype=jnp.int32)
    chips = (x ^ (r // Y_CHIPS)) * Y_CHIPS + (y + r % Y_CHIPS) % Y_CHIPS

    images, perm, numbers, outgoing = route_images(image_rows, image_route, section_place, fsdp_place)
    table = jnp.concatenate([chips, core[None], numbers]).astype(jnp.int32)

    w0 = jnp.stack([down_weight[0], up_weight[0]])
    w3, w1, w4 = to_next(w0), to_previous(w0), to_across(w0)
    sibling_x = to_sibling(section_inputs)
    moved = {id(w0): to_sibling(w0)}
    w2 = to_next(w3)
    up4 = w4[1]
    up5 = to_previous(up4)
    down57 = to_across(jnp.stack([w1[0], w3[0]]))
    round2 = (w2, up5, down57)
    up7 = to_next(hold(up4, round2))
    up6 = to_previous(up5)
    down6 = to_across(w2[0])
    for array in (w1, w3, w4):
        moved[id(array)] = to_sibling(hold(array, round2))
    for array in (w2, up5, down57, up7, up6, down6):
        moved[id(array)] = to_sibling(array)
    head, scaled_ct, inverse = prepare(
        hold(table, round2, sibling_x), section_inputs, value_cotangent, perm, images
    )
    sibling_head = to_sibling(head)
    sibling_ct = to_sibling(scaled_ct)
    down_own = [(w0, 0), (w1, 0), (w2, 0), (w3, 0), (w4, 0), (down57, 0), (down6, None), (down57, 1)]
    up_own = [(w0, 1), (w1, 1), (w2, 1), (w3, 1), (w4, 1), (up5, None), (up6, None), (up7, None)]
    down_sibling = [(moved[id(array)], at) for array, at in down_own]
    up_sibling = [(moved[id(array)], at) for array, at in up_own]

    up_groups = ((2, 5), (6, 3), (1,), (7,), (0, 4))
    down_groups = ((6,), (5, 7, 4), (2,), (1, 3), (0,))
    up_blocks = products(
        1, hold(table, up7, up6, down6, *moved.values()), section_inputs, sibling_x, head, sibling_head, scaled_ct, sibling_ct, up_groups
    )
    down_blocks = products(
        0, hold(table, up_blocks[0]), section_inputs, sibling_x, head, sibling_head, scaled_ct, sibling_ct, down_groups
    )

    far0_near1, far1_back0, near0, back1, own01 = up_blocks
    below1 = to_next(far0_near1)
    above0 = to_previous(far1_back0)
    send2, send130, keep2, keep13, keep0 = down_blocks
    half = keep2.shape[1] // 2
    came2, came130 = to_across(send2), to_across(send130)
    filled = layer(
        0,
        hold(table, down_blocks[0]),
        section_inputs, head, value_cotangent, scaled_ct, inverse, down_gain, down_own, down_sibling, (),
    )
    below1, above0, came2 = hold((below1, above0, came2), filled[0])
    up_near = near0[0] + below1[0]
    up_back = back1[0] + above0[0]
    down_far = keep2[0] + came2[0]
    down_below = to_next(down_far[:half])
    down_above = to_previous(down_far[half:])
    below0 = to_next(up_near)
    above1 = to_previous(up_back)

    values, input_grad = layer(
        1,
        hold(table, up_near, up_back, down_far),
        section_inputs, head, value_cotangent, scaled_ct, inverse, up_gain, up_own, up_sibling, tuple(filled),
    )
    below0, above1, down_below, down_above, came130 = hold(
        (below0, above1, down_below, down_above, came130), values
    )
    across = own01[1].astype(F32) + below1[1].astype(F32) + above1.astype(F32)
    kept = own01[0].astype(F32) + below0.astype(F32) + above0[1].astype(F32)
    across = to_across(across.astype(BF16))
    ups = keep13[0] + came130[0]
    downs = keep13[1] + came130[1]
    ups = jnp.concatenate([ups[:half] + down_below, ups[half:]])
    downs = jnp.concatenate([downs[:half], downs[half:] + down_above])
    below = to_next(ups)
    above = to_previous(downs)
    up_share = kept + across.astype(F32)
    down_share = keep0[0].astype(F32) + came130[2].astype(F32) + below.astype(F32) + above.astype(F32)

    shard = down_weight.shape[1]

    def gradients(weight, share, gain):
        part = lax.dynamic_slice(gain[0], (fsdp_place * shard,), (shard,)).astype(F32)
        return part[:, None] * share, jnp.sum(weight[0].astype(F32) * share, axis=1)

    up_weight_grad, up_gain_grad = gradients(up_weight, up_share, up_gain)
    down_weight_grad, down_gain_grad = gradients(down_weight, down_share, down_gain)
    moved_weight = to_mirror(up_weight_grad.astype(BF16))
    moved_gain = to_mirror(up_gain_grad.astype(BF16))
    weight_grad = (down_weight_grad + moved_weight.astype(F32))[None]
    gain_grad = (down_gain_grad + moved_gain.astype(F32))[None]
    return (values, input_grad, weight_grad, gain_grad)


def solution(mesh):
    return jax.shard_map(
        per_device,
        mesh=mesh,
        in_specs=(
            P(None, "section", "fsdp", None),
            P(None, "section", "fsdp", None),
            P("section", "fsdp", None),
            P("section", "fsdp", None),
            P("section", None),
            P("section", None),
            P(None, "fsdp", None),
            P(),
        ),
        out_specs=(
            P(None, "section", "fsdp", None),
            P(None, "section", "fsdp", None),
            P("section", "fsdp", None),
            P("section", "fsdp"),
        ),
        check_vma=False,
    )
```

```python
import jax
import jax.numpy as jnp
from jax import lax
from jax.experimental import pallas as pl
from jax.experimental.pallas import tpu as pltpu
from jax.sharding import PartitionSpec as P

BLOCK_ROWS = 4
CAP = 2
EPSILON = 1e-05
HEAD = 128
VMEM_BYTES = 60 * 1024 * 1024
SMALL = pl.CostEstimate(flops=1, bytes_accessed=1, transcendentals=0)
F32 = jnp.float32
BF16 = jnp.bfloat16

X_CHIPS, Y_CHIPS = 2, 4
CHIPS = X_CHIPS * Y_CHIPS
CORE, LIVE, FLAG, PART, PIPE, X_HALF = 8, 9, 10, 12, 15, 16


def fsdp_route(step):
    route = []
    for x in range(X_CHIPS):
        for y in range(Y_CHIPS):
            for core in range(2):
                to_x, to_y, to_core = step(x, y, core)
                target = (to_x % X_CHIPS * Y_CHIPS + to_y % Y_CHIPS) * 2 + to_core % 2
                route.append(((x * Y_CHIPS + y) * 2 + core, target))
    return route


def to_next(block):
    return lax.ppermute(block, "fsdp", fsdp_route(lambda x, y, core: (x, y + 1, core)))


def to_previous(block):
    return lax.ppermute(block, "fsdp", fsdp_route(lambda x, y, core: (x, y - 1, core)))


def to_across(block):
    return lax.ppermute(block, "fsdp", fsdp_route(lambda x, y, core: (x + 1, y, core)))


def to_sibling(block):
    return lax.ppermute(block, "fsdp", fsdp_route(lambda x, y, core: (x, y, core + 1)))


def to_mirror(block, flip):
    sections, fsdps = lax.axis_size("section"), lax.axis_size("fsdp")
    route = []
    for section in range(sections):
        for fsdp in range(fsdps):
            to_fsdp = (fsdp + flip * fsdps // X_CHIPS) % fsdps
            route.append((section * fsdps + fsdp, (sections - 1 - section) * fsdps + to_fsdp))
    return lax.ppermute(block, ("section", "fsdp"), route)


def columns(chip, size):
    return pl.ds(pl.multiple_of(chip * size, 128), size)


def inverse_rms(rows):
    tokens, width = rows.shape
    pair = width // CHIPS
    total = jnp.zeros((tokens, pair), F32)
    for chip in range(CHIPS):
        part = rows[:, chip * pair : (chip + 1) * pair].astype(F32)
        total = total + part * part
    return lax.rsqrt(jnp.sum(total, axis=1, keepdims=True) / width + EPSILON)


def scale_kernel(x_ref, ct_ref, ct_out, inverse_out):
    inverse = inverse_rms(x_ref.at[0, 0])
    ct_out[0, 0] = (ct_ref[0, 0].astype(F32) * inverse).astype(BF16)
    inverse_out[0] = jnp.broadcast_to(inverse, inverse_out.shape[1:])


def scale(section_inputs, cotangent):
    pipes, _, tokens, width = section_inputs.shape
    kv = cotangent.shape[3]
    tile = 64
    ct_spec = pl.BlockSpec((1, 1, tile, kv), lambda p, t: (p, 0, t, 0))
    return pl.pallas_call(
        scale_kernel,
        grid=(pipes, tokens // tile),
        in_specs=[pl.BlockSpec((1, 1, tile, width), lambda p, t: (p, 0, t, 0)), ct_spec],
        out_specs=[ct_spec, pl.BlockSpec((1, tile, 128), lambda p, t: (p, t, 0))],
        out_shape=[
            jax.ShapeDtypeStruct(cotangent.shape, BF16),
            jax.ShapeDtypeStruct((pipes, tokens, 128), F32),
        ],
        compiler_params=pltpu.CompilerParams(vmem_limit_bytes=VMEM_BYTES),
        cost_estimate=SMALL,
        name="scale",
    )(section_inputs, cotangent)


def patch_kernel(table, x_ref, ct_ref, perm_ref, im0, im1, im2, ct_in, inverse_in, head_ref, ct_out, inverse_out):
    pipe = table[PIPE]
    head_ref[...] = x_ref[0, 0]
    ct_out[...] = ct_in[...]
    inverse_out[...] = inverse_in[...]

    @pl.when(table[FLAG + pipe] == 1)
    def _():
        live = lax.broadcasted_iota(jnp.int32, (HEAD, 1), 0) < table[LIVE]
        for part, image in enumerate((im0, im1, im2)):
            where = pl.ds(pl.multiple_of(table[PART + part], 128), image.shape[1])
            arrived = jnp.dot(perm_ref[...], image[...], preferred_element_type=F32).astype(BF16)
            head_ref[:, where] = jnp.where(live, arrived, head_ref[:, where])
        inverse = inverse_rms(head_ref)
        ct_out[pipe, 0, :HEAD] = (ct_ref[0, 0].astype(F32) * inverse).astype(BF16)
        inverse_out[pipe, :HEAD] = jnp.broadcast_to(inverse, (HEAD, inverse_out.shape[2]))


def patch(table, section_inputs, cotangent, perm, images, scaled_ct, inverse):
    width = section_inputs.shape[3]
    kv = cotangent.shape[3]
    whole = pl.BlockSpec(memory_space=pltpu.VMEM)
    return pl.pallas_call(
        patch_kernel,
        grid_spec=pltpu.PrefetchScalarGridSpec(
            num_scalar_prefetch=1,
            grid=(1,),
            in_specs=[
                pl.BlockSpec((1, 1, HEAD, width), lambda i, table: (table[PIPE], 0, 0, 0)),
                pl.BlockSpec((1, 1, HEAD, kv), lambda i, table: (table[PIPE], 0, 0, 0)),
            ]
            + [whole] * 6,
            out_specs=[whole] * 3,
        ),
        out_shape=[
            jax.ShapeDtypeStruct((HEAD, width), BF16),
            jax.ShapeDtypeStruct(scaled_ct.shape, BF16),
            jax.ShapeDtypeStruct(inverse.shape, F32),
        ],
        compiler_params=pltpu.CompilerParams(vmem_limit_bytes=VMEM_BYTES),
        cost_estimate=SMALL,
        name="patch",
    )(table, section_inputs, cotangent, perm, *images, scaled_ct, inverse)


def pack(parts):
    count = len(parts)
    shape = parts[0][0].shape[-2:]

    def kernel(*refs):
        out, sems = refs[count:]
        copies = []
        for place, (ref, (_, at)) in enumerate(zip(refs, parts)):
            source = ref if at is None else ref.at[at]
            copies.append(pltpu.make_async_copy(source, out.at[place], sems.at[place]))
        for copy in copies:
            copy.start()
        for copy in copies:
            copy.wait()

    anywhere = pl.BlockSpec(memory_space=pl.ANY)
    return pl.pallas_call(
        kernel,
        in_specs=[anywhere] * count,
        out_specs=pl.BlockSpec(memory_space=pltpu.VMEM),
        out_shape=jax.ShapeDtypeStruct((count, *shape), BF16),
        scratch_shapes=[pltpu.SemaphoreType.DMA((count,))],
        compiler_params=pltpu.CompilerParams(vmem_limit_bytes=VMEM_BYTES),
        cost_estimate=SMALL,
        name="pack",
    )(*[array for array, _ in parts])


def start_columns(table, pipe, x_ref, head_ref, rows, sems, from_x, to_rows):
    flag = table[FLAG + pipe] == 1
    tail = pl.ds(HEAD, rows.shape[0] - HEAD)
    top = rows.at[pl.ds(0, HEAD), to_rows]
    plain = pltpu.make_async_copy(x_ref.at[pipe, 0, pl.ds(0, HEAD), from_x], top, sems.at[0])
    placed = pltpu.make_async_copy(head_ref.at[:, from_x], top, sems.at[0])
    rest = pltpu.make_async_copy(x_ref.at[pipe, 0, tail, from_x], rows.at[tail, to_rows], sems.at[1])
    pl.when(flag)(placed.start)
    pl.when(jnp.logical_not(flag))(plain.start)
    rest.start()
    return [plain, rest]


def products(table, x, sibling_x, head, sibling_head, ct, sibling_ct, groups):
    pipes, _, tokens, width = x.shape
    pair = width // CHIPS
    half = pair // 2
    window = -(-half // 128) * 128
    kv = ct.shape[3]
    order = [(g, i, *block) for g, group in enumerate(groups) for i, block in enumerate(group)]
    count = len(order)

    def kernel(table, x_ref, sibling_x_ref, head_ref, sibling_head_ref, own_ct, other_ct, *refs):
        outs = refs[: len(groups)]
        own, other, block, row_sems, out_sems = refs[len(groups) :]
        core = table[CORE]
        waits = []
        for n, (_, _, pipe, r) in enumerate(order):
            from_x = pl.ds(pl.multiple_of(table[r] * pair + core * (pair - window), 128), window)
            here = pl.ds(n * window, window)
            waits.append(
                start_columns(table, pipe, x_ref, head_ref, own, row_sems.at[n, 0], from_x, here)
                + start_columns(
                    table, pipe, sibling_x_ref, sibling_head_ref, other, row_sems.at[n, 1], from_x, here
                )
            )
        contract = (((0,), (0,)), ((), ()))
        written = []
        for n, (out, at, pipe, r) in enumerate(order):
            for copy in waits[n]:
                copy.wait()
            here = slice(n * window, (n + 1) * window)
            product = lax.dot_general(own[:, here], own_ct[pipe, 0], contract, preferred_element_type=F32)
            product += lax.dot_general(
                other[:, here], other_ct[pipe, 0], contract, preferred_element_type=F32
            )
            product = product.astype(BF16)

            @pl.when(core == 0)
            def _():
                block[n] = product[:half]

            @pl.when(core == 1)
            def _():
                block[n] = product[window - half :]

            copy = pltpu.make_async_copy(block.at[n], outs[out].at[at], out_sems.at[n])
            copy.start()
            written.append(copy)
        for copy in written:
            copy.wait()

    anywhere = pl.BlockSpec(memory_space=pl.ANY)
    whole = pl.BlockSpec(memory_space=pltpu.VMEM)
    return pl.pallas_call(
        kernel,
        in_specs=[pl.BlockSpec(memory_space=pltpu.SMEM)] + [anywhere] * 4 + [whole] * 2,
        out_specs=[anywhere for _ in groups],
        out_shape=[jax.ShapeDtypeStruct((len(g), half, kv), BF16) for g in groups],
        scratch_shapes=[
            pltpu.VMEM((tokens, count * window), BF16),
            pltpu.VMEM((tokens, count * window), BF16),
            pltpu.VMEM((count, half, kv), BF16),
            pltpu.SemaphoreType.DMA((count, 2, 2)),
            pltpu.SemaphoreType.DMA((count,)),
        ],
        compiler_params=pltpu.CompilerParams(vmem_limit_bytes=VMEM_BYTES),
        cost_estimate=SMALL,
        name="products",
    )(table, x, sibling_x, head, sibling_head, ct, sibling_ct)


def on_blocks(name, kernel, operands, outs):
    specs, arrays = [], []
    for operand in operands:
        array, at = operand if isinstance(operand, tuple) else (operand, None)
        shape = array.shape
        if len(shape) == 1:
            specs.append(pl.BlockSpec(memory_space=pltpu.SMEM))
        elif at is None:
            specs.append(pl.BlockSpec(shape, lambda i, n=len(shape): (0,) * n))
        else:
            specs.append(pl.BlockSpec((pl.squeezed, *shape[1:]), lambda i, at=at: (at, 0, 0)))
        arrays.append(array)
    return pl.pallas_call(
        kernel,
        grid=(1,),
        in_specs=specs,
        out_specs=[pl.BlockSpec(out.shape, lambda i, n=len(out.shape): (0,) * n) for out in outs],
        out_shape=outs,
        compiler_params=pltpu.CompilerParams(vmem_limit_bytes=VMEM_BYTES),
        cost_estimate=SMALL,
        name=name,
    )(*arrays)


def wide(*refs):
    total = refs[0][...].astype(F32)
    for ref in refs[1:]:
        total = total + ref[...].astype(F32)
    return total


def first_sums(near0, far0, near1, back1, far1, back0, keep2, came2, up, down):
    rows = near0.shape[0]
    half = rows // 2
    far = wide(keep2, came2).astype(BF16)
    up[:rows] = wide(near0, far0).astype(BF16)
    up[rows : 2 * rows] = near1[...]
    up[2 * rows :] = far[:half]
    down[:rows] = wide(back1, far1).astype(BF16)
    down[rows : 2 * rows] = back0[...]
    down[2 * rows :] = far[half:]


def gain_row(weight, share):
    products = weight[...].astype(F32) * share
    total = products[:, :128]
    for low in range(128, products.shape[1], 128):
        total = total + products[:, low : low + 128]
    return jnp.sum(jnp.transpose(total), axis=0, keepdims=True)


def gain_column(table, gain, chip):
    pair = gain.shape[1] // CHIPS
    both = gain[:, columns(chip, pair)].astype(F32)
    row = jnp.where(table[CORE] == 0, both[:, : pair // 2], both[:, pair // 2 :])
    return jnp.transpose(jnp.broadcast_to(row, (8, pair // 2)))[:, :1]


def mirror_sums(table, own0, own1, below, above, weight0, weight1, gain, here, there):
    rows = own0.shape[0]
    for out, own, low, high, weight, chip in (
        (here, own0, 0, rows, weight0, table[0]),
        (there, own1, rows, 0, weight1, table[Y_CHIPS]),
    ):
        share = wide(own, below.at[low : low + rows], above.at[high : high + rows])
        out[:rows] = (share * gain_column(table, gain, chip)).astype(BF16)
        out[rows:] = jnp.zeros((out.shape[0] - rows, out.shape[1]), BF16)
        out[rows : rows + 8, :rows] = jnp.broadcast_to(gain_row(weight, share), (8, rows)).astype(BF16)


def second_sums(keep1, came1, below, keep3, came3, above, ups, downs):
    rows = ups.shape[0]
    half = rows // 2
    ups[...] = wide(keep1, came1).astype(BF16)
    downs[...] = wide(keep3, came3).astype(BF16)
    ups[:half] = wide(ups.at[:half], below.at[2 * rows :]).astype(BF16)
    downs[half:] = wide(downs.at[half:], above.at[2 * rows :]).astype(BF16)


def last_sums(table, keep0, came0, below, above, weight, gain, mirrored0, mirrored1, weight_grad, gain_grad):
    share = wide(keep0, came0, below, above)
    rows = share.shape[0]
    moved = wide(mirrored0, mirrored1)
    weight_grad[0] = share * gain_column(table, gain, table[0]) + moved[:rows]
    gain_grad[...] = gain_row(weight, share) + moved[rows : rows + 1, :rows]


def layer(pipe, table, x, head, cotangent, scaled_ct, inverse, gain, own, sibling, carried):
    _, _, tokens, width = x.shape
    pair = width // CHIPS
    half = pair // 2
    kv = cotangent.shape[3]
    arrays = []
    for array, _ in [*own, *sibling]:
        if not any(array is known for known in arrays):
            arrays.append(array)
    position = [
        next(i for i, known in enumerate(arrays) if known is array) for array, _ in [*own, *sibling]
    ]
    index = [at for _, at in [*own, *sibling]]

    def kernel(table, x_ref, head_ref, ct_ref, scaled_ref, inverse_ref, gain_ref, *refs):
        pieces = refs[: len(arrays)]
        values_ref, grad_ref, rows, weight, grad, w_sems, x_sems, out_sems = refs[-8:]
        core = table[CORE]
        size = width // X_CHIPS
        row_waits = []
        for flip in range(X_CHIPS):
            half_x = table[X_HALF] if flip == 0 else 1 - table[X_HALF]
            where = columns(half_x, size)
            row_waits.append(start_columns(table, pipe, x_ref, head_ref, rows, x_sems.at[flip], where, where))
        waits = []
        for r in range(CHIPS):
            copies = []
            for side in range(2):
                piece = side * CHIPS + r
                source = pieces[position[piece]]
                if index[piece] is not None:
                    source = source.at[index[piece]]
                at = table[r] * pair + (core if side == 0 else 1 - core) * half
                copy = pltpu.make_async_copy(
                    source, weight.at[pl.ds(pl.multiple_of(at, 64), half)], w_sems.at[piece]
                )
                copy.start()
                copies.append(copy)
            waits.append(copies)
        values = jnp.zeros((tokens, kv), F32)
        for r in range(CHIPS):
            for copy in waits[r]:
                copy.wait()
            while row_waits[r // Y_CHIPS]:
                row_waits[r // Y_CHIPS].pop().wait()
            where = columns(table[r], pair)
            block = weight[pl.ds(pl.multiple_of(table[r] * pair, 128), pair)]
            values += jnp.dot(rows[:, where] * gain_ref[:, where], block, preferred_element_type=F32)
        inv = inverse_ref[0, :, :1]
        values = values * inv
        values_ref[0, 0] = values.astype(BF16)
        centre = jnp.sum(values * ct_ref[0, 0].astype(F32), axis=1, keepdims=True) / width
        pull = inv * inv * centre
        outs = []
        for chip in range(CHIPS):
            where = slice(chip * pair, (chip + 1) * pair)
            back = lax.dot_general(
                scaled_ref[0, 0], weight[where], (((1,), (1,)), ((), ())), preferred_element_type=F32
            )
            grad[:, where] = (
                back * gain_ref[:, where].astype(F32) - rows[:, where].astype(F32) * pull
            ).astype(BF16)
            if chip % 2 == 1:
                done = pl.ds((chip - 1) * pair, 2 * pair)
                copy = pltpu.make_async_copy(
                    grad.at[:, done], grad_ref.at[pipe, 0, :, done], out_sems.at[chip // 2]
                )
                copy.start()
                outs.append(copy)
        for copy in outs:
            copy.wait()

    anywhere = pl.BlockSpec(memory_space=pl.ANY)
    ct_spec = pl.BlockSpec((1, 1, tokens, kv), lambda i: (pipe, 0, 0, 0))
    operands = [table, x, head, cotangent, scaled_ct, inverse, gain, *arrays, *carried]
    return pl.pallas_call(
        kernel,
        grid=(1,),
        in_specs=[
            pl.BlockSpec(memory_space=pltpu.SMEM),
            anywhere,
            anywhere,
            ct_spec,
            ct_spec,
            pl.BlockSpec((1, tokens, 128), lambda i: (pipe, 0, 0)),
            pl.BlockSpec((1, width), lambda i: (0, 0)),
        ]
        + [anywhere] * (len(arrays) + len(carried)),
        out_specs=[ct_spec, anywhere],
        out_shape=[
            jax.ShapeDtypeStruct(cotangent.shape, BF16),
            jax.ShapeDtypeStruct(x.shape, BF16),
        ],
        scratch_shapes=[
            pltpu.VMEM((tokens, width), BF16),
            pltpu.VMEM((width, kv), BF16),
            pltpu.VMEM((tokens, width), BF16),
            pltpu.SemaphoreType.DMA((2 * CHIPS,)),
            pltpu.SemaphoreType.DMA((X_CHIPS, 2)),
            pltpu.SemaphoreType.DMA((CHIPS // 2,)),
        ],
        input_output_aliases={7 + len(arrays) + i: i for i in range(len(carried))},
        compiler_params=pltpu.CompilerParams(vmem_limit_bytes=VMEM_BYTES),
        cost_estimate=SMALL,
        name="layer",
    )(*operands)


def route_images(image_rows, image_route, section_place, fsdp_place):
    fsdp_count = lax.axis_size("fsdp")
    section_count = lax.axis_size("section")
    ring = section_count // 2
    width = image_rows.shape[2]
    size = -(-width // (3 * 128)) * 128
    pipe = section_place // ring
    z = section_place % ring
    enc_rows = image_rows.shape[1]
    enc_count = enc_rows // BLOCK_ROWS
    head = fsdp_count * CAP * BLOCK_ROWS
    routes = lax.dynamic_index_in_dim(image_route, pipe, 0, keepdims=False)
    own_route = lax.dynamic_index_in_dim(routes, fsdp_place, 0, keepdims=False)
    ids = jnp.arange(enc_count, dtype=jnp.int32)
    earlier = (own_route[:, None] == own_route[None, :]) & (ids[None, :] < ids[:, None])
    slot_of = own_route * CAP + jnp.sum(earlier.astype(jnp.int32), axis=1)
    goes_to = jnp.repeat(slot_of * BLOCK_ROWS, BLOCK_ROWS) + jnp.tile(
        jnp.arange(BLOCK_ROWS, dtype=jnp.int32), enc_count
    )
    row_ids = jnp.arange(head, dtype=jnp.int32)
    select = (row_ids[:, None] == goes_to[None, :]).astype(BF16)
    from_end = jnp.where(pipe == 0, z, ring - 1 - z)
    own_part = jnp.where(from_end == ring - 1, 2, jnp.minimum(from_end, 1))
    starts = jnp.array([0, size, width - size], jnp.int32)
    start = jnp.where(own_part == 0, 0, jnp.where(own_part == 1, size, width - size))
    part = lax.dynamic_slice(image_rows, (pipe, 0, start), (1, enc_rows, size))[0]
    outgoing = jnp.dot(select, part, preferred_element_type=F32).astype(BF16)
    incoming = lax.all_to_all(outgoing, "fsdp", split_axis=0, concat_axis=0, tiled=True)
    end = section_count - 1
    arrivals = jnp.sum((routes == fsdp_place).astype(jnp.int32), axis=1)
    offsets = jnp.cumsum(arrivals) - arrivals
    slot_rows = CAP * BLOCK_ROWS
    within = row_ids % slot_rows
    lands = jnp.repeat(offsets, slot_rows) * BLOCK_ROWS + within
    valid = within < jnp.repeat(arrivals, slot_rows) * BLOCK_ROWS
    lands = jnp.where(valid, lands, -1)
    perm = (jnp.arange(head, dtype=jnp.int32)[:, None] == lands[None, :]).astype(BF16)
    numbers = jnp.concatenate(
        [
            (jnp.sum(arrivals) * BLOCK_ROWS)[None],
            (section_place == 0).astype(jnp.int32)[None],
            (section_place == end).astype(jnp.int32)[None],
            starts,
            pipe[None],
        ]
    )
    return incoming, perm, numbers


def move_images(incoming):
    count = lax.axis_size("section")
    ring, end = count // 2, count - 1
    return [
        incoming,
        lax.ppermute(incoming, "section", [(1, 0), (end - 1, end)]),
        lax.ppermute(incoming, "section", [(ring - 1, 0), (end - ring + 1, end)]),
    ]


def hold(value, *before):
    return lax.optimization_barrier((value, before))[0]


def per_device(
    section_inputs,
    value_cotangent,
    down_weight,
    up_weight,
    down_gain,
    up_gain,
    image_rows,
    image_route,
):
    section_place = lax.axis_index("section")
    fsdp_place = lax.axis_index("fsdp")
    core = fsdp_place % 2
    y = fsdp_place // 2 % Y_CHIPS
    x = fsdp_place // (2 * Y_CHIPS)
    r = jnp.arange(CHIPS, dtype=jnp.int32)
    chips = (x ^ (r // Y_CHIPS)) * Y_CHIPS + (y + r % Y_CHIPS) % Y_CHIPS

    incoming, perm, numbers = route_images(image_rows, image_route, section_place, fsdp_place)
    table = jnp.concatenate([chips, core[None], numbers, x[None]]).astype(jnp.int32)

    shard, kv = down_weight.shape[1:]

    part = jax.ShapeDtypeStruct((shard, kv), BF16)

    sibling_x = to_sibling(section_inputs)
    w0 = pack([(down_weight, 0), (up_weight, 0)])
    w3, w1, w4 = to_next(w0), to_previous(w0), to_across(w0)
    scaled_ct, inverse = scale(section_inputs, value_cotangent)
    w3, w1, w4, incoming = hold((w3, w1, w4, incoming), scaled_ct, sibling_x)
    images = move_images(incoming)
    w2, w5, w7 = to_next(w3), to_previous(w4), to_across(w3)
    early = pack([(w0, 0), (w0, 1), (w1, 0), (w1, 1), (w3, 0), (w3, 1), (w4, 0), (w4, 1)])
    head, scaled_ct, inverse = patch(
        hold(table, early), section_inputs, value_cotangent, perm, images, scaled_ct, inverse
    )
    w2, w5, w7, head, scaled_ct = hold((w2, w5, w7, head, scaled_ct))
    sibling_head, sibling_ct = to_sibling(head), to_sibling(scaled_ct)
    down6, up6 = to_next(w7[0]), to_previous(w5[1])

    rows = (section_inputs, sibling_x, head, sibling_head, scaled_ct, sibling_ct)
    far0, far1, send2 = products(table, *rows, (((1, 2),), ((1, 6),), ((0, 6),)))
    middle = pack([(w2, 0), (w2, 1), (w5, 0), (w5, 1), (w7, 0), (hold(w7, far0), 1)])
    far0, far1, send2, down6, up6, middle = hold((far0, far1, send2, down6, up6, middle))
    from_below, from_above, came = to_next(far0[0]), to_previous(far1[0]), to_across(send2[0])
    sibling_early, sibling_middle = to_sibling(early), to_sibling(middle)
    near0, near1, back1, back0, keep2, send130, own01, keep13, keep0 = products(
        hold(table, middle),
        *rows,
        (
            ((1, 1),), ((1, 5),), ((1, 7),), ((1, 3),), ((0, 2),),
            ((0, 5), (0, 7), (0, 4)), ((1, 0), (1, 4)), ((0, 1), (0, 3)), ((0, 0),),
        ),
    )
    from_below, from_above, came = hold((from_below, from_above, came), keep0, sibling_early, sibling_middle)
    message = jax.ShapeDtypeStruct((2 * shard + shard // 2, kv), BF16)
    up, down = on_blocks(
        "first_sums",
        first_sums,
        [(near0, 0), from_below, (near1, 0), (back1, 0), from_above, (back0, 0), (keep2, 0), came],
        [message, message],
    )
    below, above = to_next(up), to_previous(down)
    came130 = to_across(hold(send130, up))

    down_places = ((0, 0), (0, 2), (1, 0), (0, 4), (0, 6), (1, 2), (2, None), (1, 4))
    up_places = ((0, 1), (0, 3), (1, 1), (0, 5), (0, 7), (1, 3), (3, None), (1, 5))
    own = (early, middle, down6, up6)
    sibling = (sibling_early, sibling_middle, to_sibling(hold(down6, up)), to_sibling(hold(up6, up)))

    def pieces(arrays, places):
        return [(arrays[array], at) for array, at in places]

    filled = layer(
        0,
        hold(table, up),
        section_inputs, head, value_cotangent, scaled_ct, inverse, down_gain,
        pieces(own, down_places), pieces(sibling, down_places), (),
    )
    below, above = hold((below, above), filled[0])
    payload = jax.ShapeDtypeStruct((shard + 16, kv), BF16)
    here, there = on_blocks(
        "mirror_sums",
        mirror_sums,
        [
            table, (own01, 0), (own01, 1), below, above, (up_weight, 0), (early, 7), up_gain,
        ],
        [payload, payload],
    )
    mirrored0, mirrored1 = to_mirror(here, 0), to_mirror(there, 1)
    ups, downs = on_blocks(
        "second_sums",
        second_sums,
        [(keep13, 0), (came130, 0), below, (keep13, 1), (came130, 1), above],
        [part, part],
    )
    last_below, last_above = to_next(ups), to_previous(downs)
    values, input_grad = layer(
        1,
        hold(table, ups),
        section_inputs, head, value_cotangent, scaled_ct, inverse, up_gain,
        pieces(own, up_places), pieces(sibling, up_places), tuple(filled),
    )
    mirrored0, mirrored1, last_below, last_above = hold((mirrored0, mirrored1, last_below, last_above), values)
    weight_grad, gain_grad = on_blocks(
        "last_sums",
        last_sums,
        [
            table, (keep0, 0), (came130, 2), last_below, last_above, (down_weight, 0), down_gain, mirrored0, mirrored1,
        ],
        [jax.ShapeDtypeStruct((1, shard, kv), F32), jax.ShapeDtypeStruct((1, shard), F32)],
    )
    return (values, input_grad, weight_grad, gain_grad)


def solution(mesh):
    return jax.shard_map(
        per_device,
        mesh=mesh,
        in_specs=(
            P(None, "section", "fsdp", None),
            P(None, "section", "fsdp", None),
            P("section", "fsdp", None),
            P("section", "fsdp", None),
            P("section", None),
            P("section", None),
            P(None, "fsdp", None),
            P(),
        ),
        out_specs=(
            P(None, "section", "fsdp", None),
            P(None, "section", "fsdp", None),
            P("section", "fsdp", None),
            P("section", "fsdp"),
        ),
        check_vma=False,
    )
```

```python
import jax
import jax.numpy as jnp
from jax import lax
from jax.experimental import pallas as pl
from jax.experimental.pallas import tpu as pltpu
from jax.sharding import PartitionSpec as P

BLOCK_ROWS = 4
CAP = 2
EPSILON = 1e-05
HEAD = 128
VMEM_BYTES = 63 * 1024 * 1024 + 512 * 1024
PATCH_VMEM_BYTES = VMEM_BYTES
SMALL = pl.CostEstimate(flops=1, bytes_accessed=1, transcendentals=0)
F32 = jnp.float32
BF16 = jnp.bfloat16

X_CHIPS, Y_CHIPS = 2, 4
CHIPS = X_CHIPS * Y_CHIPS
CORE, LIVE, FLAG, PART, PIPE, X_HALF = 8, 9, 10, 12, 15, 16


def fsdp_route(step):
    route = []
    for x in range(X_CHIPS):
        for y in range(Y_CHIPS):
            for core in range(2):
                to_x, to_y, to_core = step(x, y, core)
                target = (to_x % X_CHIPS * Y_CHIPS + to_y % Y_CHIPS) * 2 + to_core % 2
                route.append(((x * Y_CHIPS + y) * 2 + core, target))
    return route


def to_next(block):
    return lax.ppermute(block, "fsdp", fsdp_route(lambda x, y, core: (x, y + 1, core)))


def to_previous(block):
    return lax.ppermute(block, "fsdp", fsdp_route(lambda x, y, core: (x, y - 1, core)))


def to_across(block):
    return lax.ppermute(block, "fsdp", fsdp_route(lambda x, y, core: (x + 1, y, core)))


def to_sibling(block):
    return lax.ppermute(block, "fsdp", fsdp_route(lambda x, y, core: (x, y, core + 1)))


def to_mirror(block, flip):
    sections, fsdps = lax.axis_size("section"), lax.axis_size("fsdp")
    route = []
    for section in range(sections):
        for fsdp in range(fsdps):
            to_fsdp = (fsdp + flip * fsdps // X_CHIPS) % fsdps
            route.append((section * fsdps + fsdp, (sections - 1 - section) * fsdps + to_fsdp))
    return lax.ppermute(block, ("section", "fsdp"), route)


def columns(chip, size):
    return pl.ds(pl.multiple_of(chip * size, 128), size)


def core_window(width):
    return -(-(width // CHIPS // 2) // 128) * 128


def inverse_rms(rows):
    tokens, width = rows.shape
    pair = width // CHIPS
    total = jnp.zeros((tokens, pair), F32)
    for chip in range(CHIPS):
        part = rows[:, chip * pair : (chip + 1) * pair].astype(F32)
        total = total + part * part
    return lax.rsqrt(jnp.sum(total, axis=1, keepdims=True) / width + EPSILON)


def scale_kernel(x_ref, ct_ref, ct_out, inverse_out):
    inverse = inverse_rms(x_ref.at[0, 0])
    ct_out[0, 0] = (ct_ref[0, 0].astype(F32) * inverse).astype(BF16)
    inverse_out[0] = jnp.broadcast_to(inverse, inverse_out.shape[1:])


def scale(section_inputs, cotangent):
    pipes, _, tokens, width = section_inputs.shape
    kv = cotangent.shape[3]
    tile = 64
    ct_spec = pl.BlockSpec((1, 1, tile, kv), lambda p, t: (p, 0, t, 0))
    return pl.pallas_call(
        scale_kernel,
        grid=(pipes, tokens // tile),
        in_specs=[pl.BlockSpec((1, 1, tile, width), lambda p, t: (p, 0, t, 0)), ct_spec],
        out_specs=[ct_spec, pl.BlockSpec((1, tile, 128), lambda p, t: (p, t, 0))],
        out_shape=[
            jax.ShapeDtypeStruct(cotangent.shape, BF16),
            jax.ShapeDtypeStruct((pipes, tokens, 128), F32),
        ],
        compiler_params=pltpu.CompilerParams(vmem_limit_bytes=VMEM_BYTES),
        cost_estimate=SMALL,
        name="scale",
    )(section_inputs, cotangent)


def patch_kernel(
    table, x_ref, ct_ref, perm_ref, ct_in, inverse_in, im0, im1, im2, head_ref, other_ref, ct_out, inverse_out, images, sems
):
    pipe = table[PIPE]
    head_ref[...] = x_ref[0, 0]
    ct_out[...] = ct_in[...]
    inverse_out[...] = inverse_in[...]

    @pl.when(table[FLAG + pipe] == 1)
    def _():
        live = lax.broadcasted_iota(jnp.int32, (HEAD, 1), 0) < table[LIVE]
        copies = [
            pltpu.make_async_copy(image, images.at[part], sems.at[part])
            for part, image in enumerate((im0, im1, im2))
        ]
        for copy in copies:
            copy.start()
        for part, copy in enumerate(copies):
            copy.wait()
            where = pl.ds(pl.multiple_of(table[PART + part], 128), images.shape[2])
            arrived = jnp.dot(perm_ref[...], images[part], preferred_element_type=F32).astype(BF16)
            head_ref[:, where] = jnp.where(live, arrived, head_ref[:, where])
        inverse = inverse_rms(head_ref)
        ct_out[pipe, 0, :HEAD] = (ct_ref[0, 0].astype(F32) * inverse).astype(BF16)
        inverse_out[pipe, :HEAD] = jnp.broadcast_to(inverse, (HEAD, inverse_out.shape[2]))

    pair = head_ref.shape[1] // CHIPS
    window = other_ref.shape[1] // CHIPS
    for chip in range(CHIPS):
        start = chip * pair + (1 - table[CORE]) * (pair - window)
        other_ref[:, chip * window : (chip + 1) * window] = head_ref[
            :, pl.ds(pl.multiple_of(start, 128), window)
        ]


def patch(table, section_inputs, cotangent, perm, images, scaled_ct, inverse):
    width = section_inputs.shape[3]
    kv = cotangent.shape[3]
    whole = pl.BlockSpec(memory_space=pltpu.VMEM)
    return pl.pallas_call(
        patch_kernel,
        grid_spec=pltpu.PrefetchScalarGridSpec(
            num_scalar_prefetch=1,
            grid=(1,),
            in_specs=[
                pl.BlockSpec((1, 1, HEAD, width), lambda i, table: (table[PIPE], 0, 0, 0)),
                pl.BlockSpec((1, 1, HEAD, kv), lambda i, table: (table[PIPE], 0, 0, 0)),
            ]
            + [whole] * 3
            + [pl.BlockSpec(memory_space=pl.ANY)] * 3,
            out_specs=[whole] * 4,
            scratch_shapes=[
                pltpu.VMEM((3, *images[0].shape), BF16),
                pltpu.SemaphoreType.DMA((3,)),
            ],
        ),
        out_shape=[
            jax.ShapeDtypeStruct((HEAD, width), BF16),
            jax.ShapeDtypeStruct((HEAD, CHIPS * core_window(width)), BF16),
            jax.ShapeDtypeStruct(scaled_ct.shape, BF16),
            jax.ShapeDtypeStruct(inverse.shape, F32),
        ],
        compiler_params=pltpu.CompilerParams(vmem_limit_bytes=PATCH_VMEM_BYTES),
        cost_estimate=SMALL,
        name="patch",
    )(table, section_inputs, cotangent, perm, scaled_ct, inverse, *images)


def pack(parts):
    count = len(parts)
    shape = parts[0][0].shape[-2:]

    def kernel(*refs):
        out, sems = refs[count:]
        copies = []
        for place, (ref, (_, at)) in enumerate(zip(refs, parts)):
            source = ref if at is None else ref.at[at]
            copies.append(pltpu.make_async_copy(source, out.at[place], sems.at[place]))
        for copy in copies:
            copy.start()
        for copy in copies:
            copy.wait()

    anywhere = pl.BlockSpec(memory_space=pl.ANY)
    return pl.pallas_call(
        kernel,
        in_specs=[anywhere] * count,
        out_specs=pl.BlockSpec(memory_space=pltpu.VMEM),
        out_shape=jax.ShapeDtypeStruct((count, *shape), BF16),
        scratch_shapes=[pltpu.SemaphoreType.DMA((count,))],
        compiler_params=pltpu.CompilerParams(vmem_limit_bytes=VMEM_BYTES),
        cost_estimate=SMALL,
        name="pack",
    )(*[array for array, _ in parts])


def start_columns(table, pipe, x_ref, head_ref, rows, sems, from_x, to_rows, from_head=None):
    from_head = from_x if from_head is None else from_head
    flag = table[FLAG + pipe] == 1
    tail = pl.ds(HEAD, rows.shape[0] - HEAD)
    top = rows.at[pl.ds(0, HEAD), to_rows]
    plain = pltpu.make_async_copy(x_ref.at[pipe, 0, pl.ds(0, HEAD), from_x], top, sems.at[0])
    placed = pltpu.make_async_copy(head_ref.at[:, from_head], top, sems.at[0])
    rest = pltpu.make_async_copy(x_ref.at[pipe, 0, tail, from_x], rows.at[tail, to_rows], sems.at[1])
    pl.when(flag)(placed.start)
    pl.when(jnp.logical_not(flag))(plain.start)
    rest.start()
    return [plain, rest]


def products(table, x, sibling_x, head, sibling_head, ct, sibling_ct, groups):
    pipes, _, tokens, width = x.shape
    pair = width // CHIPS
    half = pair // 2
    window = core_window(width)
    kv = ct.shape[3]
    order = [(g, i, *block) for g, group in enumerate(groups) for i, block in enumerate(group)]
    count = len(order)

    def kernel(table, x_ref, sibling_x_ref, head_ref, sibling_head_ref, own_ct, other_ct, *refs):
        outs = refs[: len(groups)]
        own, other, block, row_sems, out_sems = refs[len(groups) :]
        core = table[CORE]
        waits = []
        for n, (_, _, pipe, r) in enumerate(order):
            from_x = pl.ds(pl.multiple_of(table[r] * pair + core * (pair - window), 128), window)
            here = pl.ds(n * window, window)
            waits.append(
                start_columns(table, pipe, x_ref, head_ref, own, row_sems.at[n, 0], from_x, here)
                + start_columns(
                    table, pipe, sibling_x_ref, sibling_head_ref, other, row_sems.at[n, 1], from_x, here,
                    columns(table[r], window),
                )
            )
        contract = (((0,), (0,)), ((), ()))
        written = []
        for n, (out, at, pipe, r) in enumerate(order):
            for copy in waits[n]:
                copy.wait()
            here = slice(n * window, (n + 1) * window)
            product = lax.dot_general(own[:, here], own_ct[pipe, 0], contract, preferred_element_type=F32)
            product += lax.dot_general(
                other[:, here], other_ct[pipe, 0], contract, preferred_element_type=F32
            )
            product = product.astype(BF16)

            @pl.when(core == 0)
            def _():
                block[n] = product[:half]

            @pl.when(core == 1)
            def _():
                block[n] = product[window - half :]

            copy = pltpu.make_async_copy(block.at[n], outs[out].at[at], out_sems.at[n])
            copy.start()
            written.append(copy)
        for copy in written:
            copy.wait()

    anywhere = pl.BlockSpec(memory_space=pl.ANY)
    whole = pl.BlockSpec(memory_space=pltpu.VMEM)
    return pl.pallas_call(
        kernel,
        in_specs=[pl.BlockSpec(memory_space=pltpu.SMEM)] + [anywhere] * 4 + [whole] * 2,
        out_specs=[anywhere for _ in groups],
        out_shape=[jax.ShapeDtypeStruct((len(g), half, kv), BF16) for g in groups],
        scratch_shapes=[
            pltpu.VMEM((tokens, count * window), BF16),
            pltpu.VMEM((tokens, count * window), BF16),
            pltpu.VMEM((count, half, kv), BF16),
            pltpu.SemaphoreType.DMA((count, 2, 2)),
            pltpu.SemaphoreType.DMA((count,)),
        ],
        compiler_params=pltpu.CompilerParams(vmem_limit_bytes=VMEM_BYTES),
        cost_estimate=SMALL,
        name="products",
    )(table, x, sibling_x, head, sibling_head, ct, sibling_ct)


def on_blocks(name, kernel, operands, outs):
    specs, arrays = [], []
    for operand in operands:
        array, at = operand if isinstance(operand, tuple) else (operand, None)
        shape = array.shape
        if len(shape) == 1:
            specs.append(pl.BlockSpec(memory_space=pltpu.SMEM))
        elif at is None:
            specs.append(pl.BlockSpec(shape, lambda i, n=len(shape): (0,) * n))
        else:
            specs.append(pl.BlockSpec((pl.squeezed, *shape[1:]), lambda i, at=at: (at, 0, 0)))
        arrays.append(array)
    return pl.pallas_call(
        kernel,
        grid=(1,),
        in_specs=specs,
        out_specs=[pl.BlockSpec(out.shape, lambda i, n=len(out.shape): (0,) * n) for out in outs],
        out_shape=outs,
        compiler_params=pltpu.CompilerParams(vmem_limit_bytes=VMEM_BYTES),
        cost_estimate=SMALL,
        name=name,
    )(*arrays)


def wide(*refs):
    total = refs[0][...].astype(F32)
    for ref in refs[1:]:
        total = total + ref[...].astype(F32)
    return total


def halves(first, second, first_out, second_out):
    first_out[...] = first[...]
    second_out[...] = second[...]


def first_sums(near0, far0, back1, far1, keep2, came2, up, down):
    rows = near0.shape[0]
    half = rows // 2
    far = wide(keep2, came2).astype(BF16)
    up[:rows] = wide(near0, far0).astype(BF16)
    up[rows:] = far[:half]
    down[:rows] = wide(back1, far1).astype(BF16)
    down[rows:] = far[half:]


def gain_row(weight, share):
    products = weight[...].astype(F32) * share
    total = products[:, :128]
    for low in range(128, products.shape[1], 128):
        total = total + products[:, low : low + 128]
    return jnp.sum(jnp.transpose(total), axis=0, keepdims=True)


def gain_column(table, gain, chip):
    pair = gain.shape[1] // CHIPS
    both = gain[:, columns(chip, pair)].astype(F32)
    row = jnp.where(table[CORE] == 0, both[:, : pair // 2], both[:, pair // 2 :])
    return jnp.transpose(jnp.broadcast_to(row, (8, pair // 2)))[:, :1]


def mirror_sums(table, own0, below0, above0, own1, below1, above1, weight0, weight1, gain, here, there):
    rows = own0.shape[0]
    for out, sums, weight, chip in (
        (here, (own0, below0.at[:rows], above0), weight0, table[0]),
        (there, (own1, below1, above1.at[:rows]), weight1, table[Y_CHIPS]),
    ):
        share = wide(*sums)
        out[:rows] = (share * gain_column(table, gain, chip)).astype(BF16)
        out[rows:] = jnp.zeros((out.shape[0] - rows, out.shape[1]), BF16)
        out[rows : rows + 8, :rows] = jnp.broadcast_to(gain_row(weight, share), (8, rows)).astype(BF16)


def second_sums(keep1, came1, below, keep3, came3, above, ups, downs):
    rows = ups.shape[0]
    half = rows // 2
    ups[...] = wide(keep1, came1).astype(BF16)
    downs[...] = wide(keep3, came3).astype(BF16)
    ups[:half] = wide(ups.at[:half], below.at[rows:]).astype(BF16)
    downs[half:] = wide(downs.at[half:], above.at[rows:]).astype(BF16)


def down_sums(table, keep0, came0, below, above, weight, gain, weight_part, gain_part):
    share = wide(keep0, came0, below, above)
    weight_part[...] = share * gain_column(table, gain, table[0])
    gain_part[...] = gain_row(weight, share)


def last_sums(weight_part, gain_part, mirrored0, mirrored1, weight_grad, gain_grad):
    rows = weight_part.shape[0]
    moved = wide(mirrored0, mirrored1)
    weight_grad[0] = weight_part[...] + moved[:rows]
    gain_grad[...] = gain_part[...] + moved[rows : rows + 1, :rows]


def layer(pipe, table, x, head, cotangent, scaled_ct, inverse, gain, own, sibling, carried):
    _, _, tokens, width = x.shape
    pair = width // CHIPS
    half = pair // 2
    kv = cotangent.shape[3]
    arrays = []
    for array, _ in [*own, *sibling]:
        if not any(array is known for known in arrays):
            arrays.append(array)
    position = [
        next(i for i, known in enumerate(arrays) if known is array) for array, _ in [*own, *sibling]
    ]
    index = [at for _, at in [*own, *sibling]]

    def kernel(table, x_ref, head_ref, ct_ref, scaled_ref, inverse_ref, gain_ref, *refs):
        pieces = refs[: len(arrays)]
        values_ref, grad_ref, rows, weight, grad, w_sems, x_sems, out_sems = refs[-8:]
        core = table[CORE]
        size = width // X_CHIPS
        row_waits = []
        for flip in range(X_CHIPS):
            half_x = table[X_HALF] if flip == 0 else 1 - table[X_HALF]
            where = columns(half_x, size)
            row_waits.append(start_columns(table, pipe, x_ref, head_ref, rows, x_sems.at[flip], where, where))
        waits = []
        for r in range(CHIPS):
            copies = []
            for side in range(2):
                piece = side * CHIPS + r
                source = pieces[position[piece]]
                if index[piece] is not None:
                    source = source.at[index[piece]]
                at = table[r] * pair + (core if side == 0 else 1 - core) * half
                copy = pltpu.make_async_copy(
                    source, weight.at[pl.ds(pl.multiple_of(at, 64), half)], w_sems.at[piece]
                )
                copy.start()
                copies.append(copy)
            waits.append(copies)
        values = jnp.zeros((tokens, kv), F32)
        for r in range(CHIPS):
            for copy in waits[r]:
                copy.wait()
            while row_waits[r // Y_CHIPS]:
                row_waits[r // Y_CHIPS].pop().wait()
            where = columns(table[r], pair)
            block = weight[pl.ds(pl.multiple_of(table[r] * pair, 128), pair)]
            values += jnp.dot(rows[:, where] * gain_ref[:, where], block, preferred_element_type=F32)
        inv = inverse_ref[0, :, :1]
        values = values * inv
        values_ref[0, 0] = values.astype(BF16)
        centre = jnp.sum(values * ct_ref[0, 0].astype(F32), axis=1, keepdims=True) / width
        pull = inv * inv * centre
        outs = []
        for chip in range(CHIPS):
            where = slice(chip * pair, (chip + 1) * pair)
            back = lax.dot_general(
                scaled_ref[0, 0], weight[where], (((1,), (1,)), ((), ())), preferred_element_type=F32
            )
            grad[:, where] = (
                back * gain_ref[:, where].astype(F32) - rows[:, where].astype(F32) * pull
            ).astype(BF16)
            if chip % 2 == 1:
                done = pl.ds((chip - 1) * pair, 2 * pair)
                copy = pltpu.make_async_copy(
                    grad.at[:, done], grad_ref.at[pipe, 0, :, done], out_sems.at[chip // 2]
                )
                copy.start()
                outs.append(copy)
        for copy in outs:
            copy.wait()

    anywhere = pl.BlockSpec(memory_space=pl.ANY)
    ct_spec = pl.BlockSpec((1, 1, tokens, kv), lambda i: (pipe, 0, 0, 0))
    operands = [table, x, head, cotangent, scaled_ct, inverse, gain, *arrays, *carried]
    return pl.pallas_call(
        kernel,
        grid=(1,),
        in_specs=[
            pl.BlockSpec(memory_space=pltpu.SMEM),
            anywhere,
            anywhere,
            ct_spec,
            ct_spec,
            pl.BlockSpec((1, tokens, 128), lambda i: (pipe, 0, 0)),
            pl.BlockSpec((1, width), lambda i: (0, 0)),
        ]
        + [anywhere] * (len(arrays) + len(carried)),
        out_specs=[ct_spec, anywhere],
        out_shape=[
            jax.ShapeDtypeStruct(cotangent.shape, BF16),
            jax.ShapeDtypeStruct(x.shape, BF16),
        ],
        scratch_shapes=[
            pltpu.VMEM((tokens, width), BF16),
            pltpu.VMEM((width, kv), BF16),
            pltpu.VMEM((tokens, width), BF16),
            pltpu.SemaphoreType.DMA((2 * CHIPS,)),
            pltpu.SemaphoreType.DMA((X_CHIPS, 2)),
            pltpu.SemaphoreType.DMA((CHIPS // 2,)),
        ],
        input_output_aliases={7 + len(arrays) + i: i for i in range(len(carried))},
        compiler_params=pltpu.CompilerParams(vmem_limit_bytes=VMEM_BYTES),
        cost_estimate=SMALL,
        name="layer",
    )(*operands)


def route_images(image_rows, image_route, section_place, fsdp_place):
    fsdp_count = lax.axis_size("fsdp")
    section_count = lax.axis_size("section")
    ring = section_count // 2
    width = image_rows.shape[2]
    size = -(-width // (3 * 128)) * 128
    pipe = section_place // ring
    z = section_place % ring
    enc_rows = image_rows.shape[1]
    enc_count = enc_rows // BLOCK_ROWS
    head = fsdp_count * CAP * BLOCK_ROWS
    routes = lax.dynamic_index_in_dim(image_route, pipe, 0, keepdims=False)
    own_route = lax.dynamic_index_in_dim(routes, fsdp_place, 0, keepdims=False)
    ids = jnp.arange(enc_count, dtype=jnp.int32)
    earlier = (own_route[:, None] == own_route[None, :]) & (ids[None, :] < ids[:, None])
    slot_of = own_route * CAP + jnp.sum(earlier.astype(jnp.int32), axis=1)
    goes_to = jnp.repeat(slot_of * BLOCK_ROWS, BLOCK_ROWS) + jnp.tile(
        jnp.arange(BLOCK_ROWS, dtype=jnp.int32), enc_count
    )
    row_ids = jnp.arange(head, dtype=jnp.int32)
    select = (row_ids[:, None] == goes_to[None, :]).astype(BF16)
    from_end = jnp.where(pipe == 0, z, ring - 1 - z)
    own_part = jnp.where(from_end == ring - 1, 2, jnp.minimum(from_end, 1))
    starts = jnp.array([0, size, width - size], jnp.int32)
    start = jnp.where(own_part == 0, 0, jnp.where(own_part == 1, size, width - size))
    part = lax.dynamic_slice(image_rows, (pipe, 0, start), (1, enc_rows, size))[0]
    outgoing = jnp.dot(select, part, preferred_element_type=F32).astype(BF16)
    incoming = lax.all_to_all(outgoing, "fsdp", split_axis=0, concat_axis=0, tiled=True)
    end = section_count - 1
    arrivals = jnp.sum((routes == fsdp_place).astype(jnp.int32), axis=1)
    offsets = jnp.cumsum(arrivals) - arrivals
    slot_rows = CAP * BLOCK_ROWS
    within = row_ids % slot_rows
    lands = jnp.repeat(offsets, slot_rows) * BLOCK_ROWS + within
    valid = within < jnp.repeat(arrivals, slot_rows) * BLOCK_ROWS
    lands = jnp.where(valid, lands, -1)
    perm = (jnp.arange(head, dtype=jnp.int32)[:, None] == lands[None, :]).astype(BF16)
    numbers = jnp.concatenate(
        [
            (jnp.sum(arrivals) * BLOCK_ROWS)[None],
            (section_place == 0).astype(jnp.int32)[None],
            (section_place == end).astype(jnp.int32)[None],
            starts,
            pipe[None],
        ]
    )
    return incoming, perm, numbers


def move_images(incoming):
    count = lax.axis_size("section")
    ring, end = count // 2, count - 1
    return [
        incoming,
        lax.ppermute(incoming, "section", [(1, 0), (end - 1, end)]),
        lax.ppermute(incoming, "section", [(ring - 1, 0), (end - ring + 1, end)]),
    ]


def hold(value, *before):
    return lax.optimization_barrier((value, before))[0]


def per_device(
    section_inputs,
    value_cotangent,
    down_weight,
    up_weight,
    down_gain,
    up_gain,
    image_rows,
    image_route,
):
    section_place = lax.axis_index("section")
    fsdp_place = lax.axis_index("fsdp")
    core = fsdp_place % 2
    y = fsdp_place // 2 % Y_CHIPS
    x = fsdp_place // (2 * Y_CHIPS)
    r = jnp.arange(CHIPS, dtype=jnp.int32)
    chips = (x ^ (r // Y_CHIPS)) * Y_CHIPS + (y + r % Y_CHIPS) % Y_CHIPS

    incoming, perm, numbers = route_images(image_rows, image_route, section_place, fsdp_place)
    table = jnp.concatenate([chips, core[None], numbers, x[None]]).astype(jnp.int32)

    shard, kv = down_weight.shape[1:]

    part = jax.ShapeDtypeStruct((shard, kv), BF16)

    sibling_x = to_sibling(section_inputs)
    w0 = pack([(down_weight, 0), (up_weight, 0)])
    w3, w1, w4 = to_next(w0), to_previous(w0), to_across(w0)
    scaled_ct, inverse = scale(section_inputs, value_cotangent)
    w3, w1, w4, incoming = hold((w3, w1, w4, incoming), scaled_ct, sibling_x)
    images = move_images(incoming)
    w2, w5, w7 = to_next(w3), to_previous(w4), to_across(w3)
    early = pack([(w0, 0), (w0, 1), (w1, 0), (w1, 1), (w3, 0), (w3, 1), (w4, 0), (w4, 1)])
    head, other_head, scaled_ct, inverse = patch(
        hold(table, early), section_inputs, value_cotangent, perm, images, scaled_ct, inverse
    )
    w2, w5, w7, other_head, scaled_ct, early = hold((w2, w5, w7, other_head, scaled_ct, early))
    sibling_head, sibling_ct = to_sibling(other_head), to_sibling(scaled_ct)
    down7, up5 = on_blocks("halves", halves, [(w7, 0), (w5, 1)], [part, part])
    down6, up6 = to_next(down7), to_previous(up5)

    rows = (section_inputs, sibling_x, head, sibling_head, scaled_ct, sibling_ct)
    far0_near1, far1_back0, send20 = products(
        table, *rows, (((1, 2), (1, 5)), ((1, 6), (1, 3)), ((0, 6), (0, 4)))
    )
    far0_near1, far1_back0, send20, down6, up6, w7, early = hold(
        (far0_near1, far1_back0, send20, down6, up6, w7, early)
    )
    sibling_early = to_sibling(early)
    from_below, from_above, came20 = to_next(far0_near1), to_previous(far1_back0), to_across(send20)
    down_places = ((0, 0), (0, 2), (1, 0), (0, 4), (0, 6), (1, 2), (2, None), (1, 4))
    up_places = ((0, 1), (0, 3), (1, 1), (0, 5), (0, 7), (1, 3), (3, None), (1, 5))
    near0, back1, keep2, send13, own01, keep13, keep0 = products(
        hold(table, up6),
        *rows,
        (((1, 1),), ((1, 7),), ((0, 2),), ((0, 5), (0, 7)), ((1, 0), (1, 4)), ((0, 1), (0, 3)), ((0, 0),)),
    )

    def pieces(arrays, places):
        return [(arrays[array], at) for array, at in places]

    middle = pack([(w2, 0), (w2, 1), (w5, 0), (w5, 1), (w7, 0), (w7, 1)])
    from_below, from_above, came20, send13 = hold(
        (from_below, from_above, came20, send13), keep0, middle, sibling_early
    )
    message = jax.ShapeDtypeStruct((shard + shard // 2, kv), BF16)
    up, down = on_blocks(
        "first_sums",
        first_sums,
        [(near0, 0), (from_below, 0), (back1, 0), (from_above, 0), (keep2, 0), (came20, 0)],
        [message, message],
    )
    below, above = to_next(up), to_previous(down)
    came13 = to_across(hold(send13, up))
    own = (early, middle, down6, up6)
    sibling = [sibling_early, *[to_sibling(hold(array, up)) for array in (middle, down6, up6)]]
    filled = layer(
        0,
        hold(table, up),
        section_inputs, head, value_cotangent, scaled_ct, inverse, down_gain,
        pieces(own, down_places), pieces(sibling, down_places), (),
    )
    below, above = hold((below, above), filled[0])
    payload = jax.ShapeDtypeStruct((shard + 16, kv), BF16)
    here, there = on_blocks(
        "mirror_sums",
        mirror_sums,
        [
            table, (own01, 0), below, (from_above, 1), (own01, 1), (from_below, 1), above,
            (up_weight, 0), (early, 7), up_gain,
        ],
        [payload, payload],
    )
    mirrored0, mirrored1 = to_mirror(here, 0), to_mirror(there, 1)
    ups, downs = on_blocks(
        "second_sums",
        second_sums,
        [(keep13, 0), (came13, 0), below, (keep13, 1), (came13, 1), above],
        [part, part],
    )
    last_below, last_above = to_next(ups), to_previous(downs)
    values, input_grad = layer(
        1,
        hold(table, ups),
        section_inputs, head, value_cotangent, scaled_ct, inverse, up_gain,
        pieces(own, up_places), pieces(sibling, up_places), tuple(filled),
    )
    last_below, last_above = hold((last_below, last_above), values)
    weight_part, gain_part = on_blocks(
        "down_sums",
        down_sums,
        [table, (keep0, 0), (came20, 1), last_below, last_above, (down_weight, 0), down_gain],
        [jax.ShapeDtypeStruct((shard, kv), F32), jax.ShapeDtypeStruct((1, shard), F32)],
    )
    mirrored0, mirrored1 = hold((mirrored0, mirrored1), weight_part)
    weight_grad, gain_grad = on_blocks(
        "last_sums",
        last_sums,
        [weight_part, gain_part, mirrored0, mirrored1],
        [jax.ShapeDtypeStruct((1, shard, kv), F32), jax.ShapeDtypeStruct((1, shard), F32)],
    )
    return (values, input_grad, weight_grad, gain_grad)


def solution(mesh):
    return jax.shard_map(
        per_device,
        mesh=mesh,
        in_specs=(
            P(None, "section", "fsdp", None),
            P(None, "section", "fsdp", None),
            P("section", "fsdp", None),
            P("section", "fsdp", None),
            P("section", None),
            P("section", None),
            P(None, "fsdp", None),
            P(),
        ),
        out_specs=(
            P(None, "section", "fsdp", None),
            P(None, "section", "fsdp", None),
            P("section", "fsdp", None),
            P("section", "fsdp"),
        ),
        check_vma=False,
    )
```

```python
import jax
import jax.numpy as jnp
from jax import lax
from jax.experimental import pallas as pl
from jax.experimental.pallas import tpu as pltpu
from jax.sharding import PartitionSpec as P

BLOCK_ROWS = 4
CAP = 2
EPSILON = 1e-05
HEAD = 128
VMEM_BYTES = 63 * 1024 * 1024 + 512 * 1024
SMALL = pl.CostEstimate(flops=1, bytes_accessed=1, transcendentals=0)
F32 = jnp.float32
BF16 = jnp.bfloat16

X_CHIPS, Y_CHIPS = 2, 4
CHIPS = X_CHIPS * Y_CHIPS
CORE, LIVE, FLAG, PART, PIPE, X_HALF = 8, 9, 10, 12, 15, 16


def fsdp_route(step):
    route = []
    for x in range(X_CHIPS):
        for y in range(Y_CHIPS):
            for core in range(2):
                to_x, to_y, to_core = step(x, y, core)
                target = (to_x % X_CHIPS * Y_CHIPS + to_y % Y_CHIPS) * 2 + to_core % 2
                route.append(((x * Y_CHIPS + y) * 2 + core, target))
    return route


def to_next(block):
    return lax.ppermute(block, "fsdp", fsdp_route(lambda x, y, core: (x, y + 1, core)))


def to_previous(block):
    return lax.ppermute(block, "fsdp", fsdp_route(lambda x, y, core: (x, y - 1, core)))


def to_across(block):
    return lax.ppermute(block, "fsdp", fsdp_route(lambda x, y, core: (x + 1, y, core)))


def to_sibling(block):
    return lax.ppermute(block, "fsdp", fsdp_route(lambda x, y, core: (x, y, core + 1)))


def to_mirror(block, flip):
    sections, fsdps = lax.axis_size("section"), lax.axis_size("fsdp")
    route = []
    for section in range(sections):
        for fsdp in range(fsdps):
            to_fsdp = (fsdp + flip * fsdps // X_CHIPS) % fsdps
            route.append((section * fsdps + fsdp, (sections - 1 - section) * fsdps + to_fsdp))
    return lax.ppermute(block, ("section", "fsdp"), route)


def columns(chip, size):
    return pl.ds(pl.multiple_of(chip * size, 128), size)


def core_window(width):
    return -(-(width // CHIPS // 2) // 128) * 128


def inverse_rms(rows):
    tokens, width = rows.shape
    pair = width // CHIPS
    total = jnp.zeros((tokens, pair), F32)
    for chip in range(CHIPS):
        part = rows[:, chip * pair : (chip + 1) * pair].astype(F32)
        total = total + part * part
    return lax.rsqrt(jnp.sum(total, axis=1, keepdims=True) / width + EPSILON)


def scale_kernel(x_ref, ct_ref, ct_out, inverse_out):
    inverse = inverse_rms(x_ref.at[0, 0])
    ct_out[0, 0] = (ct_ref[0, 0].astype(F32) * inverse).astype(BF16)
    inverse_out[0] = jnp.broadcast_to(inverse, inverse_out.shape[1:])


def scale(section_inputs, cotangent):
    pipes, _, tokens, width = section_inputs.shape
    kv = cotangent.shape[3]
    tile = 64
    ct_spec = pl.BlockSpec((1, 1, tile, kv), lambda p, t: (p, 0, t, 0))
    return pl.pallas_call(
        scale_kernel,
        grid=(pipes, tokens // tile),
        in_specs=[pl.BlockSpec((1, 1, tile, width), lambda p, t: (p, 0, t, 0)), ct_spec],
        out_specs=[ct_spec, pl.BlockSpec((1, tile, 128), lambda p, t: (p, t, 0))],
        out_shape=[
            jax.ShapeDtypeStruct(cotangent.shape, BF16),
            jax.ShapeDtypeStruct((pipes, tokens, 128), F32),
        ],
        compiler_params=pltpu.CompilerParams(vmem_limit_bytes=VMEM_BYTES),
        cost_estimate=SMALL,
        name="scale",
    )(section_inputs, cotangent)


def patch_kernel(
    table, ct_ref, perm_ref, x_ref, im0, im1, im2, ct_in, inverse_in, head_ref, other_ref, ct_out, inverse_out,
    rows, others, images, new_ct, new_inverse, in_sems, out_sems,
):
    pipe = table[PIPE]
    width = rows.shape[1]
    pair = width // CHIPS
    window = others.shape[1] // CHIPS

    @pl.when(table[FLAG + pipe] == 1)
    def _():
        coming = [pltpu.make_async_copy(x_ref.at[pipe, 0, pl.ds(0, HEAD)], rows, in_sems.at[0])]
        for part, image in enumerate((im0, im1, im2)):
            coming.append(pltpu.make_async_copy(image, images.at[part], in_sems.at[1 + part]))
        for copy in coming:
            copy.start()
        for copy in coming:
            copy.wait()
        live = lax.broadcasted_iota(jnp.int32, (HEAD, 1), 0) < table[LIVE]
        for part in range(3):
            where = pl.ds(pl.multiple_of(table[PART + part], 128), images.shape[2])
            arrived = jnp.dot(perm_ref[...], images[part], preferred_element_type=F32).astype(BF16)
            rows[:, where] = jnp.where(live, arrived, rows[:, where])
        going = []
        total = jnp.zeros((HEAD, pair), F32)
        for chip in range(CHIPS):
            start = chip * pair + (1 - table[CORE]) * (pair - window)
            others[:, chip * window : (chip + 1) * window] = rows[
                :, pl.ds(pl.multiple_of(start, 128), window)
            ]
            part = rows[:, chip * pair : (chip + 1) * pair].astype(F32)
            total = total + part * part
            if chip % 4 == 3:
                for n, (source, target, size) in enumerate(((rows, head_ref, pair), (others, other_ref, window))):
                    done = pl.ds((chip - 3) * size, 4 * size)
                    going.append(
                        pltpu.make_async_copy(source.at[:, done], target.at[:, done], out_sems.at[n, chip // 4])
                    )
                    going[-1].start()
        inverse = lax.rsqrt(jnp.sum(total, axis=1, keepdims=True) / width + EPSILON)
        new_ct[...] = (ct_ref[0, 0].astype(F32) * inverse).astype(BF16)
        new_inverse[...] = jnp.broadcast_to(inverse, new_inverse.shape)
        top = pl.ds(0, HEAD)
        for n, (source, target) in enumerate(
            ((new_ct, ct_out.at[pipe, 0, top]), (new_inverse, inverse_out.at[pipe, top]))
        ):
            going.append(pltpu.make_async_copy(source, target, out_sems.at[2, n]))
            going[-1].start()
        for copy in going:
            copy.wait()


def patch(table, section_inputs, cotangent, perm, images, scaled_ct, inverse):
    width = section_inputs.shape[3]
    kv = cotangent.shape[3]
    window = core_window(width)
    anywhere = pl.BlockSpec(memory_space=pl.ANY)
    return pl.pallas_call(
        patch_kernel,
        grid_spec=pltpu.PrefetchScalarGridSpec(
            num_scalar_prefetch=1,
            grid=(1,),
            in_specs=[
                pl.BlockSpec((1, 1, HEAD, kv), lambda i, table: (table[PIPE], 0, 0, 0)),
                pl.BlockSpec(memory_space=pltpu.VMEM),
            ]
            + [anywhere] * 6,
            out_specs=[anywhere] * 4,
            scratch_shapes=[
                pltpu.VMEM((HEAD, width), BF16),
                pltpu.VMEM((HEAD, CHIPS * window), BF16),
                pltpu.VMEM((3, *images[0].shape), BF16),
                pltpu.VMEM((HEAD, kv), BF16),
                pltpu.VMEM((HEAD, inverse.shape[2]), F32),
                pltpu.SemaphoreType.DMA((4,)),
                pltpu.SemaphoreType.DMA((3, 2)),
            ],
        ),
        out_shape=[
            jax.ShapeDtypeStruct((HEAD, width), BF16),
            jax.ShapeDtypeStruct((HEAD, CHIPS * window), BF16),
            jax.ShapeDtypeStruct(scaled_ct.shape, BF16),
            jax.ShapeDtypeStruct(inverse.shape, F32),
        ],
        input_output_aliases={7: 2, 8: 3},
        compiler_params=pltpu.CompilerParams(vmem_limit_bytes=VMEM_BYTES),
        cost_estimate=SMALL,
        name="patch",
    )(table, cotangent, perm, section_inputs, *images, scaled_ct, inverse)


def pack(parts):
    count = len(parts)
    shape = parts[0][0].shape[-2:]

    def kernel(*refs):
        out, sems = refs[count:]
        copies = []
        for place, (ref, (_, at)) in enumerate(zip(refs, parts)):
            source = ref if at is None else ref.at[at]
            copies.append(pltpu.make_async_copy(source, out.at[place], sems.at[place]))
        for copy in copies:
            copy.start()
        for copy in copies:
            copy.wait()

    anywhere = pl.BlockSpec(memory_space=pl.ANY)
    return pl.pallas_call(
        kernel,
        in_specs=[anywhere] * count,
        out_specs=pl.BlockSpec(memory_space=pltpu.VMEM),
        out_shape=jax.ShapeDtypeStruct((count, *shape), BF16),
        scratch_shapes=[pltpu.SemaphoreType.DMA((count,))],
        compiler_params=pltpu.CompilerParams(vmem_limit_bytes=VMEM_BYTES),
        cost_estimate=SMALL,
        name="pack",
    )(*[array for array, _ in parts])


def start_columns(table, pipe, x_ref, head_ref, rows, sems, from_x, to_rows, from_head=None):
    from_head = from_x if from_head is None else from_head
    flag = table[FLAG + pipe] == 1
    tail = pl.ds(HEAD, rows.shape[0] - HEAD)
    top = rows.at[pl.ds(0, HEAD), to_rows]
    plain = pltpu.make_async_copy(x_ref.at[pipe, 0, pl.ds(0, HEAD), from_x], top, sems.at[0])
    placed = pltpu.make_async_copy(head_ref.at[:, from_head], top, sems.at[0])
    rest = pltpu.make_async_copy(x_ref.at[pipe, 0, tail, from_x], rows.at[tail, to_rows], sems.at[1])
    pl.when(flag)(placed.start)
    pl.when(jnp.logical_not(flag))(plain.start)
    rest.start()
    return [plain, rest]


def products(table, x, sibling_x, head, sibling_head, ct, sibling_ct, groups):
    pipes, _, tokens, width = x.shape
    pair = width // CHIPS
    half = pair // 2
    window = core_window(width)
    kv = ct.shape[3]
    order, sizes = [], []
    for g, group in enumerate(groups):
        sizes.append(0)
        for pipe, r, low, high in group:
            order.append((g, sizes[g], pipe, r, low, high))
            sizes[g] += high - low
    count = len(order)

    def kernel(table, x_ref, sibling_x_ref, head_ref, sibling_head_ref, own_ct, other_ct, *refs):
        outs = refs[: len(groups)]
        own, other, block, row_sems, out_sems = refs[len(groups) :]
        core = table[CORE]
        waits = []
        for n, (_, _, pipe, r, _, _) in enumerate(order):
            from_x = pl.ds(pl.multiple_of(table[r] * pair + core * (pair - window), 128), window)
            here = pl.ds(n * window, window)
            waits.append(
                start_columns(table, pipe, x_ref, head_ref, own, row_sems.at[n, 0], from_x, here)
                + start_columns(
                    table, pipe, sibling_x_ref, sibling_head_ref, other, row_sems.at[n, 1], from_x, here,
                    columns(table[r], window),
                )
            )
        contract = (((0,), (0,)), ((), ()))
        written = []
        for n, (out, at, pipe, r, low, high) in enumerate(order):
            for copy in waits[n]:
                copy.wait()
            here = slice(n * window, (n + 1) * window)
            product = lax.dot_general(own[:, here], own_ct[pipe, 0], contract, preferred_element_type=F32)
            product += lax.dot_general(
                other[:, here], other_ct[pipe, 0], contract, preferred_element_type=F32
            )
            product = product.astype(BF16)

            @pl.when(core == 0)
            def _():
                block[n] = product[:half]

            @pl.when(core == 1)
            def _():
                block[n] = product[window - half :]

            copy = pltpu.make_async_copy(
                block.at[n, pl.ds(low, high - low)], outs[out].at[pl.ds(at, high - low)], out_sems.at[n]
            )
            copy.start()
            written.append(copy)
        for copy in written:
            copy.wait()

    anywhere = pl.BlockSpec(memory_space=pl.ANY)
    whole = pl.BlockSpec(memory_space=pltpu.VMEM)
    return pl.pallas_call(
        kernel,
        in_specs=[pl.BlockSpec(memory_space=pltpu.SMEM)] + [anywhere] * 4 + [whole] * 2,
        out_specs=[anywhere for _ in groups],
        out_shape=[jax.ShapeDtypeStruct((size, kv), BF16) for size in sizes],
        scratch_shapes=[
            pltpu.VMEM((tokens, count * window), BF16),
            pltpu.VMEM((tokens, count * window), BF16),
            pltpu.VMEM((count, half, kv), BF16),
            pltpu.SemaphoreType.DMA((count, 2, 2)),
            pltpu.SemaphoreType.DMA((count,)),
        ],
        compiler_params=pltpu.CompilerParams(vmem_limit_bytes=VMEM_BYTES),
        cost_estimate=SMALL,
        name="products",
    )(table, x, sibling_x, head, sibling_head, ct, sibling_ct)


def on_blocks(name, kernel, operands, outs):
    specs, arrays = [], []
    for operand in operands:
        array, at = operand if isinstance(operand, tuple) else (operand, None)
        shape = array.shape
        if len(shape) == 1:
            specs.append(pl.BlockSpec(memory_space=pltpu.SMEM))
        elif at is None:
            specs.append(pl.BlockSpec(shape, lambda i, n=len(shape): (0,) * n))
        else:
            specs.append(pl.BlockSpec((pl.squeezed, *shape[1:]), lambda i, at=at: (at, 0, 0)))
        arrays.append(array)
    return pl.pallas_call(
        kernel,
        grid=(1,),
        in_specs=specs,
        out_specs=[pl.BlockSpec(out.shape, lambda i, n=len(out.shape): (0,) * n) for out in outs],
        out_shape=outs,
        compiler_params=pltpu.CompilerParams(vmem_limit_bytes=VMEM_BYTES),
        cost_estimate=SMALL,
        name=name,
    )(*arrays)


def wide(*refs):
    total = refs[0][...].astype(F32)
    for ref in refs[1:]:
        total = total + ref[...].astype(F32)
    return total


def halves(first, second, first_out, second_out):
    first_out[...] = first[...]
    second_out[...] = second[...]


def first_sums(near0, from_below, back1, from_above, keep2, came20, up, down):
    rows = near0.shape[0]
    far0, far1, came2 = from_below.at[:rows], from_above.at[:rows], came20.at[:rows]
    half = rows // 2
    far = wide(keep2, came2).astype(BF16)
    up[:rows] = wide(near0, far0).astype(BF16)
    up[rows:] = far[:half]
    down[:rows] = wide(back1, far1).astype(BF16)
    down[rows:] = far[half:]


def gain_row(weight, share):
    products = weight[...].astype(F32) * share
    total = products[:, :128]
    for low in range(128, products.shape[1], 128):
        total = total + products[:, low : low + 128]
    return jnp.sum(jnp.transpose(total), axis=0, keepdims=True)


def gain_column(table, gain, chip):
    pair = gain.shape[1] // CHIPS
    both = gain[:, columns(chip, pair)].astype(F32)
    row = jnp.where(table[CORE] == 0, both[:, : pair // 2], both[:, pair // 2 :])
    return jnp.transpose(jnp.broadcast_to(row, (8, pair // 2)))[:, :1]


def mirror_sums(table, own, below0, from_above, from_below, above1, weight0, weight1, gain, here, there):
    rows = own.shape[0] // 2
    own0, own1 = own.at[:rows], own.at[rows:]
    above0, below1 = from_above.at[rows:], from_below.at[rows:]
    for out, sums, weight, chip in (
        (here, (own0, below0.at[:rows], above0), weight0, table[0]),
        (there, (own1, below1, above1.at[:rows]), weight1, table[Y_CHIPS]),
    ):
        share = wide(*sums)
        out[:rows] = (share * gain_column(table, gain, chip)).astype(BF16)
        out[rows:] = jnp.zeros((out.shape[0] - rows, out.shape[1]), BF16)
        out[rows : rows + 8, :rows] = jnp.broadcast_to(gain_row(weight, share), (8, rows)).astype(BF16)


def second_sums(keep13, came130, below, above, ups, downs):
    rows = ups.shape[0]
    keep1, keep3 = keep13.at[:rows], keep13.at[rows:]
    came1, came3 = came130.at[:rows], came130.at[rows : 2 * rows]
    half = rows // 2
    ups[...] = wide(keep1, came1).astype(BF16)
    downs[...] = wide(keep3, came3).astype(BF16)
    ups[:half] = wide(ups.at[:half], below.at[rows:]).astype(BF16)
    downs[half:] = wide(downs.at[half:], above.at[rows:]).astype(BF16)


def down_sums(table, keep0, came20, came130, below, above, weight, gain, weight_part, gain_part):
    rows = keep0.shape[0]
    came0 = jnp.concatenate([came20[rows:], came130[2 * rows :]]).astype(F32)
    share = wide(keep0, below, above) + came0
    weight_part[...] = share * gain_column(table, gain, table[0])
    gain_part[...] = gain_row(weight, share)


def last_sums(weight_part, gain_part, mirrored0, mirrored1, weight_grad, gain_grad):
    rows = weight_part.shape[0]
    moved = wide(mirrored0, mirrored1)
    weight_grad[0] = weight_part[...] + moved[:rows]
    gain_grad[...] = gain_part[...] + moved[rows : rows + 1, :rows]


def layer(pipe, table, x, head, cotangent, scaled_ct, inverse, gain, own, sibling, carried):
    _, _, tokens, width = x.shape
    pair = width // CHIPS
    half = pair // 2
    kv = cotangent.shape[3]
    arrays = []
    for array, _ in [*own, *sibling]:
        if not any(array is known for known in arrays):
            arrays.append(array)
    position = [
        next(i for i, known in enumerate(arrays) if known is array) for array, _ in [*own, *sibling]
    ]
    index = [at for _, at in [*own, *sibling]]

    def kernel(table, x_ref, head_ref, ct_ref, scaled_ref, inverse_ref, gain_ref, *refs):
        pieces = refs[: len(arrays)]
        values_ref, grad_ref, rows, weight, grad, w_sems, x_sems, out_sems = refs[-8:]
        core = table[CORE]
        size = width // X_CHIPS
        row_waits = []
        for flip in range(X_CHIPS):
            half_x = table[X_HALF] if flip == 0 else 1 - table[X_HALF]
            where = columns(half_x, size)
            row_waits.append(start_columns(table, pipe, x_ref, head_ref, rows, x_sems.at[flip], where, where))
        waits = []
        for r in range(CHIPS):
            copies = []
            for side in range(2):
                piece = side * CHIPS + r
                source = pieces[position[piece]]
                if index[piece] is not None:
                    source = source.at[index[piece]]
                at = table[r] * pair + (core if side == 0 else 1 - core) * half
                copy = pltpu.make_async_copy(
                    source, weight.at[pl.ds(pl.multiple_of(at, 64), half)], w_sems.at[piece]
                )
                copy.start()
                copies.append(copy)
            waits.append(copies)
        values = jnp.zeros((tokens, kv), F32)
        for r in range(CHIPS):
            for copy in waits[r]:
                copy.wait()
            while row_waits[r // Y_CHIPS]:
                row_waits[r // Y_CHIPS].pop().wait()
            where = columns(table[r], pair)
            block = weight[pl.ds(pl.multiple_of(table[r] * pair, 128), pair)]
            values += jnp.dot(rows[:, where] * gain_ref[:, where], block, preferred_element_type=F32)
        inv = inverse_ref[0, :, :1]
        values = values * inv
        values_ref[0, 0] = values.astype(BF16)
        centre = jnp.sum(values * ct_ref[0, 0].astype(F32), axis=1, keepdims=True) / width
        pull = inv * inv * centre
        outs = []
        for chip in range(CHIPS):
            where = slice(chip * pair, (chip + 1) * pair)
            back = lax.dot_general(
                scaled_ref[0, 0], weight[where], (((1,), (1,)), ((), ())), preferred_element_type=F32
            )
            grad[:, where] = (
                back * gain_ref[:, where].astype(F32) - rows[:, where].astype(F32) * pull
            ).astype(BF16)
            if chip % 2 == 1:
                done = pl.ds((chip - 1) * pair, 2 * pair)
                copy = pltpu.make_async_copy(
                    grad.at[:, done], grad_ref.at[pipe, 0, :, done], out_sems.at[chip // 2]
                )
                copy.start()
                outs.append(copy)
        for copy in outs:
            copy.wait()

    anywhere = pl.BlockSpec(memory_space=pl.ANY)
    ct_spec = pl.BlockSpec((1, 1, tokens, kv), lambda i: (pipe, 0, 0, 0))
    operands = [table, x, head, cotangent, scaled_ct, inverse, gain, *arrays, *carried]
    return pl.pallas_call(
        kernel,
        grid=(1,),
        in_specs=[
            pl.BlockSpec(memory_space=pltpu.SMEM),
            anywhere,
            anywhere,
            ct_spec,
            ct_spec,
            pl.BlockSpec((1, tokens, 128), lambda i: (pipe, 0, 0)),
            pl.BlockSpec((1, width), lambda i: (0, 0)),
        ]
        + [anywhere] * (len(arrays) + len(carried)),
        out_specs=[ct_spec, anywhere],
        out_shape=[
            jax.ShapeDtypeStruct(cotangent.shape, BF16),
            jax.ShapeDtypeStruct(x.shape, BF16),
        ],
        scratch_shapes=[
            pltpu.VMEM((tokens, width), BF16),
            pltpu.VMEM((width, kv), BF16),
            pltpu.VMEM((tokens, width), BF16),
            pltpu.SemaphoreType.DMA((2 * CHIPS,)),
            pltpu.SemaphoreType.DMA((X_CHIPS, 2)),
            pltpu.SemaphoreType.DMA((CHIPS // 2,)),
        ],
        input_output_aliases={7 + len(arrays) + i: i for i in range(len(carried))},
        compiler_params=pltpu.CompilerParams(vmem_limit_bytes=VMEM_BYTES),
        cost_estimate=SMALL,
        name="layer",
    )(*operands)


def route_images(image_rows, image_route, section_place, fsdp_place):
    fsdp_count = lax.axis_size("fsdp")
    section_count = lax.axis_size("section")
    ring = section_count // 2
    width = image_rows.shape[2]
    size = -(-width // (3 * 128)) * 128
    pipe = section_place // ring
    z = section_place % ring
    enc_rows = image_rows.shape[1]
    enc_count = enc_rows // BLOCK_ROWS
    head = fsdp_count * CAP * BLOCK_ROWS
    routes = lax.dynamic_index_in_dim(image_route, pipe, 0, keepdims=False)
    own_route = lax.dynamic_index_in_dim(routes, fsdp_place, 0, keepdims=False)
    ids = jnp.arange(enc_count, dtype=jnp.int32)
    earlier = (own_route[:, None] == own_route[None, :]) & (ids[None, :] < ids[:, None])
    slot_of = own_route * CAP + jnp.sum(earlier.astype(jnp.int32), axis=1)
    goes_to = jnp.repeat(slot_of * BLOCK_ROWS, BLOCK_ROWS) + jnp.tile(
        jnp.arange(BLOCK_ROWS, dtype=jnp.int32), enc_count
    )
    row_ids = jnp.arange(head, dtype=jnp.int32)
    select = (row_ids[:, None] == goes_to[None, :]).astype(BF16)
    from_end = jnp.where(pipe == 0, z, ring - 1 - z)
    own_part = jnp.where(from_end == ring - 1, 2, jnp.minimum(from_end, 1))
    starts = jnp.array([0, size, width - size], jnp.int32)
    start = jnp.where(own_part == 0, 0, jnp.where(own_part == 1, size, width - size))
    part = lax.dynamic_slice(image_rows, (pipe, 0, start), (1, enc_rows, size))[0]
    outgoing = jnp.dot(select, part, preferred_element_type=F32).astype(BF16)
    incoming = lax.all_to_all(outgoing, "fsdp", split_axis=0, concat_axis=0, tiled=True)
    end = section_count - 1
    arrivals = jnp.sum((routes == fsdp_place).astype(jnp.int32), axis=1)
    offsets = jnp.cumsum(arrivals) - arrivals
    slot_rows = CAP * BLOCK_ROWS
    within = row_ids % slot_rows
    lands = jnp.repeat(offsets, slot_rows) * BLOCK_ROWS + within
    valid = within < jnp.repeat(arrivals, slot_rows) * BLOCK_ROWS
    lands = jnp.where(valid, lands, -1)
    perm = (jnp.arange(head, dtype=jnp.int32)[:, None] == lands[None, :]).astype(BF16)
    numbers = jnp.concatenate(
        [
            (jnp.sum(arrivals) * BLOCK_ROWS)[None],
            (section_place == 0).astype(jnp.int32)[None],
            (section_place == end).astype(jnp.int32)[None],
            starts,
            pipe[None],
        ]
    )
    return incoming, perm, numbers


def move_images(incoming):
    count = lax.axis_size("section")
    ring, end = count // 2, count - 1
    return [
        incoming,
        lax.ppermute(incoming, "section", [(1, 0), (end - 1, end)]),
        lax.ppermute(incoming, "section", [(ring - 1, 0), (end - ring + 1, end)]),
    ]


def hold(value, *before):
    return lax.optimization_barrier((value, before))[0]


def per_device(
    section_inputs,
    value_cotangent,
    down_weight,
    up_weight,
    down_gain,
    up_gain,
    image_rows,
    image_route,
):
    section_place = lax.axis_index("section")
    fsdp_place = lax.axis_index("fsdp")
    core = fsdp_place % 2
    y = fsdp_place // 2 % Y_CHIPS
    x = fsdp_place // (2 * Y_CHIPS)
    r = jnp.arange(CHIPS, dtype=jnp.int32)
    chips = (x ^ (r // Y_CHIPS)) * Y_CHIPS + (y + r % Y_CHIPS) % Y_CHIPS

    incoming, perm, numbers = route_images(image_rows, image_route, section_place, fsdp_place)
    table = jnp.concatenate([chips, core[None], numbers, x[None]]).astype(jnp.int32)

    shard, kv = down_weight.shape[1:]

    part = jax.ShapeDtypeStruct((shard, kv), BF16)

    sibling_x = to_sibling(section_inputs)
    w0 = pack([(down_weight, 0), (up_weight, 0)])
    w3, w1, w4 = to_next(w0), to_previous(w0), to_across(w0)
    scaled_ct, inverse = scale(section_inputs, value_cotangent)
    w3, w1, w4, incoming = hold((w3, w1, w4, incoming), scaled_ct, sibling_x)
    images = move_images(incoming)
    w2, w5, w7 = to_next(w3), to_previous(w4), to_across(w3)
    early = pack([(w0, 0), (w0, 1), (w1, 0), (w1, 1), (w3, 0), (w3, 1), (w4, 0), (w4, 1)])
    head, other_head, scaled_ct, inverse = patch(
        hold(table, early), section_inputs, value_cotangent, perm, images, scaled_ct, inverse
    )
    w2, w5, w7, other_head, scaled_ct, early = hold((w2, w5, w7, other_head, scaled_ct, early))
    sibling_head, sibling_ct = to_sibling(other_head), to_sibling(scaled_ct)
    down7, up5 = on_blocks("halves", halves, [(w7, 0), (w5, 1)], [part, part])
    down6, up6 = to_next(down7), to_previous(up5)

    rows = (section_inputs, sibling_x, head, sibling_head, scaled_ct, sibling_ct)
    half = shard // 2

    def blocks(*parts):
        return tuple((pipe, r, 0, shard) for pipe, r in parts)

    far0_near1, far1_back0, send20 = products(
        table,
        *rows,
        (blocks((1, 2), (1, 5)), blocks((1, 6), (1, 3)), (*blocks((0, 6)), (0, 4, 0, half))),
    )
    far0_near1, far1_back0, send20, down6, up6, w7, early = hold(
        (far0_near1, far1_back0, send20, down6, up6, w7, early)
    )
    from_below, from_above, came20 = to_next(far0_near1), to_previous(far1_back0), to_across(send20)
    sibling_early = to_sibling(early)
    down_places = ((0, 0), (0, 2), (1, 0), (0, 4), (0, 6), (1, 2), (2, None), (1, 4))
    up_places = ((0, 1), (0, 3), (1, 1), (0, 5), (0, 7), (1, 3), (3, None), (1, 5))
    near0, back1, keep2, send130, own01, keep13, keep0 = products(
        hold(table, up6),
        *rows,
        (
            blocks((1, 1)), blocks((1, 7)), blocks((0, 2)), (*blocks((0, 5), (0, 7)), (0, 4, half, shard)),
            blocks((1, 0), (1, 4)), blocks((0, 1), (0, 3)), blocks((0, 0)),
        ),
    )

    def pieces(arrays, places):
        return [(arrays[array], at) for array, at in places]

    middle = pack([(w2, 0), (w2, 1), (w5, 0), (w5, 1), (w7, 0), (w7, 1)])
    from_below, from_above, came20, send130 = hold(
        (from_below, from_above, came20, send130), keep0, middle, sibling_early
    )
    message = jax.ShapeDtypeStruct((shard + shard // 2, kv), BF16)
    up, down = on_blocks(
        "first_sums",
        first_sums,
        [near0, from_below, back1, from_above, keep2, came20],
        [message, message],
    )
    below, above = to_next(up), to_previous(down)
    came130 = to_across(hold(send130, up))
    own = (early, middle, down6, up6)
    sibling = [sibling_early, *[to_sibling(hold(array, up)) for array in (middle, down6, up6)]]
    filled = layer(
        0,
        hold(table, up),
        section_inputs, head, value_cotangent, scaled_ct, inverse, down_gain,
        pieces(own, down_places), pieces(sibling, down_places), (),
    )
    below, above = hold((below, above), filled[0])
    payload = jax.ShapeDtypeStruct((shard + 16, kv), BF16)
    here, there = on_blocks(
        "mirror_sums",
        mirror_sums,
        [
            table, own01, below, from_above, from_below, above, (up_weight, 0), (early, 7), up_gain,
        ],
        [payload, payload],
    )
    mirrored0, mirrored1 = to_mirror(here, 0), to_mirror(there, 1)
    ups, downs = on_blocks(
        "second_sums",
        second_sums,
        [keep13, came130, below, above],
        [part, part],
    )
    last_below, last_above = to_next(ups), to_previous(downs)
    values, input_grad = layer(
        1,
        hold(table, ups),
        section_inputs, head, value_cotangent, scaled_ct, inverse, up_gain,
        pieces(own, up_places), pieces(sibling, up_places), tuple(filled),
    )
    last_below, last_above = hold((last_below, last_above), values)
    weight_part, gain_part = on_blocks(
        "down_sums",
        down_sums,
        [table, keep0, came20, came130, last_below, last_above, (down_weight, 0), down_gain],
        [jax.ShapeDtypeStruct((shard, kv), F32), jax.ShapeDtypeStruct((1, shard), F32)],
    )
    mirrored0, mirrored1 = hold((mirrored0, mirrored1), weight_part)
    weight_grad, gain_grad = on_blocks(
        "last_sums",
        last_sums,
        [weight_part, gain_part, mirrored0, mirrored1],
        [jax.ShapeDtypeStruct((1, shard, kv), F32), jax.ShapeDtypeStruct((1, shard), F32)],
    )
    return (values, input_grad, weight_grad, gain_grad)


def solution(mesh):
    return jax.shard_map(
        per_device,
        mesh=mesh,
        in_specs=(
            P(None, "section", "fsdp", None),
            P(None, "section", "fsdp", None),
            P("section", "fsdp", None),
            P("section", "fsdp", None),
            P("section", None),
            P("section", None),
            P(None, "fsdp", None),
            P(),
        ),
        out_specs=(
            P(None, "section", "fsdp", None),
            P(None, "section", "fsdp", None),
            P("section", "fsdp", None),
            P("section", "fsdp"),
        ),
        check_vma=False,
    )
```

```python
import jax
import jax.numpy as jnp
from jax import lax
from jax.experimental import pallas as pl
from jax.experimental.pallas import tpu as pltpu
from jax.sharding import PartitionSpec as P

BLOCK_ROWS = 4
CAP = 2
EPSILON = 1e-05
HEAD = 128
VMEM_BYTES = 63 * 1024 * 1024 + 512 * 1024
SMALL = pl.CostEstimate(flops=1, bytes_accessed=1, transcendentals=0)
F32 = jnp.float32
BF16 = jnp.bfloat16

X_CHIPS, Y_CHIPS = 2, 4
CHIPS = X_CHIPS * Y_CHIPS
CORE, LIVE, FLAG, PART, PIPE, X_HALF = 8, 9, 10, 12, 15, 16


def fsdp_route(step):
    route = []
    for x in range(X_CHIPS):
        for y in range(Y_CHIPS):
            for core in range(2):
                to_x, to_y, to_core = step(x, y, core)
                target = (to_x % X_CHIPS * Y_CHIPS + to_y % Y_CHIPS) * 2 + to_core % 2
                route.append(((x * Y_CHIPS + y) * 2 + core, target))
    return route


def to_next(block):
    return lax.ppermute(block, "fsdp", fsdp_route(lambda x, y, core: (x, y + 1, core)))


def to_previous(block):
    return lax.ppermute(block, "fsdp", fsdp_route(lambda x, y, core: (x, y - 1, core)))


def to_across(block):
    return lax.ppermute(block, "fsdp", fsdp_route(lambda x, y, core: (x + 1, y, core)))


def to_sibling(block):
    return lax.ppermute(block, "fsdp", fsdp_route(lambda x, y, core: (x, y, core + 1)))


def to_mirror(block, flip):
    sections, fsdps = lax.axis_size("section"), lax.axis_size("fsdp")
    route = []
    for section in range(sections):
        for fsdp in range(fsdps):
            to_fsdp = (fsdp + flip * fsdps // X_CHIPS) % fsdps
            route.append((section * fsdps + fsdp, (sections - 1 - section) * fsdps + to_fsdp))
    return lax.ppermute(block, ("section", "fsdp"), route)


def columns(chip, size):
    return pl.ds(pl.multiple_of(chip * size, 128), size)


def core_window(width):
    return -(-(width // CHIPS // 2) // 128) * 128


def inverse_rms(rows):
    tokens, width = rows.shape
    pair = width // CHIPS
    total = jnp.zeros((tokens, pair), F32)
    for chip in range(CHIPS):
        part = rows[:, chip * pair : (chip + 1) * pair].astype(F32)
        total = total + part * part
    return lax.rsqrt(jnp.sum(total, axis=1, keepdims=True) / width + EPSILON)


def scale_kernel(x_ref, ct_ref, ct_out, inverse_out):
    inverse = inverse_rms(x_ref.at[0, 0])
    ct_out[0, 0] = (ct_ref[0, 0].astype(F32) * inverse).astype(BF16)
    inverse_out[0] = jnp.broadcast_to(inverse, inverse_out.shape[1:])


def scale(section_inputs, cotangent):
    pipes, _, tokens, width = section_inputs.shape
    kv = cotangent.shape[3]
    tile = 64
    ct_spec = pl.BlockSpec((1, 1, tile, kv), lambda p, t: (p, 0, t, 0))
    return pl.pallas_call(
        scale_kernel,
        grid=(pipes, tokens // tile),
        in_specs=[pl.BlockSpec((1, 1, tile, width), lambda p, t: (p, 0, t, 0)), ct_spec],
        out_specs=[ct_spec, pl.BlockSpec((1, tile, 128), lambda p, t: (p, t, 0))],
        out_shape=[
            jax.ShapeDtypeStruct(cotangent.shape, BF16),
            jax.ShapeDtypeStruct((pipes, tokens, 128), F32),
        ],
        compiler_params=pltpu.CompilerParams(vmem_limit_bytes=VMEM_BYTES),
        cost_estimate=SMALL,
        name="scale",
    )(section_inputs, cotangent)


def patch_kernel(
    table, ct_ref, perm_ref, x_ref, im0, im1, im2, ct_in, inverse_in, head_ref, other_ref, ct_out, inverse_out,
    rows, others, images, new_ct, new_inverse, in_sems, out_sems,
):
    pipe = table[PIPE]
    width = rows.shape[1]
    pair = width // CHIPS
    window = others.shape[1] // CHIPS

    @pl.when(table[FLAG + pipe] == 1)
    def _():
        coming = [pltpu.make_async_copy(x_ref.at[pipe, 0, pl.ds(0, HEAD)], rows, in_sems.at[0])]
        for part, image in enumerate((im0, im1, im2)):
            coming.append(pltpu.make_async_copy(image, images.at[part], in_sems.at[1 + part]))
        for copy in coming:
            copy.start()
        for copy in coming:
            copy.wait()
        live = lax.broadcasted_iota(jnp.int32, (HEAD, 1), 0) < table[LIVE]
        for part in range(3):
            where = pl.ds(pl.multiple_of(table[PART + part], 128), images.shape[2])
            arrived = jnp.dot(perm_ref[...], images[part], preferred_element_type=F32).astype(BF16)
            rows[:, where] = jnp.where(live, arrived, rows[:, where])
        going = []
        total = jnp.zeros((HEAD, pair), F32)
        for chip in range(CHIPS):
            start = chip * pair + (1 - table[CORE]) * (pair - window)
            others[:, chip * window : (chip + 1) * window] = rows[
                :, pl.ds(pl.multiple_of(start, 128), window)
            ]
            part = rows[:, chip * pair : (chip + 1) * pair].astype(F32)
            total = total + part * part
            if chip % 4 == 3:
                for n, (source, target, size) in enumerate(((rows, head_ref, pair), (others, other_ref, window))):
                    done = pl.ds((chip - 3) * size, 4 * size)
                    going.append(
                        pltpu.make_async_copy(source.at[:, done], target.at[:, done], out_sems.at[n, chip // 4])
                    )
                    going[-1].start()
        inverse = lax.rsqrt(jnp.sum(total, axis=1, keepdims=True) / width + EPSILON)
        new_ct[...] = (ct_ref[0, 0].astype(F32) * inverse).astype(BF16)
        new_inverse[...] = jnp.broadcast_to(inverse, new_inverse.shape)
        top = pl.ds(0, HEAD)
        for n, (source, target) in enumerate(
            ((new_ct, ct_out.at[pipe, 0, top]), (new_inverse, inverse_out.at[pipe, top]))
        ):
            going.append(pltpu.make_async_copy(source, target, out_sems.at[2, n]))
            going[-1].start()
        for copy in going:
            copy.wait()


def patch(table, section_inputs, cotangent, perm, images, scaled_ct, inverse):
    width = section_inputs.shape[3]
    kv = cotangent.shape[3]
    window = core_window(width)
    anywhere = pl.BlockSpec(memory_space=pl.ANY)
    return pl.pallas_call(
        patch_kernel,
        grid_spec=pltpu.PrefetchScalarGridSpec(
            num_scalar_prefetch=1,
            grid=(1,),
            in_specs=[
                pl.BlockSpec((1, 1, HEAD, kv), lambda i, table: (table[PIPE], 0, 0, 0)),
                pl.BlockSpec(memory_space=pltpu.VMEM),
            ]
            + [anywhere] * 6,
            out_specs=[anywhere] * 4,
            scratch_shapes=[
                pltpu.VMEM((HEAD, width), BF16),
                pltpu.VMEM((HEAD, CHIPS * window), BF16),
                pltpu.VMEM((3, *images[0].shape), BF16),
                pltpu.VMEM((HEAD, kv), BF16),
                pltpu.VMEM((HEAD, inverse.shape[2]), F32),
                pltpu.SemaphoreType.DMA((4,)),
                pltpu.SemaphoreType.DMA((3, 2)),
            ],
        ),
        out_shape=[
            jax.ShapeDtypeStruct((HEAD, width), BF16),
            jax.ShapeDtypeStruct((HEAD, CHIPS * window), BF16),
            jax.ShapeDtypeStruct(scaled_ct.shape, BF16),
            jax.ShapeDtypeStruct(inverse.shape, F32),
        ],
        input_output_aliases={7: 2, 8: 3},
        compiler_params=pltpu.CompilerParams(vmem_limit_bytes=VMEM_BYTES),
        cost_estimate=SMALL,
        name="patch",
    )(table, cotangent, perm, section_inputs, *images, scaled_ct, inverse)


def pack(parts):
    count = len(parts)
    shape = parts[0][0].shape[-2:]

    def kernel(*refs):
        out, sems = refs[count:]
        copies = []
        for place, (ref, (_, at)) in enumerate(zip(refs, parts)):
            source = ref if at is None else ref.at[at]
            copies.append(pltpu.make_async_copy(source, out.at[place], sems.at[place]))
        for copy in copies:
            copy.start()
        for copy in copies:
            copy.wait()

    anywhere = pl.BlockSpec(memory_space=pl.ANY)
    return pl.pallas_call(
        kernel,
        in_specs=[anywhere] * count,
        out_specs=pl.BlockSpec(memory_space=pltpu.VMEM),
        out_shape=jax.ShapeDtypeStruct((count, *shape), BF16),
        scratch_shapes=[pltpu.SemaphoreType.DMA((count,))],
        compiler_params=pltpu.CompilerParams(vmem_limit_bytes=VMEM_BYTES),
        cost_estimate=SMALL,
        name="pack",
    )(*[array for array, _ in parts])


def start_columns(table, pipe, x_ref, head_ref, rows, sems, from_x, to_rows, from_head=None):
    from_head = from_x if from_head is None else from_head
    flag = table[FLAG + pipe] == 1
    tail = pl.ds(HEAD, rows.shape[0] - HEAD)
    top = rows.at[pl.ds(0, HEAD), to_rows]
    plain = pltpu.make_async_copy(x_ref.at[pipe, 0, pl.ds(0, HEAD), from_x], top, sems.at[0])
    placed = pltpu.make_async_copy(head_ref.at[:, from_head], top, sems.at[0])
    rest = pltpu.make_async_copy(x_ref.at[pipe, 0, tail, from_x], rows.at[tail, to_rows], sems.at[1])
    pl.when(flag)(placed.start)
    pl.when(jnp.logical_not(flag))(plain.start)
    rest.start()
    return [plain, rest]


def products(table, x, sibling_x, head, sibling_head, ct, sibling_ct, groups):
    pipes, _, tokens, width = x.shape
    pair = width // CHIPS
    half = pair // 2
    window = core_window(width)
    kv = ct.shape[3]
    order, sizes = [], []
    for g, group in enumerate(groups):
        sizes.append(0)
        for pipe, r, low, high in group:
            order.append((g, sizes[g], pipe, r, low, high))
            sizes[g] += high - low
    count = len(order)

    def kernel(table, x_ref, sibling_x_ref, head_ref, sibling_head_ref, own_ct, other_ct, *refs):
        outs = refs[: len(groups)]
        own, other, block, row_sems, out_sems = refs[len(groups) :]
        core = table[CORE]
        waits = []
        for n, (_, _, pipe, r, _, _) in enumerate(order):
            from_x = pl.ds(pl.multiple_of(table[r] * pair + core * (pair - window), 128), window)
            here = pl.ds(n * window, window)
            waits.append(
                start_columns(table, pipe, x_ref, head_ref, own, row_sems.at[n, 0], from_x, here)
                + start_columns(
                    table, pipe, sibling_x_ref, sibling_head_ref, other, row_sems.at[n, 1], from_x, here,
                    columns(table[r], window),
                )
            )
        contract = (((0,), (0,)), ((), ()))
        written = []
        for n, (out, at, pipe, r, low, high) in enumerate(order):
            for copy in waits[n]:
                copy.wait()
            here = slice(n * window, (n + 1) * window)
            product = lax.dot_general(own[:, here], own_ct[pipe, 0], contract, preferred_element_type=F32)
            product += lax.dot_general(
                other[:, here], other_ct[pipe, 0], contract, preferred_element_type=F32
            )
            product = product.astype(BF16)

            @pl.when(core == 0)
            def _():
                block[n] = product[:half]

            @pl.when(core == 1)
            def _():
                block[n] = product[window - half :]

            copy = pltpu.make_async_copy(
                block.at[n, pl.ds(low, high - low)], outs[out].at[pl.ds(at, high - low)], out_sems.at[n]
            )
            copy.start()
            written.append(copy)
        for copy in written:
            copy.wait()

    anywhere = pl.BlockSpec(memory_space=pl.ANY)
    whole = pl.BlockSpec(memory_space=pltpu.VMEM)
    return pl.pallas_call(
        kernel,
        in_specs=[pl.BlockSpec(memory_space=pltpu.SMEM)] + [anywhere] * 4 + [whole] * 2,
        out_specs=[anywhere for _ in groups],
        out_shape=[jax.ShapeDtypeStruct((size, kv), BF16) for size in sizes],
        scratch_shapes=[
            pltpu.VMEM((tokens, count * window), BF16),
            pltpu.VMEM((tokens, count * window), BF16),
            pltpu.VMEM((count, half, kv), BF16),
            pltpu.SemaphoreType.DMA((count, 2, 2)),
            pltpu.SemaphoreType.DMA((count,)),
        ],
        compiler_params=pltpu.CompilerParams(vmem_limit_bytes=VMEM_BYTES),
        cost_estimate=SMALL,
        name="products",
    )(table, x, sibling_x, head, sibling_head, ct, sibling_ct)


def on_blocks(name, kernel, operands, outs):
    specs, arrays = [], []
    for operand in operands:
        array, *which = operand if isinstance(operand, tuple) else (operand,)
        shape = array.shape
        if len(shape) == 1:
            specs.append(pl.BlockSpec(memory_space=pltpu.SMEM))
        elif not which:
            specs.append(pl.BlockSpec(shape, lambda i, n=len(shape): (0,) * n))
        elif len(which) == 1:
            specs.append(pl.BlockSpec((pl.squeezed, *shape[1:]), lambda i, at=which[0]: (at, 0, 0)))
        else:
            specs.append(pl.BlockSpec((which[0], shape[1]), lambda i, at=which[1]: (at, 0)))
        arrays.append(array)
    return pl.pallas_call(
        kernel,
        grid=(1,),
        in_specs=specs,
        out_specs=[pl.BlockSpec(out.shape, lambda i, n=len(out.shape): (0,) * n) for out in outs],
        out_shape=outs,
        compiler_params=pltpu.CompilerParams(vmem_limit_bytes=VMEM_BYTES),
        cost_estimate=SMALL,
        name=name,
    )(*arrays)


def wide(*refs):
    total = refs[0][...].astype(F32)
    for ref in refs[1:]:
        total = total + ref[...].astype(F32)
    return total


def halves(first, second, first_out, second_out):
    first_out[...] = first[...]
    second_out[...] = second[...]


def first_sums(near0, far0, back1, far1, keep2, came2, up, down):
    rows = near0.shape[0]
    half = rows // 2
    far = wide(keep2, came2).astype(BF16)
    up[:rows] = wide(near0, far0).astype(BF16)
    up[rows:] = far[:half]
    down[:rows] = wide(back1, far1).astype(BF16)
    down[rows:] = far[half:]


def gain_row(weight, share):
    products = weight[...].astype(F32) * share
    total = products[:, :128]
    for low in range(128, products.shape[1], 128):
        total = total + products[:, low : low + 128]
    return jnp.sum(jnp.transpose(total), axis=0, keepdims=True)


def gain_column(table, gain, chip):
    pair = gain.shape[1] // CHIPS
    both = gain[:, columns(chip, pair)].astype(F32)
    row = jnp.where(table[CORE] == 0, both[:, : pair // 2], both[:, pair // 2 :])
    return jnp.transpose(jnp.broadcast_to(row, (8, pair // 2)))[:, :1]


def mirror_sums(table, own0, below0, above0, own1, below1, above1, weight0, weight1, gain, here, there):
    rows = own0.shape[0]
    for out, sums, weight, chip in (
        (here, (own0, below0, above0), weight0, table[0]),
        (there, (own1, below1, above1), weight1, table[Y_CHIPS]),
    ):
        share = wide(*sums)
        out[:rows] = (share * gain_column(table, gain, chip)).astype(BF16)
        out[rows:] = jnp.zeros((out.shape[0] - rows, out.shape[1]), BF16)
        out[rows : rows + 8, :rows] = jnp.broadcast_to(gain_row(weight, share), (8, rows)).astype(BF16)


def second_sums(keep1, came1, below, keep3, came3, above, ups, downs):
    half = ups.shape[0] // 2
    up, down = wide(keep1, came1), wide(keep3, came3)
    ups[:half] = (up[:half] + below[...].astype(F32)).astype(BF16)
    ups[half:] = up[half:].astype(BF16)
    downs[:half] = down[:half].astype(BF16)
    downs[half:] = (down[half:] + above[...].astype(F32)).astype(BF16)


def down_sums(table, keep0, came_low, came_high, below, above, weight, gain, weight_part, gain_part):
    share = wide(keep0, below, above) + jnp.concatenate([came_low[...], came_high[...]]).astype(F32)
    weight_part[...] = share * gain_column(table, gain, table[0])
    gain_part[...] = gain_row(weight, share)


def last_sums(weight_part, gain_part, mirrored0, mirrored1, weight_grad, gain_grad):
    rows = weight_part.shape[0]
    moved = wide(mirrored0, mirrored1)
    weight_grad[0] = weight_part[...] + moved[:rows]
    gain_grad[...] = gain_part[...] + moved[rows : rows + 1, :rows]


def layer(pipe, table, x, head, cotangent, scaled_ct, inverse, gain, own, sibling, carried):
    _, _, tokens, width = x.shape
    pair = width // CHIPS
    half = pair // 2
    kv = cotangent.shape[3]
    arrays = []
    for array, _ in [*own, *sibling]:
        if not any(array is known for known in arrays):
            arrays.append(array)
    position = [
        next(i for i, known in enumerate(arrays) if known is array) for array, _ in [*own, *sibling]
    ]
    index = [at for _, at in [*own, *sibling]]

    def kernel(table, x_ref, head_ref, ct_ref, scaled_ref, inverse_ref, gain_ref, *refs):
        pieces = refs[: len(arrays)]
        values_ref, grad_ref, rows, weight, grad, w_sems, x_sems, out_sems = refs[-8:]
        core = table[CORE]
        size = width // X_CHIPS
        row_waits = []
        for flip in range(X_CHIPS):
            half_x = table[X_HALF] if flip == 0 else 1 - table[X_HALF]
            where = columns(half_x, size)
            row_waits.append(start_columns(table, pipe, x_ref, head_ref, rows, x_sems.at[flip], where, where))
        waits = []
        for r in range(CHIPS):
            copies = []
            for side in range(2):
                piece = side * CHIPS + r
                source = pieces[position[piece]]
                if index[piece] is not None:
                    source = source.at[index[piece]]
                at = table[r] * pair + (core if side == 0 else 1 - core) * half
                copy = pltpu.make_async_copy(
                    source, weight.at[pl.ds(pl.multiple_of(at, 64), half)], w_sems.at[piece]
                )
                copy.start()
                copies.append(copy)
            waits.append(copies)
        values = jnp.zeros((tokens, kv), F32)
        for r in range(CHIPS):
            for copy in waits[r]:
                copy.wait()
            while row_waits[r // Y_CHIPS]:
                row_waits[r // Y_CHIPS].pop().wait()
            where = columns(table[r], pair)
            block = weight[pl.ds(pl.multiple_of(table[r] * pair, 128), pair)]
            values += jnp.dot(rows[:, where] * gain_ref[:, where], block, preferred_element_type=F32)
        inv = inverse_ref[0, :, :1]
        values = values * inv
        values_ref[0, 0] = values.astype(BF16)
        centre = jnp.sum(values * ct_ref[0, 0].astype(F32), axis=1, keepdims=True) / width
        pull = inv * inv * centre
        outs = []
        for chip in range(CHIPS):
            where = slice(chip * pair, (chip + 1) * pair)
            back = lax.dot_general(
                scaled_ref[0, 0], weight[where], (((1,), (1,)), ((), ())), preferred_element_type=F32
            )
            grad[:, where] = (
                back * gain_ref[:, where].astype(F32) - rows[:, where].astype(F32) * pull
            ).astype(BF16)
            if chip % 2 == 1:
                done = pl.ds((chip - 1) * pair, 2 * pair)
                copy = pltpu.make_async_copy(
                    grad.at[:, done], grad_ref.at[pipe, 0, :, done], out_sems.at[chip // 2]
                )
                copy.start()
                outs.append(copy)
        for copy in outs:
            copy.wait()

    anywhere = pl.BlockSpec(memory_space=pl.ANY)
    ct_spec = pl.BlockSpec((1, 1, tokens, kv), lambda i: (pipe, 0, 0, 0))
    operands = [table, x, head, cotangent, scaled_ct, inverse, gain, *arrays, *carried]
    return pl.pallas_call(
        kernel,
        grid=(1,),
        in_specs=[
            pl.BlockSpec(memory_space=pltpu.SMEM),
            anywhere,
            anywhere,
            ct_spec,
            ct_spec,
            pl.BlockSpec((1, tokens, 128), lambda i: (pipe, 0, 0)),
            pl.BlockSpec((1, width), lambda i: (0, 0)),
        ]
        + [anywhere] * (len(arrays) + len(carried)),
        out_specs=[ct_spec, anywhere],
        out_shape=[
            jax.ShapeDtypeStruct(cotangent.shape, BF16),
            jax.ShapeDtypeStruct(x.shape, BF16),
        ],
        scratch_shapes=[
            pltpu.VMEM((tokens, width), BF16),
            pltpu.VMEM((width, kv), BF16),
            pltpu.VMEM((tokens, width), BF16),
            pltpu.SemaphoreType.DMA((2 * CHIPS,)),
            pltpu.SemaphoreType.DMA((X_CHIPS, 2)),
            pltpu.SemaphoreType.DMA((CHIPS // 2,)),
        ],
        input_output_aliases={7 + len(arrays) + i: i for i in range(len(carried))},
        compiler_params=pltpu.CompilerParams(vmem_limit_bytes=VMEM_BYTES),
        cost_estimate=SMALL,
        name="layer",
    )(*operands)


def route_images(image_rows, image_route, section_place, fsdp_place):
    fsdp_count = lax.axis_size("fsdp")
    section_count = lax.axis_size("section")
    ring = section_count // 2
    width = image_rows.shape[2]
    size = -(-width // (3 * 128)) * 128
    pipe = section_place // ring
    z = section_place % ring
    enc_rows = image_rows.shape[1]
    enc_count = enc_rows // BLOCK_ROWS
    head = fsdp_count * CAP * BLOCK_ROWS
    routes = lax.dynamic_index_in_dim(image_route, pipe, 0, keepdims=False)
    own_route = lax.dynamic_index_in_dim(routes, fsdp_place, 0, keepdims=False)
    ids = jnp.arange(enc_count, dtype=jnp.int32)
    earlier = (own_route[:, None] == own_route[None, :]) & (ids[None, :] < ids[:, None])
    slot_of = own_route * CAP + jnp.sum(earlier.astype(jnp.int32), axis=1)
    goes_to = jnp.repeat(slot_of * BLOCK_ROWS, BLOCK_ROWS) + jnp.tile(
        jnp.arange(BLOCK_ROWS, dtype=jnp.int32), enc_count
    )
    row_ids = jnp.arange(head, dtype=jnp.int32)
    select = (row_ids[:, None] == goes_to[None, :]).astype(BF16)
    from_end = jnp.where(pipe == 0, z, ring - 1 - z)
    own_part = jnp.where(from_end == ring - 1, 2, jnp.minimum(from_end, 1))
    starts = jnp.array([0, size, width - size], jnp.int32)
    start = jnp.where(own_part == 0, 0, jnp.where(own_part == 1, size, width - size))
    part = lax.dynamic_slice(image_rows, (pipe, 0, start), (1, enc_rows, size))[0]
    outgoing = jnp.dot(select, part, preferred_element_type=F32).astype(BF16)
    incoming = lax.all_to_all(outgoing, "fsdp", split_axis=0, concat_axis=0, tiled=True)
    end = section_count - 1
    arrivals = jnp.sum((routes == fsdp_place).astype(jnp.int32), axis=1)
    offsets = jnp.cumsum(arrivals) - arrivals
    slot_rows = CAP * BLOCK_ROWS
    within = row_ids % slot_rows
    lands = jnp.repeat(offsets, slot_rows) * BLOCK_ROWS + within
    valid = within < jnp.repeat(arrivals, slot_rows) * BLOCK_ROWS
    lands = jnp.where(valid, lands, -1)
    perm = (jnp.arange(head, dtype=jnp.int32)[:, None] == lands[None, :]).astype(BF16)
    numbers = jnp.concatenate(
        [
            (jnp.sum(arrivals) * BLOCK_ROWS)[None],
            (section_place == 0).astype(jnp.int32)[None],
            (section_place == end).astype(jnp.int32)[None],
            starts,
            pipe[None],
        ]
    )
    return incoming, perm, numbers


def move_images(incoming):
    count = lax.axis_size("section")
    ring, end = count // 2, count - 1
    return [
        incoming,
        lax.ppermute(incoming, "section", [(1, 0), (end - 1, end)]),
        lax.ppermute(incoming, "section", [(ring - 1, 0), (end - ring + 1, end)]),
    ]


def hold(value, *before):
    return lax.optimization_barrier((value, before))[0]


def per_device(
    section_inputs,
    value_cotangent,
    down_weight,
    up_weight,
    down_gain,
    up_gain,
    image_rows,
    image_route,
):
    section_place = lax.axis_index("section")
    fsdp_place = lax.axis_index("fsdp")
    core = fsdp_place % 2
    y = fsdp_place // 2 % Y_CHIPS
    x = fsdp_place // (2 * Y_CHIPS)
    r = jnp.arange(CHIPS, dtype=jnp.int32)
    chips = (x ^ (r // Y_CHIPS)) * Y_CHIPS + (y + r % Y_CHIPS) % Y_CHIPS

    incoming, perm, numbers = route_images(image_rows, image_route, section_place, fsdp_place)
    table = jnp.concatenate([chips, core[None], numbers, x[None]]).astype(jnp.int32)

    shard, kv = down_weight.shape[1:]

    part = jax.ShapeDtypeStruct((shard, kv), BF16)

    sibling_x = to_sibling(section_inputs)
    w0 = pack([(down_weight, 0), (up_weight, 0)])
    w3, w1, w4 = to_next(w0), to_previous(w0), to_across(w0)
    scaled_ct, inverse = scale(section_inputs, value_cotangent)
    w3, w1, w4, incoming = hold((w3, w1, w4, incoming), scaled_ct, sibling_x)
    images = move_images(incoming)
    w2, w5, w7 = to_next(w3), to_previous(w4), to_across(w3)
    early = pack([(w0, 0), (w0, 1), (w1, 0), (w1, 1), (w3, 0), (w3, 1), (w4, 0), (w4, 1)])
    head, other_head, scaled_ct, inverse = patch(
        hold(table, early), section_inputs, value_cotangent, perm, images, scaled_ct, inverse
    )
    w2, w5, w7, other_head, scaled_ct, early = hold((w2, w5, w7, other_head, scaled_ct, early))
    sibling_head, sibling_ct = to_sibling(other_head), to_sibling(scaled_ct)
    down7, up5 = on_blocks("halves", halves, [(w7, 0), (w5, 1)], [part, part])
    down6, up6 = to_next(down7), to_previous(up5)

    rows = (section_inputs, sibling_x, head, sibling_head, scaled_ct, sibling_ct)
    half = shard // 2

    def blocks(*parts):
        return tuple((pipe, r, 0, shard) for pipe, r in parts)

    far0_near1, far1_back0, send20 = products(
        table,
        *rows,
        (blocks((1, 2), (1, 5)), blocks((1, 6), (1, 3)), (*blocks((0, 6)), (0, 4, 0, half))),
    )
    far0_near1, far1_back0, send20, down6, up6, w7, early = hold(
        (far0_near1, far1_back0, send20, down6, up6, w7, early)
    )
    from_below, from_above, came20 = to_next(far0_near1), to_previous(far1_back0), to_across(send20)
    sibling_early = to_sibling(early)
    down_places = ((0, 0), (0, 2), (1, 0), (0, 4), (0, 6), (1, 2), (2, None), (1, 4))
    up_places = ((0, 1), (0, 3), (1, 1), (0, 5), (0, 7), (1, 3), (3, None), (1, 5))
    near0, back1, keep2, send130, own01, keep13, keep0 = products(
        hold(table, up6),
        *rows,
        (
            blocks((1, 1)), blocks((1, 7)), blocks((0, 2)), (*blocks((0, 5), (0, 7)), (0, 4, half, shard)),
            blocks((1, 0), (1, 4)), blocks((0, 1), (0, 3)), blocks((0, 0)),
        ),
    )

    def pieces(arrays, places):
        return [(arrays[array], at) for array, at in places]

    middle = pack([(w2, 0), (w2, 1), (w5, 0), (w5, 1), (w7, 0), (w7, 1)])
    from_below, from_above, came20, send130 = hold(
        (from_below, from_above, came20, send130), keep0, middle, sibling_early
    )
    message = jax.ShapeDtypeStruct((shard + shard // 2, kv), BF16)
    up, down = on_blocks(
        "first_sums",
        first_sums,
        [near0, (from_below, shard, 0), back1, (from_above, shard, 0), keep2, (came20, shard, 0)],
        [message, message],
    )
    below, above = to_next(up), to_previous(down)
    came130 = to_across(hold(send130, up))
    own = (early, middle, down6, up6)
    sibling = [sibling_early, *[to_sibling(hold(array, up)) for array in (middle, down6, up6)]]
    filled = layer(
        0,
        hold(table, up),
        section_inputs, head, value_cotangent, scaled_ct, inverse, down_gain,
        pieces(own, down_places), pieces(sibling, down_places), (),
    )
    below, above = hold((below, above), filled[0])
    payload = jax.ShapeDtypeStruct((shard + 16, kv), BF16)
    here, there = on_blocks(
        "mirror_sums",
        mirror_sums,
        [
            table, (own01, shard, 0), (below, shard, 0), (from_above, shard, 1),
            (own01, shard, 1), (from_below, shard, 1), (above, shard, 0), (up_weight, 0), (early, 7), up_gain,
        ],
        [payload, payload],
    )
    mirrored0, mirrored1 = to_mirror(here, 0), to_mirror(there, 1)
    ups, downs = on_blocks(
        "second_sums",
        second_sums,
        [
            (keep13, shard, 0), (came130, shard, 0), (below, half, 2),
            (keep13, shard, 1), (came130, shard, 1), (above, half, 2),
        ],
        [part, part],
    )
    last_below, last_above = to_next(ups), to_previous(downs)
    values, input_grad = layer(
        1,
        hold(table, ups),
        section_inputs, head, value_cotangent, scaled_ct, inverse, up_gain,
        pieces(own, up_places), pieces(sibling, up_places), tuple(filled),
    )
    last_below, last_above = hold((last_below, last_above), values)
    weight_part, gain_part = on_blocks(
        "down_sums",
        down_sums,
        [
            table, keep0, (came20, half, 2), (came130, half, 4), last_below, last_above, (down_weight, 0), down_gain,
        ],
        [jax.ShapeDtypeStruct((shard, kv), F32), jax.ShapeDtypeStruct((1, shard), F32)],
    )
    mirrored0, mirrored1 = hold((mirrored0, mirrored1), weight_part)
    weight_grad, gain_grad = on_blocks(
        "last_sums",
        last_sums,
        [weight_part, gain_part, mirrored0, mirrored1],
        [jax.ShapeDtypeStruct((1, shard, kv), F32), jax.ShapeDtypeStruct((1, shard), F32)],
    )
    return (values, input_grad, weight_grad, gain_grad)


def solution(mesh):
    return jax.shard_map(
        per_device,
        mesh=mesh,
        in_specs=(
            P(None, "section", "fsdp", None),
            P(None, "section", "fsdp", None),
            P("section", "fsdp", None),
            P("section", "fsdp", None),
            P("section", None),
            P("section", None),
            P(None, "fsdp", None),
            P(),
        ),
        out_specs=(
            P(None, "section", "fsdp", None),
            P(None, "section", "fsdp", None),
            P("section", "fsdp", None),
            P("section", "fsdp"),
        ),
        check_vma=False,
    )
```

```python
import jax
import jax.numpy as jnp
from jax import lax
from jax.experimental import pallas as pl
from jax.experimental.pallas import tpu as pltpu
from jax.sharding import PartitionSpec as P

BLOCK_ROWS = 4
CAP = 2
EPSILON = 1e-05
HEAD = 128
VMEM_BYTES = 63 * 1024 * 1024 + 512 * 1024
SMALL = pl.CostEstimate(flops=1, bytes_accessed=1, transcendentals=0)
F32 = jnp.float32
BF16 = jnp.bfloat16

X_CHIPS, Y_CHIPS = 2, 4
CHIPS = X_CHIPS * Y_CHIPS
CORE, LIVE, FLAG, PART, PIPE, X_HALF = 8, 9, 10, 12, 15, 16


def fsdp_route(step):
    route = []
    for x in range(X_CHIPS):
        for y in range(Y_CHIPS):
            for core in range(2):
                to_x, to_y, to_core = step(x, y, core)
                target = (to_x % X_CHIPS * Y_CHIPS + to_y % Y_CHIPS) * 2 + to_core % 2
                route.append(((x * Y_CHIPS + y) * 2 + core, target))
    return route


def to_next(block):
    return lax.ppermute(block, "fsdp", fsdp_route(lambda x, y, core: (x, y + 1, core)))


def to_previous(block):
    return lax.ppermute(block, "fsdp", fsdp_route(lambda x, y, core: (x, y - 1, core)))


def to_across(block):
    return lax.ppermute(block, "fsdp", fsdp_route(lambda x, y, core: (x + 1, y, core)))


def to_sibling(block):
    return lax.ppermute(block, "fsdp", fsdp_route(lambda x, y, core: (x, y, core + 1)))


def to_mirror(block, flip):
    sections, fsdps = lax.axis_size("section"), lax.axis_size("fsdp")
    route = []
    for section in range(sections):
        for fsdp in range(fsdps):
            to_fsdp = (fsdp + flip * fsdps // X_CHIPS) % fsdps
            route.append((section * fsdps + fsdp, (sections - 1 - section) * fsdps + to_fsdp))
    return lax.ppermute(block, ("section", "fsdp"), route)


def columns(chip, size):
    return pl.ds(pl.multiple_of(chip * size, 128), size)


def core_window(width):
    return -(-(width // CHIPS // 2) // 128) * 128


def inverse_rms(rows):
    tokens, width = rows.shape
    pair = width // CHIPS
    total = jnp.zeros((tokens, pair), F32)
    for chip in range(CHIPS):
        part = rows[:, chip * pair : (chip + 1) * pair].astype(F32)
        total = total + part * part
    return lax.rsqrt(jnp.sum(total, axis=1, keepdims=True) / width + EPSILON)


def scale_kernel(x_ref, ct_ref, ct_out, inverse_out):
    inverse = inverse_rms(x_ref.at[0, 0])
    ct_out[0, 0] = (ct_ref[0, 0].astype(F32) * inverse).astype(BF16)
    inverse_out[0] = jnp.broadcast_to(inverse, inverse_out.shape[1:])


def scale(section_inputs, cotangent):
    pipes, _, tokens, width = section_inputs.shape
    kv = cotangent.shape[3]
    tile = 64
    ct_spec = pl.BlockSpec((1, 1, tile, kv), lambda p, t: (p, 0, t, 0))
    return pl.pallas_call(
        scale_kernel,
        grid=(pipes, tokens // tile),
        in_specs=[pl.BlockSpec((1, 1, tile, width), lambda p, t: (p, 0, t, 0)), ct_spec],
        out_specs=[ct_spec, pl.BlockSpec((1, tile, 128), lambda p, t: (p, t, 0))],
        out_shape=[
            jax.ShapeDtypeStruct(cotangent.shape, BF16),
            jax.ShapeDtypeStruct((pipes, tokens, 128), F32),
        ],
        compiler_params=pltpu.CompilerParams(vmem_limit_bytes=VMEM_BYTES),
        cost_estimate=SMALL,
        name="scale",
    )(section_inputs, cotangent)


def patch_kernel(
    table, ct_ref, perm_ref, x_ref, im0, im1, im2, ct_in, inverse_in, head_ref, other_ref, ct_out, inverse_out,
    rows, others, images, new_ct, new_inverse, in_sems, out_sems,
):
    pipe = table[PIPE]
    width = rows.shape[1]
    pair = width // CHIPS
    window = others.shape[1] // CHIPS

    @pl.when(table[FLAG + pipe] == 1)
    def _():
        coming = [pltpu.make_async_copy(x_ref.at[pipe, 0, pl.ds(0, HEAD)], rows, in_sems.at[0])]
        for part, image in enumerate((im0, im1, im2)):
            coming.append(pltpu.make_async_copy(image, images.at[part], in_sems.at[1 + part]))
        for copy in coming:
            copy.start()
        for copy in coming:
            copy.wait()
        live = lax.broadcasted_iota(jnp.int32, (HEAD, 1), 0) < table[LIVE]
        for part in range(3):
            where = pl.ds(pl.multiple_of(table[PART + part], 128), images.shape[2])
            arrived = jnp.dot(perm_ref[...], images[part], preferred_element_type=F32).astype(BF16)
            rows[:, where] = jnp.where(live, arrived, rows[:, where])
        going = []
        total = jnp.zeros((HEAD, pair), F32)
        for chip in range(CHIPS):
            start = chip * pair + (1 - table[CORE]) * (pair - window)
            others[:, chip * window : (chip + 1) * window] = rows[
                :, pl.ds(pl.multiple_of(start, 128), window)
            ]
            part = rows[:, chip * pair : (chip + 1) * pair].astype(F32)
            total = total + part * part
            if chip % 4 == 3:
                for n, (source, target, size) in enumerate(((rows, head_ref, pair), (others, other_ref, window))):
                    done = pl.ds((chip - 3) * size, 4 * size)
                    going.append(
                        pltpu.make_async_copy(source.at[:, done], target.at[:, done], out_sems.at[n, chip // 4])
                    )
                    going[-1].start()
        inverse = lax.rsqrt(jnp.sum(total, axis=1, keepdims=True) / width + EPSILON)
        new_ct[...] = (ct_ref[0, 0].astype(F32) * inverse).astype(BF16)
        new_inverse[...] = jnp.broadcast_to(inverse, new_inverse.shape)
        top = pl.ds(0, HEAD)
        for n, (source, target) in enumerate(
            ((new_ct, ct_out.at[pipe, 0, top]), (new_inverse, inverse_out.at[pipe, top]))
        ):
            going.append(pltpu.make_async_copy(source, target, out_sems.at[2, n]))
            going[-1].start()
        for copy in going:
            copy.wait()


def patch(table, section_inputs, cotangent, perm, images, scaled_ct, inverse):
    width = section_inputs.shape[3]
    kv = cotangent.shape[3]
    window = core_window(width)
    anywhere = pl.BlockSpec(memory_space=pl.ANY)
    return pl.pallas_call(
        patch_kernel,
        grid_spec=pltpu.PrefetchScalarGridSpec(
            num_scalar_prefetch=1,
            grid=(1,),
            in_specs=[
                pl.BlockSpec((1, 1, HEAD, kv), lambda i, table: (table[PIPE], 0, 0, 0)),
                pl.BlockSpec(memory_space=pltpu.VMEM),
            ]
            + [anywhere] * 6,
            out_specs=[anywhere] * 4,
            scratch_shapes=[
                pltpu.VMEM((HEAD, width), BF16),
                pltpu.VMEM((HEAD, CHIPS * window), BF16),
                pltpu.VMEM((3, *images[0].shape), BF16),
                pltpu.VMEM((HEAD, kv), BF16),
                pltpu.VMEM((HEAD, inverse.shape[2]), F32),
                pltpu.SemaphoreType.DMA((4,)),
                pltpu.SemaphoreType.DMA((3, 2)),
            ],
        ),
        out_shape=[
            jax.ShapeDtypeStruct((HEAD, width), BF16),
            jax.ShapeDtypeStruct((HEAD, CHIPS * window), BF16),
            jax.ShapeDtypeStruct(scaled_ct.shape, BF16),
            jax.ShapeDtypeStruct(inverse.shape, F32),
        ],
        input_output_aliases={7: 2, 8: 3},
        compiler_params=pltpu.CompilerParams(vmem_limit_bytes=VMEM_BYTES),
        cost_estimate=SMALL,
        name="patch",
    )(table, cotangent, perm, section_inputs, *images, scaled_ct, inverse)


def pack(parts):
    count = len(parts)
    shape = parts[0][0].shape[-2:]

    def kernel(*refs):
        out, sems = refs[count:]
        copies = []
        for place, (ref, (_, at)) in enumerate(zip(refs, parts)):
            source = ref if at is None else ref.at[at]
            copies.append(pltpu.make_async_copy(source, out.at[place], sems.at[place]))
        for copy in copies:
            copy.start()
        for copy in copies:
            copy.wait()

    anywhere = pl.BlockSpec(memory_space=pl.ANY)
    return pl.pallas_call(
        kernel,
        in_specs=[anywhere] * count,
        out_specs=pl.BlockSpec(memory_space=pltpu.VMEM),
        out_shape=jax.ShapeDtypeStruct((count, *shape), BF16),
        scratch_shapes=[pltpu.SemaphoreType.DMA((count,))],
        compiler_params=pltpu.CompilerParams(vmem_limit_bytes=VMEM_BYTES),
        cost_estimate=SMALL,
        name="pack",
    )(*[array for array, _ in parts])


def start_columns(table, pipe, x_ref, head_ref, rows, sems, from_x, to_rows, from_head=None):
    from_head = from_x if from_head is None else from_head
    flag = table[FLAG + pipe] == 1
    tail = pl.ds(HEAD, rows.shape[0] - HEAD)
    top = rows.at[pl.ds(0, HEAD), to_rows]
    plain = pltpu.make_async_copy(x_ref.at[pipe, 0, pl.ds(0, HEAD), from_x], top, sems.at[0])
    placed = pltpu.make_async_copy(head_ref.at[:, from_head], top, sems.at[0])
    rest = pltpu.make_async_copy(x_ref.at[pipe, 0, tail, from_x], rows.at[tail, to_rows], sems.at[1])
    pl.when(flag)(placed.start)
    pl.when(jnp.logical_not(flag))(plain.start)
    rest.start()
    return [plain, rest]


def products(table, x, sibling_x, head, sibling_head, ct, sibling_ct, groups):
    pipes, _, tokens, width = x.shape
    pair = width // CHIPS
    half = pair // 2
    window = core_window(width)
    kv = ct.shape[3]
    order, sizes = [], []
    for g, group in enumerate(groups):
        sizes.append(0)
        for pipe, r, low, high in group:
            order.append((g, sizes[g], pipe, r, low, high))
            sizes[g] += high - low
    count = len(order)

    def kernel(table, x_ref, sibling_x_ref, head_ref, sibling_head_ref, own_ct, other_ct, *refs):
        outs = refs[: len(groups)]
        own, other, block, row_sems, out_sems = refs[len(groups) :]
        core = table[CORE]
        waits = []
        for n, (_, _, pipe, r, _, _) in enumerate(order):
            from_x = pl.ds(pl.multiple_of(table[r] * pair + core * (pair - window), 128), window)
            here = pl.ds(n * window, window)
            waits.append(
                start_columns(table, pipe, x_ref, head_ref, own, row_sems.at[n, 0], from_x, here)
                + start_columns(
                    table, pipe, sibling_x_ref, sibling_head_ref, other, row_sems.at[n, 1], from_x, here,
                    columns(table[r], window),
                )
            )
        contract = (((0,), (0,)), ((), ()))
        written = []
        for n, (out, at, pipe, r, low, high) in enumerate(order):
            for copy in waits[n]:
                copy.wait()
            here = slice(n * window, (n + 1) * window)
            product = lax.dot_general(own[:, here], own_ct[pipe, 0], contract, preferred_element_type=F32)
            product += lax.dot_general(
                other[:, here], other_ct[pipe, 0], contract, preferred_element_type=F32
            )
            product = product.astype(BF16)

            @pl.when(core == 0)
            def _():
                block[n] = product[:half]

            @pl.when(core == 1)
            def _():
                block[n] = product[window - half :]

            copy = pltpu.make_async_copy(
                block.at[n, pl.ds(low, high - low)], outs[out].at[pl.ds(at, high - low)], out_sems.at[n]
            )
            copy.start()
            written.append(copy)
        for copy in written:
            copy.wait()

    anywhere = pl.BlockSpec(memory_space=pl.ANY)
    whole = pl.BlockSpec(memory_space=pltpu.VMEM)
    return pl.pallas_call(
        kernel,
        in_specs=[pl.BlockSpec(memory_space=pltpu.SMEM)] + [anywhere] * 4 + [whole] * 2,
        out_specs=[anywhere for _ in groups],
        out_shape=[jax.ShapeDtypeStruct((size, kv), BF16) for size in sizes],
        scratch_shapes=[
            pltpu.VMEM((tokens, count * window), BF16),
            pltpu.VMEM((tokens, count * window), BF16),
            pltpu.VMEM((count, half, kv), BF16),
            pltpu.SemaphoreType.DMA((count, 2, 2)),
            pltpu.SemaphoreType.DMA((count,)),
        ],
        compiler_params=pltpu.CompilerParams(vmem_limit_bytes=VMEM_BYTES),
        cost_estimate=SMALL,
        name="products",
    )(table, x, sibling_x, head, sibling_head, ct, sibling_ct)


def on_blocks(name, kernel, operands, outs):
    specs, arrays = [], []
    for operand in operands:
        array, *which = operand if isinstance(operand, tuple) else (operand,)
        shape = array.shape
        if len(shape) == 1:
            specs.append(pl.BlockSpec(memory_space=pltpu.SMEM))
        elif not which:
            specs.append(pl.BlockSpec(shape, lambda i, n=len(shape): (0,) * n))
        elif len(which) == 1:
            specs.append(pl.BlockSpec((pl.squeezed, *shape[1:]), lambda i, at=which[0]: (at, 0, 0)))
        else:
            specs.append(pl.BlockSpec((which[0], shape[1]), lambda i, at=which[1]: (at, 0)))
        arrays.append(array)
    return pl.pallas_call(
        kernel,
        grid=(1,),
        in_specs=specs,
        out_specs=[pl.BlockSpec(out.shape, lambda i, n=len(out.shape): (0,) * n) for out in outs],
        out_shape=outs,
        compiler_params=pltpu.CompilerParams(vmem_limit_bytes=VMEM_BYTES),
        cost_estimate=SMALL,
        name=name,
    )(*arrays)


def wide(*refs):
    total = refs[0][...].astype(F32)
    for ref in refs[1:]:
        total = total + ref[...].astype(F32)
    return total


def halves(first, second, first_out, second_out):
    first_out[...] = first[...]
    second_out[...] = second[...]


def first_sums(near0, far0, back1, far1, keep2, came2, up, down):
    rows = near0.shape[0]
    half = rows // 2
    far = wide(keep2, came2).astype(BF16)
    up[:rows] = wide(near0, far0).astype(BF16)
    up[rows:] = far[:half]
    down[:rows] = wide(back1, far1).astype(BF16)
    down[rows:] = far[half:]


def gain_row(weight, share):
    products = weight[...].astype(F32) * share
    total = products[:, :128]
    for low in range(128, products.shape[1], 128):
        total = total + products[:, low : low + 128]
    return jnp.sum(jnp.transpose(total), axis=0, keepdims=True)


def gain_column(table, gain, chip):
    pair = gain.shape[1] // CHIPS
    both = gain[:, columns(chip, pair)].astype(F32)
    row = jnp.where(table[CORE] == 0, both[:, : pair // 2], both[:, pair // 2 :])
    return jnp.transpose(jnp.broadcast_to(row, (8, pair // 2)))[:, :1]


def mirror_sums(table, own0, below0, above0, own1, below1, above1, weight0, weight1, gain, here, there):
    rows = own0.shape[0]
    for out, sums, weight, chip in (
        (here, (own0, below0, above0), weight0, table[0]),
        (there, (own1, below1, above1), weight1, table[Y_CHIPS]),
    ):
        share = wide(*sums)
        out[:rows] = (share * gain_column(table, gain, chip)).astype(BF16)
        out[rows:] = jnp.zeros((out.shape[0] - rows, out.shape[1]), BF16)
        out[rows : rows + 8, :rows] = jnp.broadcast_to(gain_row(weight, share), (8, rows)).astype(BF16)


def second_sums(keep1, came1, below, keep3, came3, above, ups, downs):
    half = ups.shape[0] // 2
    up, down = wide(keep1, came1), wide(keep3, came3)
    ups[:half] = (up[:half] + below[...].astype(F32)).astype(BF16)
    ups[half:] = up[half:].astype(BF16)
    downs[:half] = down[:half].astype(BF16)
    downs[half:] = (down[half:] + above[...].astype(F32)).astype(BF16)


def down_sums(table, keep0, came_low, came_high, below, above, weight, gain, weight_part, gain_part):
    share = wide(keep0, below, above) + jnp.concatenate([came_low[...], came_high[...]]).astype(F32)
    weight_part[...] = share * gain_column(table, gain, table[0])
    gain_part[...] = gain_row(weight, share)


def last_sums(weight_part, gain_part, mirrored0, mirrored1, weight_grad, gain_grad):
    rows = weight_part.shape[0]
    moved = wide(mirrored0, mirrored1)
    weight_grad[0] = weight_part[...] + moved[:rows]
    gain_grad[...] = gain_part[...] + moved[rows : rows + 1, :rows]


def layer(pipe, table, x, head, cotangent, scaled_ct, inverse, gain, own, sibling, carried):
    _, _, tokens, width = x.shape
    pair = width // CHIPS
    half = pair // 2
    kv = cotangent.shape[3]
    arrays = []
    for array, _ in [*own, *sibling]:
        if not any(array is known for known in arrays):
            arrays.append(array)
    position = [
        next(i for i, known in enumerate(arrays) if known is array) for array, _ in [*own, *sibling]
    ]
    index = [at for _, at in [*own, *sibling]]

    def kernel(table, x_ref, head_ref, ct_ref, scaled_ref, inverse_ref, gain_ref, *refs):
        pieces = refs[: len(arrays)]
        values_ref, grad_ref, rows, weight, grad, w_sems, x_sems, out_sems = refs[-8:]
        core = table[CORE]
        size = width // X_CHIPS
        row_waits = []
        for flip in range(X_CHIPS):
            half_x = table[X_HALF] if flip == 0 else 1 - table[X_HALF]
            where = columns(half_x, size)
            row_waits.append(start_columns(table, pipe, x_ref, head_ref, rows, x_sems.at[flip], where, where))
        waits = []
        for r in range(CHIPS):
            copies = []
            for side in range(2):
                piece = side * CHIPS + r
                source = pieces[position[piece]]
                if index[piece] is not None:
                    source = source.at[index[piece]]
                at = table[r] * pair + (core if side == 0 else 1 - core) * half
                copy = pltpu.make_async_copy(
                    source, weight.at[pl.ds(pl.multiple_of(at, 64), half)], w_sems.at[piece]
                )
                copy.start()
                copies.append(copy)
            waits.append(copies)
        values = jnp.zeros((tokens, kv), F32)
        for r in range(CHIPS):
            for copy in waits[r]:
                copy.wait()
            while row_waits[r // Y_CHIPS]:
                row_waits[r // Y_CHIPS].pop().wait()
            where = columns(table[r], pair)
            block = weight[pl.ds(pl.multiple_of(table[r] * pair, 128), pair)]
            values += jnp.dot(rows[:, where] * gain_ref[:, where], block, preferred_element_type=F32)
        inv = inverse_ref[0, :, :1]
        values = values * inv
        values_ref[0, 0] = values.astype(BF16)
        centre = jnp.sum(values * ct_ref[0, 0].astype(F32), axis=1, keepdims=True) / width
        pull = inv * inv * centre
        outs = []
        for chip in range(CHIPS):
            where = slice(chip * pair, (chip + 1) * pair)
            back = lax.dot_general(
                scaled_ref[0, 0], weight[where], (((1,), (1,)), ((), ())), preferred_element_type=F32
            )
            grad[:, where] = (
                back * gain_ref[:, where].astype(F32) - rows[:, where].astype(F32) * pull
            ).astype(BF16)
            if chip % 2 == 1:
                done = pl.ds((chip - 1) * pair, 2 * pair)
                copy = pltpu.make_async_copy(
                    grad.at[:, done], grad_ref.at[pipe, 0, :, done], out_sems.at[chip // 2]
                )
                copy.start()
                outs.append(copy)
        for copy in outs:
            copy.wait()

    anywhere = pl.BlockSpec(memory_space=pl.ANY)
    ct_spec = pl.BlockSpec((1, 1, tokens, kv), lambda i: (pipe, 0, 0, 0))
    operands = [table, x, head, cotangent, scaled_ct, inverse, gain, *arrays, *carried]
    return pl.pallas_call(
        kernel,
        grid=(1,),
        in_specs=[
            pl.BlockSpec(memory_space=pltpu.SMEM),
            anywhere,
            anywhere,
            ct_spec,
            ct_spec,
            pl.BlockSpec((1, tokens, 128), lambda i: (pipe, 0, 0)),
            pl.BlockSpec((1, width), lambda i: (0, 0)),
        ]
        + [anywhere] * (len(arrays) + len(carried)),
        out_specs=[ct_spec, anywhere],
        out_shape=[
            jax.ShapeDtypeStruct(cotangent.shape, BF16),
            jax.ShapeDtypeStruct(x.shape, BF16),
        ],
        scratch_shapes=[
            pltpu.VMEM((tokens, width), BF16),
            pltpu.VMEM((width, kv), BF16),
            pltpu.VMEM((tokens, width), BF16),
            pltpu.SemaphoreType.DMA((2 * CHIPS,)),
            pltpu.SemaphoreType.DMA((X_CHIPS, 2)),
            pltpu.SemaphoreType.DMA((CHIPS // 2,)),
        ],
        input_output_aliases={7 + len(arrays) + i: i for i in range(len(carried))},
        compiler_params=pltpu.CompilerParams(vmem_limit_bytes=VMEM_BYTES),
        cost_estimate=SMALL,
        name="layer",
    )(*operands)


def route_images(image_rows, image_route, section_place, fsdp_place):
    fsdp_count = lax.axis_size("fsdp")
    section_count = lax.axis_size("section")
    ring = section_count // 2
    width = image_rows.shape[2]
    size = -(-width // (3 * 128)) * 128
    pipe = section_place // ring
    z = section_place % ring
    enc_rows = image_rows.shape[1]
    enc_count = enc_rows // BLOCK_ROWS
    head = fsdp_count * CAP * BLOCK_ROWS
    routes = lax.dynamic_index_in_dim(image_route, pipe, 0, keepdims=False)
    own_route = lax.dynamic_index_in_dim(routes, fsdp_place, 0, keepdims=False)
    ids = jnp.arange(enc_count, dtype=jnp.int32)
    earlier = (own_route[:, None] == own_route[None, :]) & (ids[None, :] < ids[:, None])
    slot_of = own_route * CAP + jnp.sum(earlier.astype(jnp.int32), axis=1)
    goes_to = jnp.repeat(slot_of * BLOCK_ROWS, BLOCK_ROWS) + jnp.tile(
        jnp.arange(BLOCK_ROWS, dtype=jnp.int32), enc_count
    )
    row_ids = jnp.arange(head, dtype=jnp.int32)
    select = (row_ids[:, None] == goes_to[None, :]).astype(BF16)
    from_end = jnp.where(pipe == 0, z, ring - 1 - z)
    own_part = jnp.where(from_end == ring - 1, 2, jnp.minimum(from_end, 1))
    starts = jnp.array([0, size, width - size], jnp.int32)
    start = jnp.where(own_part == 0, 0, jnp.where(own_part == 1, size, width - size))
    part = lax.dynamic_slice(image_rows, (pipe, 0, start), (1, enc_rows, size))[0]
    outgoing = jnp.dot(select, part, preferred_element_type=F32).astype(BF16)
    incoming = lax.all_to_all(outgoing, "fsdp", split_axis=0, concat_axis=0, tiled=True)
    end = section_count - 1
    arrivals = jnp.sum((routes == fsdp_place).astype(jnp.int32), axis=1)
    offsets = jnp.cumsum(arrivals) - arrivals
    slot_rows = CAP * BLOCK_ROWS
    within = row_ids % slot_rows
    lands = jnp.repeat(offsets, slot_rows) * BLOCK_ROWS + within
    valid = within < jnp.repeat(arrivals, slot_rows) * BLOCK_ROWS
    lands = jnp.where(valid, lands, -1)
    perm = (jnp.arange(head, dtype=jnp.int32)[:, None] == lands[None, :]).astype(BF16)
    numbers = jnp.concatenate(
        [
            (jnp.sum(arrivals) * BLOCK_ROWS)[None],
            (section_place == 0).astype(jnp.int32)[None],
            (section_place == end).astype(jnp.int32)[None],
            starts,
            pipe[None],
        ]
    )
    return incoming, perm, numbers


def move_images(incoming):
    count = lax.axis_size("section")
    ring, end = count // 2, count - 1
    return [
        incoming,
        lax.ppermute(incoming, "section", [(1, 0), (end - 1, end)]),
        lax.ppermute(incoming, "section", [(ring - 1, 0), (end - ring + 1, end)]),
    ]


def hold(value, *before):
    return lax.optimization_barrier((value, before))[0]


def per_device(
    section_inputs,
    value_cotangent,
    down_weight,
    up_weight,
    down_gain,
    up_gain,
    image_rows,
    image_route,
):
    section_place = lax.axis_index("section")
    fsdp_place = lax.axis_index("fsdp")
    core = fsdp_place % 2
    y = fsdp_place // 2 % Y_CHIPS
    x = fsdp_place // (2 * Y_CHIPS)
    r = jnp.arange(CHIPS, dtype=jnp.int32)
    chips = (x ^ (r // Y_CHIPS)) * Y_CHIPS + (y + r % Y_CHIPS) % Y_CHIPS

    incoming, perm, numbers = route_images(image_rows, image_route, section_place, fsdp_place)
    table = jnp.concatenate([chips, core[None], numbers, x[None]]).astype(jnp.int32)

    shard, kv = down_weight.shape[1:]

    part = jax.ShapeDtypeStruct((shard, kv), BF16)

    sibling_x = to_sibling(section_inputs)
    w0 = pack([(down_weight, 0), (up_weight, 0)])
    w3, w1, w4 = to_next(w0), to_previous(w0), to_across(w0)
    scaled_ct, inverse = scale(section_inputs, value_cotangent)
    w3, w1, w4, incoming, perm, table = hold((w3, w1, w4, incoming, perm, table), scaled_ct, sibling_x)
    images = move_images(incoming)
    w2, w5, w7 = to_next(w3), to_previous(w4), to_across(w3)
    early = pack([(w0, 0), (w0, 1), (w1, 0), (w1, 1), (w3, 0), (w3, 1), (w4, 0), (w4, 1)])
    head, other_head, scaled_ct, inverse = patch(
        hold(table, early), section_inputs, value_cotangent, perm, images, scaled_ct, inverse
    )
    w2, w5, w7, other_head, scaled_ct, early = hold((w2, w5, w7, other_head, scaled_ct, early))
    sibling_head, sibling_ct = to_sibling(other_head), to_sibling(scaled_ct)
    down7, up5 = on_blocks("halves", halves, [(w7, 0), (w5, 1)], [part, part])
    down6, up6 = to_next(down7), to_previous(up5)

    rows = (section_inputs, sibling_x, head, sibling_head, scaled_ct, sibling_ct)
    half = shard // 2

    def blocks(*parts):
        return tuple((pipe, r, 0, shard) for pipe, r in parts)

    far0_near1, far1_back0, send20 = products(
        table,
        *rows,
        (blocks((1, 2), (1, 5)), blocks((1, 6), (1, 3)), (*blocks((0, 6)), (0, 4, 0, half))),
    )
    far0_near1, far1_back0, send20, down6, up6, w7, early = hold(
        (far0_near1, far1_back0, send20, down6, up6, w7, early)
    )
    from_below, from_above, came20 = to_next(far0_near1), to_previous(far1_back0), to_across(send20)
    sibling_early = to_sibling(early)
    down_places = ((0, 0), (0, 2), (1, 0), (0, 4), (0, 6), (1, 2), (2, None), (1, 4))
    up_places = ((0, 1), (0, 3), (1, 1), (0, 5), (0, 7), (1, 3), (3, None), (1, 5))
    near0, back1, keep2, send130, own01, keep13, keep0 = products(
        hold(table, up6),
        *rows,
        (
            blocks((1, 1)), blocks((1, 7)), blocks((0, 2)), (*blocks((0, 5), (0, 7)), (0, 4, half, shard)),
            blocks((1, 0), (1, 4)), blocks((0, 1), (0, 3)), blocks((0, 0)),
        ),
    )

    def pieces(arrays, places):
        return [(arrays[array], at) for array, at in places]

    middle = pack([(w2, 0), (w2, 1), (w5, 0), (w5, 1), (w7, 0), (w7, 1)])
    from_below, from_above, came20, send130 = hold(
        (from_below, from_above, came20, send130), keep0, middle, sibling_early
    )
    message = jax.ShapeDtypeStruct((shard + shard // 2, kv), BF16)
    up, down = on_blocks(
        "first_sums",
        first_sums,
        [near0, (from_below, shard, 0), back1, (from_above, shard, 0), keep2, (came20, shard, 0)],
        [message, message],
    )
    below, above = to_next(up), to_previous(down)
    came130 = to_across(hold(send130, up))
    own = (early, middle, down6, up6)
    sibling = [sibling_early, *[to_sibling(hold(array, up)) for array in (middle, down6, up6)]]
    filled = layer(
        0,
        hold(table, up),
        section_inputs, head, value_cotangent, scaled_ct, inverse, down_gain,
        pieces(own, down_places), pieces(sibling, down_places), (),
    )
    below, above = hold((below, above), filled[0])
    payload = jax.ShapeDtypeStruct((shard + 16, kv), BF16)
    here, there = on_blocks(
        "mirror_sums",
        mirror_sums,
        [
            table, (own01, shard, 0), (below, shard, 0), (from_above, shard, 1),
            (own01, shard, 1), (from_below, shard, 1), (above, shard, 0), (up_weight, 0), (early, 7), up_gain,
        ],
        [payload, payload],
    )
    mirrored0, mirrored1 = to_mirror(here, 0), to_mirror(there, 1)
    ups, downs = on_blocks(
        "second_sums",
        second_sums,
        [
            (keep13, shard, 0), (came130, shard, 0), (below, half, 2),
            (keep13, shard, 1), (came130, shard, 1), (above, half, 2),
        ],
        [part, part],
    )
    last_below, last_above = to_next(ups), to_previous(downs)
    values, input_grad = layer(
        1,
        hold(table, ups),
        section_inputs, head, value_cotangent, scaled_ct, inverse, up_gain,
        pieces(own, up_places), pieces(sibling, up_places), tuple(filled),
    )
    last_below, last_above = hold((last_below, last_above), values)
    weight_part, gain_part = on_blocks(
        "down_sums",
        down_sums,
        [
            table, keep0, (came20, half, 2), (came130, half, 4), last_below, last_above, (down_weight, 0), down_gain,
        ],
        [jax.ShapeDtypeStruct((shard, kv), F32), jax.ShapeDtypeStruct((1, shard), F32)],
    )
    mirrored0, mirrored1 = hold((mirrored0, mirrored1), weight_part)
    weight_grad, gain_grad = on_blocks(
        "last_sums",
        last_sums,
        [weight_part, gain_part, mirrored0, mirrored1],
        [jax.ShapeDtypeStruct((1, shard, kv), F32), jax.ShapeDtypeStruct((1, shard), F32)],
    )
    return (values, input_grad, weight_grad, gain_grad)


def solution(mesh):
    return jax.shard_map(
        per_device,
        mesh=mesh,
        in_specs=(
            P(None, "section", "fsdp", None),
            P(None, "section", "fsdp", None),
            P("section", "fsdp", None),
            P("section", "fsdp", None),
            P("section", None),
            P("section", None),
            P(None, "fsdp", None),
            P(),
        ),
        out_specs=(
            P(None, "section", "fsdp", None),
            P(None, "section", "fsdp", None),
            P("section", "fsdp", None),
            P("section", "fsdp"),
        ),
        check_vma=False,
    )
```

```python
import jax
import jax.numpy as jnp
from jax import lax
from jax.experimental import pallas as pl
from jax.experimental.pallas import tpu as pltpu
from jax.sharding import PartitionSpec as P

BLOCK_ROWS = 4
CAP = 2
EPSILON = 1e-05
HEAD = 128
VMEM_BYTES = 63 * 1024 * 1024 + 512 * 1024
SMALL = pl.CostEstimate(flops=1, bytes_accessed=1, transcendentals=0)
F32 = jnp.float32
BF16 = jnp.bfloat16

X_CHIPS, Y_CHIPS = 2, 4
CHIPS = X_CHIPS * Y_CHIPS
CORE, LIVE, FLAG, PART, PIPE, X_HALF = 8, 9, 10, 12, 15, 16


def fsdp_route(step):
    route = []
    for x in range(X_CHIPS):
        for y in range(Y_CHIPS):
            for core in range(2):
                to_x, to_y, to_core = step(x, y, core)
                target = (to_x % X_CHIPS * Y_CHIPS + to_y % Y_CHIPS) * 2 + to_core % 2
                route.append(((x * Y_CHIPS + y) * 2 + core, target))
    return route


def to_next(block):
    return lax.ppermute(block, "fsdp", fsdp_route(lambda x, y, core: (x, y + 1, core)))


def to_previous(block):
    return lax.ppermute(block, "fsdp", fsdp_route(lambda x, y, core: (x, y - 1, core)))


def to_across(block):
    return lax.ppermute(block, "fsdp", fsdp_route(lambda x, y, core: (x + 1, y, core)))


def to_sibling(block):
    return lax.ppermute(block, "fsdp", fsdp_route(lambda x, y, core: (x, y, core + 1)))


def to_mirror(block, flip):
    sections, fsdps = lax.axis_size("section"), lax.axis_size("fsdp")
    route = []
    for section in range(sections):
        for fsdp in range(fsdps):
            to_fsdp = (fsdp + flip * fsdps // X_CHIPS) % fsdps
            route.append((section * fsdps + fsdp, (sections - 1 - section) * fsdps + to_fsdp))
    return lax.ppermute(block, ("section", "fsdp"), route)


def columns(chip, size):
    return pl.ds(pl.multiple_of(chip * size, 128), size)


def core_window(width):
    return -(-(width // CHIPS // 2) // 128) * 128


def inverse_rms(rows):
    tokens, width = rows.shape
    pair = width // CHIPS
    total = jnp.zeros((tokens, pair), F32)
    for chip in range(CHIPS):
        part = rows[:, chip * pair : (chip + 1) * pair].astype(F32)
        total = total + part * part
    return lax.rsqrt(jnp.sum(total, axis=1, keepdims=True) / width + EPSILON)


def scale_kernel(x_ref, ct_ref, ct_out, inverse_out):
    inverse = inverse_rms(x_ref.at[0, 0])
    ct_out[0, 0] = (ct_ref[0, 0].astype(F32) * inverse).astype(BF16)
    inverse_out[0] = jnp.broadcast_to(inverse, inverse_out.shape[1:])


def scale(section_inputs, cotangent):
    pipes, _, tokens, width = section_inputs.shape
    kv = cotangent.shape[3]
    tile = 64
    ct_spec = pl.BlockSpec((1, 1, tile, kv), lambda p, t: (p, 0, t, 0))
    return pl.pallas_call(
        scale_kernel,
        grid=(pipes, tokens // tile),
        in_specs=[pl.BlockSpec((1, 1, tile, width), lambda p, t: (p, 0, t, 0)), ct_spec],
        out_specs=[ct_spec, pl.BlockSpec((1, tile, 128), lambda p, t: (p, t, 0))],
        out_shape=[
            jax.ShapeDtypeStruct(cotangent.shape, BF16),
            jax.ShapeDtypeStruct((pipes, tokens, 128), F32),
        ],
        compiler_params=pltpu.CompilerParams(vmem_limit_bytes=VMEM_BYTES),
        cost_estimate=SMALL,
        name="scale",
    )(section_inputs, cotangent)


def patch_kernel(
    table, ct_ref, perm_ref, x_ref, im0, im1, im2, ct_in, inverse_in, head_ref, other_ref, ct_out, inverse_out,
    rows, others, images, new_ct, new_inverse, in_sems, out_sems,
):
    pipe = table[PIPE]
    width = rows.shape[1]
    pair = width // CHIPS
    window = others.shape[1] // CHIPS

    @pl.when(table[FLAG + pipe] == 1)
    def _():
        coming = [pltpu.make_async_copy(x_ref.at[pipe, 0, pl.ds(0, HEAD)], rows, in_sems.at[0])]
        for part, image in enumerate((im0, im1, im2)):
            coming.append(pltpu.make_async_copy(image, images.at[part], in_sems.at[1 + part]))
        for copy in coming:
            copy.start()
        for copy in coming:
            copy.wait()
        live = lax.broadcasted_iota(jnp.int32, (HEAD, 1), 0) < table[LIVE]
        for part in range(3):
            where = pl.ds(pl.multiple_of(table[PART + part], 128), images.shape[2])
            arrived = jnp.dot(perm_ref[...], images[part], preferred_element_type=F32).astype(BF16)
            rows[:, where] = jnp.where(live, arrived, rows[:, where])
        going = []
        total = jnp.zeros((HEAD, pair), F32)
        for chip in range(CHIPS):
            start = chip * pair + (1 - table[CORE]) * (pair - window)
            others[:, chip * window : (chip + 1) * window] = rows[
                :, pl.ds(pl.multiple_of(start, 128), window)
            ]
            part = rows[:, chip * pair : (chip + 1) * pair].astype(F32)
            total = total + part * part
            if chip % 4 == 3:
                for n, (source, target, size) in enumerate(((rows, head_ref, pair), (others, other_ref, window))):
                    done = pl.ds((chip - 3) * size, 4 * size)
                    going.append(
                        pltpu.make_async_copy(source.at[:, done], target.at[:, done], out_sems.at[n, chip // 4])
                    )
                    going[-1].start()
        inverse = lax.rsqrt(jnp.sum(total, axis=1, keepdims=True) / width + EPSILON)
        new_ct[...] = (ct_ref[0, 0].astype(F32) * inverse).astype(BF16)
        new_inverse[...] = jnp.broadcast_to(inverse, new_inverse.shape)
        top = pl.ds(0, HEAD)
        for n, (source, target) in enumerate(
            ((new_ct, ct_out.at[pipe, 0, top]), (new_inverse, inverse_out.at[pipe, top]))
        ):
            going.append(pltpu.make_async_copy(source, target, out_sems.at[2, n]))
            going[-1].start()
        for copy in going:
            copy.wait()


def patch(table, section_inputs, cotangent, perm, images, scaled_ct, inverse):
    width = section_inputs.shape[3]
    kv = cotangent.shape[3]
    window = core_window(width)
    anywhere = pl.BlockSpec(memory_space=pl.ANY)
    return pl.pallas_call(
        patch_kernel,
        grid_spec=pltpu.PrefetchScalarGridSpec(
            num_scalar_prefetch=1,
            grid=(1,),
            in_specs=[
                pl.BlockSpec((1, 1, HEAD, kv), lambda i, table: (table[PIPE], 0, 0, 0)),
                pl.BlockSpec(memory_space=pltpu.VMEM),
            ]
            + [anywhere] * 6,
            out_specs=[anywhere] * 4,
            scratch_shapes=[
                pltpu.VMEM((HEAD, width), BF16),
                pltpu.VMEM((HEAD, CHIPS * window), BF16),
                pltpu.VMEM((3, *images[0].shape), BF16),
                pltpu.VMEM((HEAD, kv), BF16),
                pltpu.VMEM((HEAD, inverse.shape[2]), F32),
                pltpu.SemaphoreType.DMA((4,)),
                pltpu.SemaphoreType.DMA((3, 2)),
            ],
        ),
        out_shape=[
            jax.ShapeDtypeStruct((HEAD, width), BF16),
            jax.ShapeDtypeStruct((HEAD, CHIPS * window), BF16),
            jax.ShapeDtypeStruct(scaled_ct.shape, BF16),
            jax.ShapeDtypeStruct(inverse.shape, F32),
        ],
        input_output_aliases={7: 2, 8: 3},
        compiler_params=pltpu.CompilerParams(vmem_limit_bytes=VMEM_BYTES),
        cost_estimate=SMALL,
        name="patch",
    )(table, cotangent, perm, section_inputs, *images, scaled_ct, inverse)


def pack(parts):
    count = len(parts)
    shape = parts[0][0].shape[-2:]

    def kernel(*refs):
        out, sems = refs[count:]
        copies = []
        for place, (ref, (_, at)) in enumerate(zip(refs, parts)):
            source = ref if at is None else ref.at[at]
            copies.append(pltpu.make_async_copy(source, out.at[place], sems.at[place]))
        for copy in copies:
            copy.start()
        for copy in copies:
            copy.wait()

    anywhere = pl.BlockSpec(memory_space=pl.ANY)
    return pl.pallas_call(
        kernel,
        in_specs=[anywhere] * count,
        out_specs=pl.BlockSpec(memory_space=pltpu.VMEM),
        out_shape=jax.ShapeDtypeStruct((count, *shape), BF16),
        scratch_shapes=[pltpu.SemaphoreType.DMA((count,))],
        compiler_params=pltpu.CompilerParams(vmem_limit_bytes=VMEM_BYTES),
        cost_estimate=SMALL,
        name="pack",
    )(*[array for array, _ in parts])


def start_columns(table, pipe, x_ref, head_ref, rows, sems, from_x, to_rows, from_head=None):
    from_head = from_x if from_head is None else from_head
    flag = table[FLAG + pipe] == 1
    tail = pl.ds(HEAD, rows.shape[0] - HEAD)
    top = rows.at[pl.ds(0, HEAD), to_rows]
    plain = pltpu.make_async_copy(x_ref.at[pipe, 0, pl.ds(0, HEAD), from_x], top, sems.at[0])
    placed = pltpu.make_async_copy(head_ref.at[:, from_head], top, sems.at[0])
    rest = pltpu.make_async_copy(x_ref.at[pipe, 0, tail, from_x], rows.at[tail, to_rows], sems.at[1])
    pl.when(flag)(placed.start)
    pl.when(jnp.logical_not(flag))(plain.start)
    rest.start()
    return [plain, rest]


def products(table, x, sibling_x, head, sibling_head, ct, sibling_ct, groups):
    pipes, _, tokens, width = x.shape
    pair = width // CHIPS
    half = pair // 2
    window = core_window(width)
    kv = ct.shape[3]
    order, sizes = [], []
    for g, group in enumerate(groups):
        sizes.append(0)
        for pipe, r, low, high in group:
            order.append((g, sizes[g], pipe, r, low, high))
            sizes[g] += high - low
    count = len(order)

    def kernel(table, x_ref, sibling_x_ref, head_ref, sibling_head_ref, own_ct, other_ct, *refs):
        outs = refs[: len(groups)]
        own, other, block, row_sems, out_sems = refs[len(groups) :]
        core = table[CORE]
        waits = []
        for n, (_, _, pipe, r, _, _) in enumerate(order):
            from_x = pl.ds(pl.multiple_of(table[r] * pair + core * (pair - window), 128), window)
            here = pl.ds(n * window, window)
            waits.append(
                start_columns(table, pipe, x_ref, head_ref, own, row_sems.at[n, 0], from_x, here)
                + start_columns(
                    table, pipe, sibling_x_ref, sibling_head_ref, other, row_sems.at[n, 1], from_x, here,
                    columns(table[r], window),
                )
            )
        contract = (((0,), (0,)), ((), ()))
        written = []
        for n, (out, at, pipe, r, low, high) in enumerate(order):
            for copy in waits[n]:
                copy.wait()
            here = slice(n * window, (n + 1) * window)
            product = lax.dot_general(own[:, here], own_ct[pipe, 0], contract, preferred_element_type=F32)
            product += lax.dot_general(
                other[:, here], other_ct[pipe, 0], contract, preferred_element_type=F32
            )
            product = product.astype(BF16)

            @pl.when(core == 0)
            def _():
                block[n] = product[:half]

            @pl.when(core == 1)
            def _():
                block[n] = product[window - half :]

            copy = pltpu.make_async_copy(
                block.at[n, pl.ds(low, high - low)], outs[out].at[pl.ds(at, high - low)], out_sems.at[n]
            )
            copy.start()
            written.append(copy)
        for copy in written:
            copy.wait()

    anywhere = pl.BlockSpec(memory_space=pl.ANY)
    whole = pl.BlockSpec(memory_space=pltpu.VMEM)
    return pl.pallas_call(
        kernel,
        in_specs=[pl.BlockSpec(memory_space=pltpu.SMEM)] + [anywhere] * 4 + [whole] * 2,
        out_specs=[anywhere for _ in groups],
        out_shape=[jax.ShapeDtypeStruct((size, kv), BF16) for size in sizes],
        scratch_shapes=[
            pltpu.VMEM((tokens, count * window), BF16),
            pltpu.VMEM((tokens, count * window), BF16),
            pltpu.VMEM((count, half, kv), BF16),
            pltpu.SemaphoreType.DMA((count, 2, 2)),
            pltpu.SemaphoreType.DMA((count,)),
        ],
        compiler_params=pltpu.CompilerParams(vmem_limit_bytes=VMEM_BYTES),
        cost_estimate=SMALL,
        name="products",
    )(table, x, sibling_x, head, sibling_head, ct, sibling_ct)


def on_blocks(name, kernel, operands, outs):
    specs, arrays = [], []
    for operand in operands:
        array, *which = operand if isinstance(operand, tuple) else (operand,)
        shape = array.shape
        if len(shape) == 1:
            specs.append(pl.BlockSpec(memory_space=pltpu.SMEM))
        elif not which:
            specs.append(pl.BlockSpec(shape, lambda i, n=len(shape): (0,) * n))
        elif len(which) == 1:
            specs.append(pl.BlockSpec((pl.squeezed, *shape[1:]), lambda i, at=which[0]: (at, 0, 0)))
        else:
            specs.append(pl.BlockSpec((which[0], shape[1]), lambda i, at=which[1]: (at, 0)))
        arrays.append(array)
    return pl.pallas_call(
        kernel,
        grid=(1,),
        in_specs=specs,
        out_specs=[pl.BlockSpec(out.shape, lambda i, n=len(out.shape): (0,) * n) for out in outs],
        out_shape=outs,
        compiler_params=pltpu.CompilerParams(vmem_limit_bytes=VMEM_BYTES),
        cost_estimate=SMALL,
        name=name,
    )(*arrays)


def wide(*refs):
    total = refs[0][...].astype(F32)
    for ref in refs[1:]:
        total = total + ref[...].astype(F32)
    return total


def halves(first, second, first_out, second_out):
    first_out[...] = first[...]
    second_out[...] = second[...]


def first_sums(near0, far0, back1, far1, keep2, came2, up, down):
    rows = near0.shape[0]
    half = rows // 2
    far = wide(keep2, came2).astype(BF16)
    up[:rows] = wide(near0, far0).astype(BF16)
    up[rows:] = far[:half]
    down[:rows] = wide(back1, far1).astype(BF16)
    down[rows:] = far[half:]


def gain_row(weight, share):
    products = weight[...].astype(F32) * share
    total = products[:, :128]
    for low in range(128, products.shape[1], 128):
        total = total + products[:, low : low + 128]
    return jnp.sum(jnp.transpose(total), axis=0, keepdims=True)


def gain_column(table, gain, chip):
    pair = gain.shape[1] // CHIPS
    both = gain[:, columns(chip, pair)].astype(F32)
    row = jnp.where(table[CORE] == 0, both[:, : pair // 2], both[:, pair // 2 :])
    return jnp.transpose(jnp.broadcast_to(row, (8, pair // 2)))[:, :1]


def mirror_sums(table, own0, below0, above0, own1, below1, above1, weight0, weight1, gain, here, there):
    rows = own0.shape[0]
    for out, sums, weight, chip in (
        (here, (own0, below0, above0), weight0, table[0]),
        (there, (own1, below1, above1), weight1, table[Y_CHIPS]),
    ):
        share = wide(*sums)
        out[:rows] = (share * gain_column(table, gain, chip)).astype(BF16)
        below = out.shape[0] - rows
        out[rows:] = jnp.zeros((below, out.shape[1]), BF16)
        out[rows:, :rows] = jnp.broadcast_to(gain_row(weight, share), (below, rows)).astype(BF16)


def second_sums(keep1, came1, below, keep3, came3, above, ups, downs):
    half = ups.shape[0] // 2
    up, down = wide(keep1, came1), wide(keep3, came3)
    ups[:half] = (up[:half] + below[...].astype(F32)).astype(BF16)
    ups[half:] = up[half:].astype(BF16)
    downs[:half] = down[:half].astype(BF16)
    downs[half:] = (down[half:] + above[...].astype(F32)).astype(BF16)


def down_sums(table, keep0, came_low, came_high, below, above, weight, gain, weight_part, gain_part):
    share = wide(keep0, below, above) + jnp.concatenate([came_low[...], came_high[...]]).astype(F32)
    weight_part[...] = share * gain_column(table, gain, table[0])
    gain_part[...] = gain_row(weight, share)


def last_sums(weight_part, gain_part, mirrored0, mirrored1, weight_grad, gain_grad):
    rows = weight_part.shape[0]
    moved = wide(mirrored0, mirrored1)
    weight_grad[0] = weight_part[...] + moved[:rows]
    gain_grad[...] = gain_part[...] + moved[rows : rows + 1, :rows]


def layer(pipe, table, x, head, cotangent, scaled_ct, inverse, gain, own, sibling, carried):
    _, _, tokens, width = x.shape
    pair = width // CHIPS
    half = pair // 2
    kv = cotangent.shape[3]
    arrays = []
    for array, _ in [*own, *sibling]:
        if not any(array is known for known in arrays):
            arrays.append(array)
    position = [
        next(i for i, known in enumerate(arrays) if known is array) for array, _ in [*own, *sibling]
    ]
    index = [at for _, at in [*own, *sibling]]

    def kernel(table, x_ref, head_ref, ct_ref, scaled_ref, inverse_ref, gain_ref, *refs):
        pieces = refs[: len(arrays)]
        values_ref, grad_ref, rows, weight, grad, w_sems, x_sems, out_sems = refs[-8:]
        core = table[CORE]
        size = width // X_CHIPS
        row_waits = []
        for flip in range(X_CHIPS):
            half_x = table[X_HALF] if flip == 0 else 1 - table[X_HALF]
            where = columns(half_x, size)
            row_waits.append(start_columns(table, pipe, x_ref, head_ref, rows, x_sems.at[flip], where, where))
        waits = []
        for r in range(CHIPS):
            copies = []
            for side in range(2):
                piece = side * CHIPS + r
                source = pieces[position[piece]]
                if index[piece] is not None:
                    source = source.at[index[piece]]
                at = table[r] * pair + (core if side == 0 else 1 - core) * half
                copy = pltpu.make_async_copy(
                    source, weight.at[pl.ds(pl.multiple_of(at, 64), half)], w_sems.at[piece]
                )
                copy.start()
                copies.append(copy)
            waits.append(copies)
        values = jnp.zeros((tokens, kv), F32)
        for r in range(CHIPS):
            for copy in waits[r]:
                copy.wait()
            while row_waits[r // Y_CHIPS]:
                row_waits[r // Y_CHIPS].pop().wait()
            where = columns(table[r], pair)
            block = weight[pl.ds(pl.multiple_of(table[r] * pair, 128), pair)]
            values += jnp.dot(rows[:, where] * gain_ref[:, where], block, preferred_element_type=F32)
        inv = inverse_ref[0, :, :1]
        values = values * inv
        values_ref[0, 0] = values.astype(BF16)
        centre = jnp.sum(values * ct_ref[0, 0].astype(F32), axis=1, keepdims=True) / width
        pull = inv * inv * centre
        outs = []
        for chip in range(CHIPS):
            where = slice(chip * pair, (chip + 1) * pair)
            back = lax.dot_general(
                scaled_ref[0, 0], weight[where], (((1,), (1,)), ((), ())), preferred_element_type=F32
            )
            grad[:, where] = (
                back * gain_ref[:, where].astype(F32) - rows[:, where].astype(F32) * pull
            ).astype(BF16)
            if chip % 2 == 1:
                done = pl.ds((chip - 1) * pair, 2 * pair)
                copy = pltpu.make_async_copy(
                    grad.at[:, done], grad_ref.at[pipe, 0, :, done], out_sems.at[chip // 2]
                )
                copy.start()
                outs.append(copy)
        for copy in outs:
            copy.wait()

    anywhere = pl.BlockSpec(memory_space=pl.ANY)
    ct_spec = pl.BlockSpec((1, 1, tokens, kv), lambda i: (pipe, 0, 0, 0))
    operands = [table, x, head, cotangent, scaled_ct, inverse, gain, *arrays, *carried]
    return pl.pallas_call(
        kernel,
        grid=(1,),
        in_specs=[
            pl.BlockSpec(memory_space=pltpu.SMEM),
            anywhere,
            anywhere,
            ct_spec,
            ct_spec,
            pl.BlockSpec((1, tokens, 128), lambda i: (pipe, 0, 0)),
            pl.BlockSpec((1, width), lambda i: (0, 0)),
        ]
        + [anywhere] * (len(arrays) + len(carried)),
        out_specs=[ct_spec, anywhere],
        out_shape=[
            jax.ShapeDtypeStruct(cotangent.shape, BF16),
            jax.ShapeDtypeStruct(x.shape, BF16),
        ],
        scratch_shapes=[
            pltpu.VMEM((tokens, width), BF16),
            pltpu.VMEM((width, kv), BF16),
            pltpu.VMEM((tokens, width), BF16),
            pltpu.SemaphoreType.DMA((2 * CHIPS,)),
            pltpu.SemaphoreType.DMA((X_CHIPS, 2)),
            pltpu.SemaphoreType.DMA((CHIPS // 2,)),
        ],
        input_output_aliases={7 + len(arrays) + i: i for i in range(len(carried))},
        compiler_params=pltpu.CompilerParams(vmem_limit_bytes=VMEM_BYTES),
        cost_estimate=SMALL,
        name="layer",
    )(*operands)


def route_images(image_rows, image_route, section_place, fsdp_place):
    fsdp_count = lax.axis_size("fsdp")
    section_count = lax.axis_size("section")
    ring = section_count // 2
    width = image_rows.shape[2]
    size = -(-width // (3 * 128)) * 128
    pipe = section_place // ring
    z = section_place % ring
    enc_rows = image_rows.shape[1]
    enc_count = enc_rows // BLOCK_ROWS
    head = fsdp_count * CAP * BLOCK_ROWS
    routes = lax.dynamic_index_in_dim(image_route, pipe, 0, keepdims=False)
    own_route = lax.dynamic_index_in_dim(routes, fsdp_place, 0, keepdims=False)
    ids = jnp.arange(enc_count, dtype=jnp.int32)
    earlier = (own_route[:, None] == own_route[None, :]) & (ids[None, :] < ids[:, None])
    slot_of = own_route * CAP + jnp.sum(earlier.astype(jnp.int32), axis=1)
    goes_to = jnp.repeat(slot_of * BLOCK_ROWS, BLOCK_ROWS) + jnp.tile(
        jnp.arange(BLOCK_ROWS, dtype=jnp.int32), enc_count
    )
    row_ids = jnp.arange(head, dtype=jnp.int32)
    select = (row_ids[:, None] == goes_to[None, :]).astype(BF16)
    from_end = jnp.where(pipe == 0, z, ring - 1 - z)
    own_part = jnp.where(from_end == ring - 1, 2, jnp.minimum(from_end, 1))
    starts = jnp.array([0, size, width - size], jnp.int32)
    start = jnp.where(own_part == 0, 0, jnp.where(own_part == 1, size, width - size))
    part = lax.dynamic_slice(image_rows, (pipe, 0, start), (1, enc_rows, size))[0]
    outgoing = jnp.dot(select, part, preferred_element_type=F32).astype(BF16)
    incoming = lax.all_to_all(outgoing, "fsdp", split_axis=0, concat_axis=0, tiled=True)
    end = section_count - 1
    arrivals = jnp.sum((routes == fsdp_place).astype(jnp.int32), axis=1)
    offsets = jnp.cumsum(arrivals) - arrivals
    slot_rows = CAP * BLOCK_ROWS
    within = row_ids % slot_rows
    lands = jnp.repeat(offsets, slot_rows) * BLOCK_ROWS + within
    valid = within < jnp.repeat(arrivals, slot_rows) * BLOCK_ROWS
    lands = jnp.where(valid, lands, -1)
    perm = (jnp.arange(head, dtype=jnp.int32)[:, None] == lands[None, :]).astype(BF16)
    numbers = jnp.concatenate(
        [
            (jnp.sum(arrivals) * BLOCK_ROWS)[None],
            (section_place == 0).astype(jnp.int32)[None],
            (section_place == end).astype(jnp.int32)[None],
            starts,
            pipe[None],
        ]
    )
    return incoming, perm, numbers


def move_images(incoming):
    count = lax.axis_size("section")
    ring, end = count // 2, count - 1
    return [
        incoming,
        lax.ppermute(incoming, "section", [(1, 0), (end - 1, end)]),
        lax.ppermute(incoming, "section", [(ring - 1, 0), (end - ring + 1, end)]),
    ]


def hold(value, *before):
    return lax.optimization_barrier((value, before))[0]


def per_device(
    section_inputs,
    value_cotangent,
    down_weight,
    up_weight,
    down_gain,
    up_gain,
    image_rows,
    image_route,
):
    section_place = lax.axis_index("section")
    fsdp_place = lax.axis_index("fsdp")
    core = fsdp_place % 2
    y = fsdp_place // 2 % Y_CHIPS
    x = fsdp_place // (2 * Y_CHIPS)
    r = jnp.arange(CHIPS, dtype=jnp.int32)
    chips = (x ^ (r // Y_CHIPS)) * Y_CHIPS + (y + r % Y_CHIPS) % Y_CHIPS

    incoming, perm, numbers = route_images(image_rows, image_route, section_place, fsdp_place)
    table = jnp.concatenate([chips, core[None], numbers, x[None]]).astype(jnp.int32)

    shard, kv = down_weight.shape[1:]

    part = jax.ShapeDtypeStruct((shard, kv), BF16)

    sibling_x = to_sibling(section_inputs)
    w0 = pack([(down_weight, 0), (up_weight, 0)])
    w3, w1, w4 = to_next(w0), to_previous(w0), to_across(w0)
    scaled_ct, inverse = scale(section_inputs, value_cotangent)
    w3, w1, w4, incoming, perm, table = hold((w3, w1, w4, incoming, perm, table), scaled_ct, sibling_x)
    images = move_images(incoming)
    w2, w5, w7 = to_next(w3), to_previous(w4), to_across(w3)
    early = pack([(w0, 0), (w0, 1), (w1, 0), (w1, 1), (w3, 0), (w3, 1), (w4, 0), (w4, 1)])
    head, other_head, scaled_ct, inverse = patch(
        hold(table, early), section_inputs, value_cotangent, perm, images, scaled_ct, inverse
    )
    w2, w5, w7, other_head, scaled_ct, early = hold((w2, w5, w7, other_head, scaled_ct, early))
    sibling_head, sibling_ct = to_sibling(other_head), to_sibling(scaled_ct)
    down7, up5 = on_blocks("halves", halves, [(w7, 0), (w5, 1)], [part, part])
    down6, up6 = to_next(down7), to_previous(up5)

    rows = (section_inputs, sibling_x, head, sibling_head, scaled_ct, sibling_ct)
    half = shard // 2

    def blocks(*parts):
        return tuple((pipe, r, 0, shard) for pipe, r in parts)

    far0_near1, far1_back0, send20 = products(
        table,
        *rows,
        (blocks((1, 2), (1, 5)), blocks((1, 6), (1, 3)), (*blocks((0, 6)), (0, 4, 0, half))),
    )
    far0_near1, far1_back0, send20, down6, up6, w7, early = hold(
        (far0_near1, far1_back0, send20, down6, up6, w7, early)
    )
    from_below, from_above, came20 = to_next(far0_near1), to_previous(far1_back0), to_across(send20)
    sibling_early = to_sibling(early)
    down_places = ((0, 0), (0, 2), (1, 0), (0, 4), (0, 6), (1, 2), (2, None), (1, 4))
    up_places = ((0, 1), (0, 3), (1, 1), (0, 5), (0, 7), (1, 3), (3, None), (1, 5))
    near0, back1, keep2, send130, own01, keep13, keep0 = products(
        hold(table, up6),
        *rows,
        (
            blocks((1, 1)), blocks((1, 7)), blocks((0, 2)), (*blocks((0, 5), (0, 7)), (0, 4, half, shard)),
            blocks((1, 0), (1, 4)), blocks((0, 1), (0, 3)), blocks((0, 0)),
        ),
    )

    def pieces(arrays, places):
        return [(arrays[array], at) for array, at in places]

    middle = pack([(w2, 0), (w2, 1), (w5, 0), (w5, 1), (w7, 0), (w7, 1)])
    from_below, from_above, came20, send130 = hold(
        (from_below, from_above, came20, send130), keep0, middle, sibling_early
    )
    message = jax.ShapeDtypeStruct((shard + shard // 2, kv), BF16)
    up, down = on_blocks(
        "first_sums",
        first_sums,
        [near0, (from_below, shard, 0), back1, (from_above, shard, 0), keep2, (came20, shard, 0)],
        [message, message],
    )
    below, above = to_next(up), to_previous(down)
    came130 = to_across(hold(send130, up))
    own = (early, middle, down6, up6)
    sibling = [sibling_early, *[to_sibling(hold(array, up)) for array in (middle, down6, up6)]]
    filled = layer(
        0,
        hold(table, up),
        section_inputs, head, value_cotangent, scaled_ct, inverse, down_gain,
        pieces(own, down_places), pieces(sibling, down_places), (),
    )
    below, above = hold((below, above), filled[0])
    payload = jax.ShapeDtypeStruct((shard + 16, kv), BF16)
    here, there = on_blocks(
        "mirror_sums",
        mirror_sums,
        [
            table, (own01, shard, 0), (below, shard, 0), (from_above, shard, 1),
            (own01, shard, 1), (from_below, shard, 1), (above, shard, 0), (up_weight, 0), (early, 7), up_gain,
        ],
        [payload, payload],
    )
    mirrored0, mirrored1 = to_mirror(here, 0), to_mirror(there, 1)
    ups, downs = on_blocks(
        "second_sums",
        second_sums,
        [
            (keep13, shard, 0), (came130, shard, 0), (below, half, 2),
            (keep13, shard, 1), (came130, shard, 1), (above, half, 2),
        ],
        [part, part],
    )
    last_below, last_above = to_next(ups), to_previous(downs)
    values, input_grad = layer(
        1,
        hold(table, ups),
        section_inputs, head, value_cotangent, scaled_ct, inverse, up_gain,
        pieces(own, up_places), pieces(sibling, up_places), tuple(filled),
    )
    last_below, last_above = hold((last_below, last_above), values)
    weight_part, gain_part = on_blocks(
        "down_sums",
        down_sums,
        [
            table, keep0, (came20, half, 2), (came130, half, 4), last_below, last_above, (down_weight, 0), down_gain,
        ],
        [jax.ShapeDtypeStruct((shard, kv), F32), jax.ShapeDtypeStruct((1, shard), F32)],
    )
    mirrored0, mirrored1 = hold((mirrored0, mirrored1), weight_part)
    weight_grad, gain_grad = on_blocks(
        "last_sums",
        last_sums,
        [weight_part, gain_part, mirrored0, mirrored1],
        [jax.ShapeDtypeStruct((1, shard, kv), F32), jax.ShapeDtypeStruct((1, shard), F32)],
    )
    return (values, input_grad, weight_grad, gain_grad)


def solution(mesh):
    return jax.shard_map(
        per_device,
        mesh=mesh,
        in_specs=(
            P(None, "section", "fsdp", None),
            P(None, "section", "fsdp", None),
            P("section", "fsdp", None),
            P("section", "fsdp", None),
            P("section", None),
            P("section", None),
            P(None, "fsdp", None),
            P(),
        ),
        out_specs=(
            P(None, "section", "fsdp", None),
            P(None, "section", "fsdp", None),
            P("section", "fsdp", None),
            P("section", "fsdp"),
        ),
        check_vma=False,
    )
```
